32 devices in a mesh: seq: 8 (over y, x, core), batch: 4 (over z).
Axes of the slice: x: 2, y: 2, z: 4, core: 2. Of those that a mesh axis runs over, the one named last changes fastest.
Arguments:
- tokens: bfloat16 [4, 3072, 768], P('batch', 'seq'), may hold values from -6 to 6
- segment_ids: int32 [4, 3072], P('batch', 'seq'), may hold values from 0 to 2, as said below
- neighbours: bfloat16 [4, 48, 2, 128, 768], P('batch', 'seq'), may hold values from -6 to 6
- first_gain: float32 [768], replicated, may hold values from 0.5 to 1.5
- first_shift: float32 [768], replicated, may hold values from -1.5 to 1.5
- self_weight: bfloat16 [768, 2304], replicated, may hold values from -0.21875 to 0.21875
- self_output: bfloat16 [768, 768], replicated, may hold values from -0.875 to 0.875
- second_gain: float32 [768], replicated, may hold values from 0.5 to 1.5
- second_shift: float32 [768], replicated, may hold values from -1.5 to 1.5
- query_weight: bfloat16 [768, 768], replicated, may hold values from -0.21875 to 0.21875
- memory_weight: bfloat16 [768, 1536], replicated, may hold values from -0.21875 to 0.21875
- cross_output: bfloat16 [768, 768], replicated, may hold values from -1.75 to 1.75
- third_gain: float32 [768], replicated, may hold values from 0.5 to 1.5
- third_shift: float32 [768], replicated, may hold values from -1.5 to 1.5
- up_weight: bfloat16 [768, 3072], replicated, may hold values from -0.21875 to 0.21875
- down_weight: bfloat16 [3072, 768], replicated, may hold values from -0.109375 to 0.109375
- cotangent: bfloat16 [4, 3072, 768], P('batch', 'seq'), may hold values from -6 to 6
Outputs:
- result: bfloat16 [4, 3072, 768], P('batch', 'seq')
- input_grad: float32 [4, 3072, 768], P('batch', 'seq')
- neighbour_grad: float32 [4, 48, 2, 128, 768], P('batch', 'seq')
- first_gain_grad: float32 [768], P('batch')
- first_shift_grad: float32 [768], P('batch')
- self_weight_grad: float32 [768, 2304], P('batch')
- self_output_grad: float32 [768, 768], P('batch')
- second_gain_grad: float32 [768], P('batch')
- second_shift_grad: float32 [768], P('batch')
- query_weight_grad: float32 [768, 768], P('batch')
- memory_weight_grad: float32 [768, 1536], P('batch')
- cross_output_grad: float32 [768, 768], P('batch')
- third_gain_grad: float32 [768], P('batch')
- third_shift_grad: float32 [768], P('batch')
- up_weight_grad: float32 [768, 3072], P('batch')
- down_weight_grad: float32 [3072, 768], P('batch')
The draws below stay inside these ranges and needn't reach their ends.
Inputs may be any that keep to these rules, and one draw needn't show every extreme that they name: `segment_ids`: ids never fall along a sequence; each sequence holds three documents: the middle one starts at a position from 1 to 192, the last one at a position from 2880 to 3071.
All inputs are finite; a program needn't handle non-finite values.
Results may differ from the reference program's by a relative error of at most 0.025.
Values may be sent and summed in bfloat16 or wider, within the bound.
A program may use at most 256 MiB of HBM per device.

```python
import jax
import jax.numpy as jnp
from jax import lax

D = 768
FF = 3072
HEADS = 12
HEAD = 64
STRETCH = 64
NEIGHBOURS = 2
NEIGHBOUR_LEN = 128
TOK_DEV = 384
SEQS = 4
LEN = 3072
STRETCHES = 48


def draw_segment_ids(key, part):
    key = jax.random.fold_in(key, 11)
    first_key, last_key = jax.random.split(key)
    first = jax.random.randint(first_key, (SEQS, 1), 1, TOK_DEV // 2 + 1)
    last = LEN - jax.random.randint(last_key, (SEQS, 1), 1, TOK_DEV // 2 + 1)
    positions = jnp.arange(LEN, dtype=jnp.int32)[None, :]
    return (positions >= first).astype(jnp.int32) + (positions >= last).astype(jnp.int32)


def steps_of(own_key, shape, cuts, least, top_value):
    level = 1.0
    for dim, blocks in cuts:
        draws = jax.random.uniform(jax.random.fold_in(jax.random.fold_in(own_key, 6), dim), (blocks,), jnp.float32, least / len(cuts), top_value / len(cuts))
        level = level * jnp.repeat(jnp.exp(draws), shape[dim] // blocks).reshape((-1,) + (1,) * (len(shape) - 1 - dim))
    return level


def scatter_about(own_key, shape, scale, most, cuts=(), kind=jnp.bfloat16):
    array = jax.random.normal(own_key, shape, jnp.float32) * scale
    if len(cuts) > 0:
        array = steps_of(own_key, shape, cuts, -0.22, 0.18) * array
    return jnp.clip(array, min=-most, max=most).astype(kind)


def setup_inputs(seed: int = 0) -> dict:
    key_list = jax.random.split(jax.random.key(seed), 18)
    return {
        "tokens": scatter_about(key_list[0], (SEQS, LEN, D), 1.0, 6.0, ((0, 4), (1, 8))),
        "segment_ids": draw_segment_ids(jax.random.fold_in(key_list[17], 71), 0),
        "neighbours": scatter_about(key_list[2], (SEQS, STRETCHES, NEIGHBOURS, NEIGHBOUR_LEN, D), 1.0, 6.0, ((0, 4), (1, 8))),
        "first_gain": jnp.clip(1.0 + 0.1 * jax.random.normal(key_list[3], (D,), jnp.float32), 0.5, 1.5),
        "first_shift": scatter_about(key_list[4], (D,), 0.3, 1.5, (), jnp.float32),
        "self_weight": scatter_about(key_list[5], (D, 3 * D), D ** -0.5, 0.21875),
        "self_output": scatter_about(key_list[6], (D, D), (D // 16) ** -0.5, 0.875),
        "second_gain": jnp.clip(1.0 + 0.1 * jax.random.normal(key_list[7], (D,), jnp.float32), 0.5, 1.5),
        "second_shift": scatter_about(key_list[8], (D,), 0.3, 1.5, (), jnp.float32),
        "query_weight": scatter_about(key_list[9], (D, D), D ** -0.5, 0.21875),
        "memory_weight": scatter_about(key_list[10], (D, 2 * D), D ** -0.5, 0.21875),
        "cross_output": scatter_about(key_list[11], (D, D), (D // 64) ** -0.5, 1.75),
        "third_gain": jnp.clip(1.0 + 0.1 * jax.random.normal(key_list[12], (D,), jnp.float32), 0.5, 1.5),
        "third_shift": scatter_about(key_list[13], (D,), 0.3, 1.5, (), jnp.float32),
        "up_weight": scatter_about(key_list[14], (D, FF), D ** -0.5, 0.21875),
        "down_weight": scatter_about(key_list[15], (FF, D), FF ** -0.5, 0.109375),
        "cotangent": scatter_about(key_list[16], (SEQS, LEN, D), 1.0, 6.0, ((0, 4), (1, 8))),
    }


EPSILON = 1e-05
NEGATIVE = -1e+30
HIGH = lax.Precision.HIGHEST

@jax.custom_vjp
def low(v):
    return lax.optimization_barrier(v.astype(jnp.bfloat16)).astype(jnp.float32)

@jax.custom_vjp
def low_back(v):
    return v

def low_keep(v):
    return (low(v), None)

def low_pass(kept, grad):
    return (grad,)

def back_keep(v):
    return (v, None)

def back_low(kept, grad):
    return (low(grad),)
low.defvjp(low_keep, low_pass)
low_back.defvjp(back_keep, back_low)

def layer_norm(values, gain, shift):
    mean = lax.optimization_barrier(jnp.mean(values, axis=-1, keepdims=True))
    centred = values - mean
    spread = lax.optimization_barrier(jnp.mean(centred * centred, axis=-1, keepdims=True))
    return centred * lax.rsqrt(spread + EPSILON) * gain + shift

def product(left, right):
    return jnp.dot(left, right, precision=HIGH)

def self_attention(projected, segments):
    length = projected.shape[0]
    scale = HEAD ** (-0.5)
    queries = projected[:, :D].reshape(length, HEADS, HEAD)
    keys = projected[:, D:2 * D].reshape(length, HEADS, HEAD)
    values = projected[:, 2 * D:].reshape(length, HEADS, HEAD)
    block = 512 if length % 512 == 0 else length
    positions = jnp.arange(length, dtype=jnp.int32)

    def one_block(index):
        first = index * block
        query_rows = lax.dynamic_slice_in_dim(queries, first, block, 0)
        row_seg = lax.dynamic_slice_in_dim(segments, first, block, 0)
        row_pos = first + jnp.arange(block, dtype=jnp.int32)
        allowed = (row_pos[:, None] >= positions[None, :]) & (row_seg[:, None] == segments[None, :])
        scores = low_back(jnp.einsum('qhd,khd->hqk', query_rows, keys, precision=HIGH) * scale)
        scores = jnp.where(allowed[None], scores, NEGATIVE)
        chances = low(jax.nn.softmax(scores, axis=-1))
        return jnp.einsum('hqk,khd->qhd', chances, values, precision=HIGH).reshape(block, D)
    blocks = lax.map(jax.checkpoint(one_block), jnp.arange(length // block, dtype=jnp.int32))
    return blocks.reshape(length, D)

def cross_attention(cross_queries, memory):
    length = cross_queries.shape[0]
    stretch_count = length // STRETCH
    span = NEIGHBOURS * NEIGHBOUR_LEN
    groups = stretch_count + 1
    scale = HEAD ** (-0.5)
    memory = memory.reshape(stretch_count, span, 2 * D)
    extended = jnp.concatenate([jnp.zeros((1, span, 2 * D), jnp.float32), memory], axis=0)
    memory_keys = extended[:, :, :D].reshape(groups, span, HEADS, HEAD)
    memory_values = extended[:, :, D:].reshape(groups, span, HEADS, HEAD)
    padded = jnp.concatenate([jnp.zeros((1, D), jnp.float32), cross_queries, jnp.zeros((STRETCH - 1, D), jnp.float32)], axis=0)
    padded = padded.reshape(groups, STRETCH, HEADS, HEAD)
    scores = low_back(jnp.einsum('gqhd,gkhd->ghqk', padded, memory_keys, precision=HIGH) * scale)
    chances = low(jax.nn.softmax(scores, axis=-1))
    context = jnp.einsum('ghqk,gkhd->gqhd', chances, memory_values, precision=HIGH).reshape(groups * STRETCH, D)
    keep = (jnp.arange(length, dtype=jnp.int32) >= STRETCH - 1).astype(jnp.float32)[:, None]
    return context[1:length + 1] * keep

def forward(tokens, segments, neighbours, params):
    first_gain, first_shift, self_weight, self_output, second_gain, second_shift, query_weight, memory_weight, cross_output, third_gain, third_shift, up_weight, down_weight = params
    normed_one = low(layer_norm(tokens, first_gain, first_shift))
    projected = low(low_back(product(normed_one, self_weight)))
    context = low(low_back(self_attention(projected, segments)))
    stream_one = tokens + low_back(product(context, self_output))
    normed_two = low(layer_norm(stream_one, second_gain, second_shift))
    cross_queries = low(low_back(product(normed_two, query_weight)))
    memory = low(low_back(product(neighbours.reshape(-1, D), memory_weight)))
    cross_context = low(low_back(cross_attention(cross_queries, memory)))
    stream_two = stream_one + low_back(product(cross_context, cross_output))
    normed_three = low(layer_norm(stream_two, third_gain, third_shift))
    upper = low_back(product(normed_three, up_weight))
    active = low(jax.nn.gelu(upper, approximate=False))
    return stream_two + low_back(product(active, down_weight))

def reference(tokens, segment_ids, neighbours, first_gain, first_shift, self_weight, self_output, second_gain, second_shift, query_weight, memory_weight, cross_output, third_gain, third_shift, up_weight, down_weight, cotangent):
    params = tuple((weight.astype(jnp.float32) for weight in (first_gain, first_shift, self_weight, self_output, second_gain, second_shift, query_weight, memory_weight, cross_output, third_gain, third_shift, up_weight, down_weight)))

    def one_sequence(sums, inputs):
        token_row, seg_row, neighbour_row, grad_row = inputs

        def local(token_values, neighbour_values, *weights):
            return forward(token_values, seg_row, neighbour_values, weights)
        output, pullback = jax.vjp(local, token_row.astype(jnp.float32), neighbour_row.astype(jnp.float32), *params)
        grads = pullback(grad_row.astype(jnp.float32))
        sums = tuple((total + part for total, part in zip(sums, grads[2:])))
        return (sums, (output.astype(jnp.bfloat16), grads[0], grads[1]))
    zeros = tuple((jnp.zeros_like(weight) for weight in params))
    sums, (results, token_grads, neighbour_grads) = lax.scan(one_sequence, zeros, (tokens, segment_ids, neighbours, cotangent))
    return (results, token_grads, neighbour_grads, sums[0], sums[1], sums[2], sums[3], sums[4], sums[5], sums[6], sums[7], sums[8], sums[9], sums[10], sums[11], sums[12])
```

```python
from functools import partial

import jax
import jax.numpy as jnp
from jax import lax
from jax.experimental import pallas as pl
from jax.experimental.pallas import tpu as pltpu
from jax.sharding import PartitionSpec as P
import math

D = 768
HEADS = 12
HEAD = 64
STRETCH = 64
NEIGHBOURS = 2
NEIGHBOUR_LEN = 128
SPAN = NEIGHBOURS * NEIGHBOUR_LEN
EPSILON = 1e-05
NEGATIVE = -1e30
MESH = pl.DeviceIdType.MESH
VM = pltpu.VMEM
F32 = jnp.float32
BF16 = jnp.bfloat16


def matmul(left, right):
    return jnp.dot(left, right, preferred_element_type=F32)


def outer_sum(left, right):
    return lax.dot_general(left, right, (((0,), (0,)), ((), ())), preferred_element_type=F32)


def back_product(left, right):
    return lax.dot_general(left, right, (((1,), (1,)), ((), ())), preferred_element_type=F32)


def low_lanes(shape):
    return lax.broadcasted_iota(jnp.int32, shape, len(shape) - 1) < HEAD


def swap_lanes(values):
    return pltpu.roll(values, HEAD, 1)


def full_norm(values, gain, shift):
    mean = jnp.mean(values, axis=-1, keepdims=True)
    centred = values - mean
    spread = jnp.mean(centred * centred, axis=-1, keepdims=True)
    return centred * lax.rsqrt(spread + EPSILON) * gain + shift


class Plan:
    def __init__(self, devices, rows):
        self.devices = devices
        self.rows = rows
        self.groups = math.gcd(devices, HEADS)
        self.members = devices // self.groups
        self.slots = HEADS // self.groups

    def place(self):
        me = lax.axis_index("seq")
        return me, lax.div(me, self.members), lax.rem(me, self.members)


def seq_device(index):
    return (index, lax.axis_index("batch"))


def greet(devices):
    barrier = pltpu.get_barrier_semaphore()
    for device in devices:
        pl.semaphore_signal(barrier, inc=1, device_id=device, device_id_type=MESH)
    pl.semaphore_wait(barrier, len(devices))


def send(source, target, send_sem, recv_sem, device):
    return pltpu.make_async_remote_copy(
        src_ref=source,
        dst_ref=target,
        send_sem=send_sem,
        recv_sem=recv_sem,
        device_id=device,
        device_id_type=MESH,
    )


def pack_rows(values, head):
    half = values.shape[0] // 2
    top, bottom = values[:half], values[half:]
    low = low_lanes((half, 2 * HEAD))
    if head % 2 == 0:
        return jnp.where(low, top, swap_lanes(bottom))
    return jnp.where(low, swap_lanes(top), bottom)


def to_column(row):
    return jnp.transpose(jnp.broadcast_to(row[0:1], (128, row.shape[1])))


def attend_kernel(plan, *refs):
    (
        tokens, gain, shift, weight, neighbours, memory_weight, segments,
        normed, queries, pairs, outs, logs, segs, context, memory,
        projected, pack_pairs, pack_queries, got_queries, sent_context, got_context, state, seg_col,
        pair_send, pair_recv, query_send, query_recv, pass_send, pass_recv,
        back_send, back_recv, seg_send, seg_recv, edge_send, edge_recv, edge,
    ) = refs
    me, group, member = plan.place()
    devices, groups, members, slots, rows = plan.devices, plan.groups, plan.members, plan.slots, plan.rows
    others = [lax.rem(me + i, devices) for i in range(1, devices)]
    greet([seq_device(o) for o in others])
    half = rows // 2
    stretches = neighbours.shape[0] // SPAN
    low = low_lanes((rows, 2 * HEAD))

    seg_copies = []
    segs[me] = segments[...]
    for i, o in enumerate(others):
        copy = send(segs.at[me], segs.at[me], seg_send.at[i], seg_recv.at[me], seq_device(o))
        copy.start()
        seg_copies.append(copy)
    last_rows = pl.ds((stretches - 1) * SPAN, SPAN)
    edge_copy = send(neighbours.at[last_rows], edge, edge_send, edge_recv, seq_device(jnp.minimum(me + 1, devices - 1)))

    @pl.when(me < devices - 1)
    def _():
        edge_copy.start()

    normed[...] = full_norm(tokens[...].astype(F32), gain[...], shift[...]).astype(BF16)

    @pl.loop(0, 3)
    def _(j):
        columns = pl.ds(pl.multiple_of(j * D, D), D)
        projected[:, columns] = matmul(normed[...], weight[:, columns])

    for head in range(HEADS):
        block = (head // 2) * 128
        key = projected[:, D + block : D + block + 128]
        value = projected[:, 2 * D + block : 2 * D + block + 128]
        if head % 2 == 0:
            pair = jnp.where(low, key, swap_lanes(value))
        else:
            pair = jnp.where(low, swap_lanes(key), value)
        pack_pairs[head] = pair.astype(BF16)
        query = projected[:, block : block + 128].astype(BF16).astype(F32) * (HEAD ** -0.5)
        pack_queries[head] = pack_rows(query, head).astype(BF16)

    def pair_copy(slot, away):
        to = lax.rem(group + away, groups)
        return send(
            pack_pairs.at[to * slots + slot], pairs.at[slot, me],
            pair_send.at[slot, away - 1], pair_recv.at[slot, group], seq_device(to * members + member),
        )

    def query_copy(slot, away):
        to = lax.rem(group + away, groups)
        return send(
            pack_queries.at[to * slots + slot], got_queries.at[slot, group],
            query_send.at[slot, away - 1], query_recv.at[slot, group], seq_device(to * members + member),
        )

    def arrived_pair(slot, origin):
        return send(
            pack_pairs.at[0], pairs.at[slot, origin * members + member],
            pair_send.at[slot, 0], pair_recv.at[slot, origin], seq_device(me),
        )

    def arrived_query(slot, origin):
        return send(
            pack_queries.at[0], got_queries.at[slot, origin],
            query_send.at[slot, 0], query_recv.at[slot, origin], seq_device(me),
        )

    def pass_copy(slot, origin, away):
        to = lax.rem(member + away, members)
        place = origin * members + member
        return send(
            pairs.at[slot, place], pairs.at[slot, place],
            pass_send.at[slot, origin, away - 1], pass_recv.at[slot, place], seq_device(group * members + to),
        )

    def passed(slot, origin, away):
        source = lax.rem(member + away, members)
        place = origin * members + source
        return send(
            pairs.at[slot, place], pairs.at[slot, place],
            pass_send.at[slot, origin, 0], pass_recv.at[slot, place], seq_device(me),
        )

    for slot in range(slots):
        for away in range(1, groups):
            pair_copy(slot, away).start()
            query_copy(slot, away).start()
    for slot in range(slots):
        pairs[slot, me] = pack_pairs[group * slots + slot]
        got_queries[slot, group] = pack_queries[group * slots + slot]
        for away in range(1, members):
            pass_copy(slot, group, away).start()

    @pl.loop(0, stretches)
    def _(s):
        some = pl.ds(pl.multiple_of(s * SPAN, SPAN), SPAN)
        memory[s + 1] = matmul(neighbours[some], memory_weight[...]).astype(BF16)

    for copy in seg_copies:
        copy.wait_send()
    for i in range(1, devices):
        source = lax.rem(me + i, devices)
        send(segs.at[source], segs.at[source], seg_send.at[0], seg_recv.at[source], seq_device(me)).wait_recv()

    @pl.loop(0, groups)
    def _(g):
        seg_col[g] = to_column(segs[g * members + member])

    def back_copy(slot, to):
        return send(
            sent_context.at[slot, to], got_context.at[group * slots + slot],
            back_send.at[slot, to], back_recv.at[group * slots + slot], seq_device(to * members + member),
        )

    for slot in range(slots):
        for away in range(1, groups):
            origin = lax.rem(group + away, groups)
            arrived_pair(slot, origin).wait_recv()
            for beyond in range(1, members):
                pass_copy(slot, origin, beyond).start()
        for away in range(1, groups):
            origin = lax.rem(group + away, groups)
            arrived_query(slot, origin).wait_recv()
        for origin in range(groups):
            for beyond in range(1, members):
                passed(slot, origin, beyond).wait_recv()

        def block(step, carry, slot=slot):
            origin = lax.rem(group + 1 + step, groups)
            place = origin * members + member
            packed = got_queries[slot, origin].astype(F32)
            half_low = low_lanes((half, 2 * HEAD))
            queries[slot, origin, :half] = jnp.where(half_low, packed, 0.0).astype(BF16)
            queries[slot, origin, half:] = jnp.where(half_low, swap_lanes(packed), 0.0).astype(BF16)
            state[0] = jnp.full((rows, 128), NEGATIVE, F32)
            state[1] = jnp.zeros((rows, 128), F32)
            outs[slot, origin] = jnp.zeros((rows, 128), F32)

            def fold(k, causal, masked):
                pair = pairs[slot, k]
                scores = back_product(queries[slot, origin], pair)
                if masked:
                    allowed = seg_col[origin][:, :1] == segs[k][:1]
                    if causal:
                        at = lax.broadcasted_iota(jnp.int32, (rows, rows), 0)
                        key_at = lax.broadcasted_iota(jnp.int32, (rows, rows), 1)
                        allowed = allowed & (at >= key_at)
                    scores = jnp.where(allowed, scores, NEGATIVE)
                old = state[0][:, :1]
                top = jnp.maximum(old, jnp.max(scores, axis=1, keepdims=True))
                factor = jnp.exp(old - top)
                chance = jnp.exp(scores - top)
                total = state[1][:, :1] * factor + jnp.sum(chance, axis=1, keepdims=True)
                outs[slot, origin] = outs[slot, origin] * factor + matmul(chance.astype(BF16), pair)
                state[0] = jnp.broadcast_to(top, (rows, 128))
                state[1] = jnp.broadcast_to(total, (rows, 128))

            def inner(k, c):
                edge_block = (k == 0) | (place == devices - 1)

                @pl.when(edge_block)
                def _():
                    fold(k, False, True)

                @pl.when(jnp.logical_not(edge_block))
                def _():
                    fold(k, False, False)

                return c

            lax.fori_loop(0, place, inner, 0)
            fold(place, True, True)
            total = state[1]
            done = outs[slot, origin] / total
            outs[slot, origin] = done
            logs[slot, origin] = jnp.transpose(state[0] + jnp.log(total))[:8]
            out_low = done.astype(BF16).astype(F32)
            packed_out = jnp.where(half_low, swap_lanes(out_low[:half]), out_low[half:]).astype(BF16)

            @pl.when(origin != group)
            def _():
                sent_context[slot, origin] = packed_out
                back_copy(slot, origin).start()

            @pl.when(origin == group)
            def _():
                got_context[group * slots + slot] = packed_out

            return carry

        lax.fori_loop(0, groups, block, 0)

    @pl.when(me > 0)
    def _():
        edge_copy.wait_recv()
        memory[0] = matmul(edge[...], memory_weight[...]).astype(BF16)

    @pl.when(me == 0)
    def _():
        memory[0] = jnp.zeros_like(memory[0])

    @pl.when(me < devices - 1)
    def _():
        edge_copy.wait_send()

    for slot in range(slots):
        for away in range(1, groups):
            origin = lax.rem(group + away, groups)
            pair_copy(slot, away).wait_send()
            query_copy(slot, away).wait_send()
            send(
                sent_context.at[slot, 0], got_context.at[origin * slots + slot],
                back_send.at[slot, 0], back_recv.at[origin * slots + slot], seq_device(me),
            ).wait_recv()
            back_copy(slot, origin).wait_send()
        for origin in range(groups):
            for beyond in range(1, members):
                pass_copy(slot, origin, beyond).wait_send()

    for two in range(HEADS // 2):
        first = got_context[2 * two].astype(F32)
        second = got_context[2 * two + 1].astype(F32)
        half_low = low_lanes((half, 2 * HEAD))
        columns = slice(two * 128, two * 128 + 128)
        context[:half, columns] = jnp.where(half_low, first, swap_lanes(second)).astype(BF16)
        context[half:, columns] = jnp.where(half_low, swap_lanes(first), second).astype(BF16)


def attend(plan, tokens, gain, shift, weight, neighbours, memory_weight, segments):
    devices, groups, members, slots, rows = plan.devices, plan.groups, plan.members, plan.slots, plan.rows
    half = rows // 2
    stretches = neighbours.shape[0] // SPAN
    dma = pltpu.SemaphoreType.DMA
    shapes = [
        ((rows, D), BF16),
        ((slots, groups, rows, 128), BF16),
        ((slots, devices, rows, 128), BF16),
        ((slots, groups, rows, 128), F32),
        ((slots, groups, 8, rows), F32),
        ((devices, 8, rows), F32),
        ((rows, D), BF16),
        ((stretches + 1, SPAN, 2 * D), BF16),
    ]
    return pl.pallas_call(
        partial(attend_kernel, plan),
        out_shape=[jax.ShapeDtypeStruct(*s) for s in shapes],
        in_specs=[pl.BlockSpec(memory_space=VM)] * 7,
        out_specs=[pl.BlockSpec(memory_space=VM)] * len(shapes),
        scratch_shapes=[
            VM((rows, 3 * D), F32),
            VM((HEADS, rows, 128), BF16),
            VM((HEADS, half, 128), BF16),
            VM((slots, groups, half, 128), BF16),
            VM((slots, groups, half, 128), BF16),
            VM((HEADS, half, 128), BF16),
            VM((2, rows, 128), F32),
            VM((groups, rows, 128), F32),
            dma((slots, groups)),
            dma((slots, groups)),
            dma((slots, groups)),
            dma((slots, groups)),
            dma((slots, groups, members)),
            dma((slots, devices)),
            dma((slots, groups)),
            dma((HEADS,)),
            dma((devices,)),
            dma((devices,)),
            dma,
            dma,
            VM((SPAN, D), BF16),
        ],
        compiler_params=pltpu.CompilerParams(
            collective_id=0, has_side_effects=True, vmem_limit_bytes=60 << 20
        ),
        name="attend",
    )(tokens, gain.reshape(1, D), shift.reshape(1, D), weight, neighbours, memory_weight, segments)


def unattend_kernel(plan, *refs):
    (
        grad_out, queries, pairs, outs, logs, segs,
        result,
        pack_grads, got_grads, grads, deltas, seg_col, pair_sum, query_sum,
        give, took, sent_pair, got_pair, sent_query, got_query,
        out_send, out_recv, give_send, give_recv, pair_send, pair_recv, query_send, query_recv,
    ) = refs
    me, group, member = plan.place()
    devices, groups, members, slots, rows = plan.devices, plan.groups, plan.members, plan.slots, plan.rows
    half = rows // 2
    half_low = low_lanes((half, 2 * HEAD))
    peers = [seq_device(lax.rem(group + i, groups) * members + member) for i in range(1, groups)]
    peers += [seq_device(group * members + lax.rem(member + i, members)) for i in range(1, members)]
    greet(peers)

    for head in range(HEADS):
        block = (head // 2) * 128
        pack_grads[head] = pack_rows(grad_out[:, block : block + 128].astype(F32), head).astype(BF16)

    def out_copy(slot, away):
        to = lax.rem(group + away, groups)
        return send(
            pack_grads.at[to * slots + slot], got_grads.at[slot, group],
            out_send.at[slot, away - 1], out_recv.at[slot, group], seq_device(to * members + member),
        )

    for slot in range(slots):
        for away in range(1, groups):
            out_copy(slot, away).start()
    for slot in range(slots):
        got_grads[slot, group] = pack_grads[group * slots + slot]

    @pl.loop(0, devices)
    def _(d):
        seg_col[d] = to_column(segs[d])

    def give_copy(slot, away):
        to = lax.rem(member + away, members)
        return send(
            give.at[slot, away - 1], took.at[slot, away - 1],
            give_send.at[slot, away - 1], give_recv.at[slot, away - 1], seq_device(group * members + to),
        )

    def pair_copy(slot, to):
        return send(
            sent_pair.at[slot, to], got_pair.at[group * slots + slot],
            pair_send.at[slot, to], pair_recv.at[group * slots + slot], seq_device(to * members + member),
        )

    def query_copy(slot, to):
        return send(
            sent_query.at[slot, to], got_query.at[group * slots + slot],
            query_send.at[slot, to], query_recv.at[group * slots + slot], seq_device(to * members + member),
        )

    for slot in range(slots):
        for away in range(1, groups):
            origin = lax.rem(group + away, groups)
            send(
                pack_grads.at[0], got_grads.at[slot, origin],
                out_send.at[slot, 0], out_recv.at[slot, origin], seq_device(me),
            ).wait_recv()

        @pl.loop(0, groups)
        def _(g, slot=slot):
            packed = got_grads[slot, g].astype(F32)
            top = jnp.where(half_low, 0.0, swap_lanes(packed))
            bottom = jnp.where(half_low, 0.0, packed)
            grads[g, :half] = top.astype(BF16)
            grads[g, half:] = bottom.astype(BF16)
            product = jnp.concatenate([top, bottom], axis=0) * outs[slot, g]
            deltas[g] = jnp.broadcast_to(jnp.sum(jnp.transpose(product), axis=0, keepdims=True), (8, rows))
            query_sum[g] = jnp.zeros((128, rows), F32)

        def key_block(k, carry, slot=slot):
            pair_sum[k] = jnp.zeros((rows, 128), F32)
            first = lax.div(jnp.maximum(k - member, 0) + members - 1, members)

            def fold(g, place, masked):
                pair = pairs[slot, k]
                query = queries[slot, g]
                grad = grads[g]
                scores = back_product(pair, query)
                if masked:
                    allowed = seg_col[k][:, :1] == segs[place][:1]
                    at = place * rows + lax.broadcasted_iota(jnp.int32, (rows, rows), 1)
                    key_at = k * rows + lax.broadcasted_iota(jnp.int32, (rows, rows), 0)
                    scores = jnp.where(allowed & (at >= key_at), scores, NEGATIVE)
                chance = jnp.exp(scores - logs[slot, g][:1])
                chance_grad = back_product(pair, grad)
                score_grad = (chance * (chance_grad - deltas[g][:1])).astype(BF16)
                pair_sum[k] += matmul(score_grad, query) + matmul(chance.astype(BF16), grad)
                query_sum[g] += outer_sum(pair, score_grad)

            def inner(g, c):
                place = g * members + member
                edge_block = (k == 0) | (place == devices - 1) | (place == k)

                @pl.when(edge_block)
                def _():
                    fold(g, place, True)

                @pl.when(jnp.logical_not(edge_block))
                def _():
                    fold(g, place, False)

                return c

            lax.fori_loop(first, groups, inner, 0)
            return carry

        lax.fori_loop(0, devices, key_block, 0)

        for away in range(1, members):
            to = lax.rem(member + away, members)
            for g in range(groups):
                give[slot, away - 1, g] = pair_sum[g * members + to].astype(BF16)
            give_copy(slot, away).start()

        @pl.loop(0, groups)
        def _(i, slot=slot):
            g = lax.rem(group + 1 + i, groups)
            total = jnp.transpose(query_sum[g]) * (HEAD ** -0.5)
            packed = jnp.where(half_low, total[:half], swap_lanes(total[half:])).astype(BF16)

            @pl.when(g != group)
            def _():
                sent_query[slot, g] = packed
                query_copy(slot, g).start()

            @pl.when(g == group)
            def _():
                got_query[group * slots + slot] = packed

        for away in range(1, members):
            give_copy(slot, away).wait_recv()

        @pl.loop(0, groups)
        def _(i, slot=slot):
            g = lax.rem(group + 1 + i, groups)
            total = pair_sum[g * members + member]
            for away in range(1, members):
                total = total + took[slot, away - 1, g].astype(F32)
            total = total.astype(BF16)

            @pl.when(g != group)
            def _():
                sent_pair[slot, g] = total
                pair_copy(slot, g).start()

            @pl.when(g == group)
            def _():
                got_pair[group * slots + slot] = total

    for slot in range(slots):
        for away in range(1, members):
            give_copy(slot, away).wait_send()
        for away in range(1, groups):
            origin = lax.rem(group + away, groups)
            out_copy(slot, away).wait_send()
            pair_copy(slot, origin).wait_send()
            query_copy(slot, origin).wait_send()
            head = origin * slots + slot
            send(
                sent_pair.at[slot, 0], got_pair.at[head],
                pair_send.at[slot, 0], pair_recv.at[head], seq_device(me),
            ).wait_recv()
            send(
                sent_query.at[slot, 0], got_query.at[head],
                query_send.at[slot, 0], query_recv.at[head], seq_device(me),
            ).wait_recv()

    low = low_lanes((rows, 2 * HEAD))
    for two in range(HEADS // 2):
        columns = slice(two * 128, two * 128 + 128)
        first = got_query[2 * two].astype(F32)
        second = got_query[2 * two + 1].astype(F32)
        result[:half, columns] = jnp.where(half_low, first, swap_lanes(second)).astype(BF16)
        result[half:, columns] = jnp.where(half_low, swap_lanes(first), second).astype(BF16)
        first = got_pair[2 * two].astype(F32)
        second = got_pair[2 * two + 1].astype(F32)
        result[:, slice(D + two * 128, D + two * 128 + 128)] = jnp.where(low, first, swap_lanes(second)).astype(BF16)
        result[:, slice(2 * D + two * 128, 2 * D + two * 128 + 128)] = jnp.where(
            low, swap_lanes(first), second
        ).astype(BF16)


def unattend(plan, grad_out, queries, pairs, outs, logs, segs):
    devices, groups, members, slots, rows = plan.devices, plan.groups, plan.members, plan.slots, plan.rows
    half = rows // 2
    dma = pltpu.SemaphoreType.DMA
    others = max(members - 1, 1)
    return pl.pallas_call(
        partial(unattend_kernel, plan),
        out_shape=jax.ShapeDtypeStruct((rows, 3 * D), BF16),
        in_specs=[pl.BlockSpec(memory_space=VM)] * 6,
        out_specs=pl.BlockSpec(memory_space=VM),
        scratch_shapes=[
            VM((HEADS, half, 128), BF16),
            VM((slots, groups, half, 128), BF16),
            VM((groups, rows, 128), BF16),
            VM((groups, 8, rows), F32),
            VM((devices, rows, 128), F32),
            VM((devices, rows, 128), F32),
            VM((groups, 128, rows), F32),
            VM((slots, others, groups, rows, 128), BF16),
            VM((slots, others, groups, rows, 128), BF16),
            VM((slots, groups, rows, 128), BF16),
            VM((HEADS, rows, 128), BF16),
            VM((slots, groups, half, 128), BF16),
            VM((HEADS, half, 128), BF16),
            dma((slots, groups)),
            dma((slots, groups)),
            dma((slots, others)),
            dma((slots, others)),
            dma((slots, groups)),
            dma((HEADS,)),
            dma((slots, groups)),
            dma((HEADS,)),
        ],
        compiler_params=pltpu.CompilerParams(
            collective_id=1, has_side_effects=True, vmem_limit_bytes=60 << 20
        ),
        name="unattend",
    )(grad_out, queries, pairs, outs, logs, segs)


FOLD = 256 // HEAD


def stack_heads(values):
    lane = lax.broadcasted_iota(jnp.int32, values.shape, 1) // HEAD
    return jnp.concatenate([jnp.where(lane == h, values, jnp.zeros_like(values)) for h in range(FOLD)], axis=0)


def unstack_heads(stacked):
    count = stacked.shape[0] // FOLD
    lane = lax.broadcasted_iota(jnp.int32, (count, stacked.shape[1]), 1) // HEAD
    total = jnp.where(lane == 0, stacked[:count], 0.0)
    for h in range(1, FOLD):
        total = total + jnp.where(lane == h, stacked[h * count : (h + 1) * count], 0.0)
    return total


def cross_chances(queries, keys):
    scores = back_product(queries, keys) * (HEAD ** -0.5)
    chance = jnp.exp(scores - jnp.max(scores, axis=1, keepdims=True))
    return chance / jnp.sum(chance, axis=1, keepdims=True)


def cross_kernel(queries, memory, out):
    for c in range(D // 256):
        columns = slice(c * 256, c * 256 + 256)
        values = slice(D + c * 256, D + c * 256 + 256)
        chances = cross_chances(stack_heads(queries[0, :, columns]), memory[0, :, columns])
        out[0, :, columns] = unstack_heads(matmul(chances.astype(BF16), memory[0, :, values]))


def cross(queries, memory):
    groups, count, _ = queries.shape
    block = lambda *shape: pl.BlockSpec((1,) + shape, lambda i: (i, 0, 0))
    return pl.pallas_call(
        cross_kernel,
        grid=(groups,),
        out_shape=jax.ShapeDtypeStruct((groups, count, D), F32),
        in_specs=[block(count, D), block(SPAN, 2 * D)],
        out_specs=block(count, D),
        compiler_params=pltpu.CompilerParams(vmem_limit_bytes=32 << 20),
        cost_estimate=pl.CostEstimate(flops=4 * groups * 4 * count * SPAN * D, bytes_accessed=8 << 20, transcendentals=0),
        name="cross",
    )(queries, memory)


def uncross_kernel(queries, memory, grads, query_grad, memory_grad):
    for c in range(D // 256):
        columns = slice(c * 256, c * 256 + 256)
        values = slice(D + c * 256, D + c * 256 + 256)
        stacked = stack_heads(queries[0, :, columns])
        stacked_grad = stack_heads(grads[0, :, columns])
        chances = cross_chances(stacked, memory[0, :, columns])
        chance_grad = back_product(stacked_grad, memory[0, :, values])
        total = jnp.sum(chances * chance_grad, axis=1, keepdims=True)
        score_grad = (chances * (chance_grad - total)).astype(BF16)
        query_grad[0, :, columns] = unstack_heads(matmul(score_grad, memory[0, :, columns])) * (HEAD ** -0.5)
        memory_grad[0, :, columns] = (outer_sum(score_grad, stacked) * (HEAD ** -0.5)).astype(BF16)
        memory_grad[0, :, values] = outer_sum(chances.astype(BF16), stacked_grad).astype(BF16)


def uncross(queries, memory, grads):
    groups, count, _ = queries.shape
    block = lambda *shape: pl.BlockSpec((1,) + shape, lambda i: (i, 0, 0))
    return pl.pallas_call(
        uncross_kernel,
        grid=(groups,),
        out_shape=[
            jax.ShapeDtypeStruct((groups, count, D), F32),
            jax.ShapeDtypeStruct((groups, SPAN, 2 * D), BF16),
        ],
        in_specs=[block(count, D), block(SPAN, 2 * D), block(count, D)],
        out_specs=[block(count, D), block(SPAN, 2 * D)],
        compiler_params=pltpu.CompilerParams(vmem_limit_bytes=32 << 20),
        cost_estimate=pl.CostEstimate(flops=10 * groups * 4 * count * SPAN * D, bytes_accessed=16 << 20, transcendentals=0),
        name="uncross",
    )(queries, memory, grads)


class Piece:
    def __init__(self, matrix, first, count, at=0):
        self.matrix, self.first, self.count, self.at = matrix, first, count, at


class Share:
    def __init__(self, rows, columns, pieces, part=None, vectors=None):
        self.rows, self.columns, self.pieces, self.part, self.vectors = rows, columns, pieces, part, vectors


def shares_of(batch, groups, ff):
    short, tall = D // (batch * groups), ff // (batch * groups * 2)
    half = D // 2
    return [
        Share(tall, half, [Piece(0, 0, half)], part=0),
        Share(tall, half, [Piece(0, 0, half)], part=1),
        Share(short, ff // 4, [Piece(1, 0, ff // 4)]),
        Share(short, ff // 4, [Piece(1, ff // 4, ff // 4)]),
        Share(short, 512, [Piece(3, 0, 512)]),
        Share(short, 256 + half, [Piece(3, 512, 256), Piece(2, 0, half, 256)]),
        Share(short, half, [Piece(4, 0, half)]),
        Share(short, half, [Piece(5, 0, half)]),
        Share(short, 640, [Piece(6, 0, 640)]),
        Share(short, 640, [Piece(6, 640, 512)], vectors=512),
    ]


def tile_of(count):
    for tile in (384, 512, 256, 128):
        if count % tile == 0:
            return tile


def gather_kernel(plan, batch, shares, matrices, *refs):
    lefts, rights = refs[:matrices], refs[matrices : 2 * matrices]
    vectors = refs[2 * matrices]
    refs = refs[2 * matrices + 1 :]
    gathered, refs = refs[: len(shares)], refs[len(shares) :]
    two_left, refs = refs[:matrices], refs[matrices:]
    two_right, refs = refs[:matrices], refs[matrices:]
    sums, refs = refs[: len(shares)], refs[len(shares) :]
    firsts, refs = refs[: len(shares)], refs[len(shares) :]
    seconds, refs = refs[: len(shares)], refs[len(shares) :]
    thirds, refs = refs[: len(shares)], refs[len(shares) :]
    other_vectors, own_send, swap_send, swap_recv, send_sems, recv_sems = refs

    me, group, member = plan.place()
    members, groups = plan.members, plan.groups
    z = lax.axis_index("batch")
    right, down = lax.rem(group, 2), lax.div(group, 2)
    partner = seq_device(group * members + 1 - member)
    chip = lambda g: seq_device(g * members + member)
    across = {"x": chip(down * 2 + 1 - right), "y": chip((1 - down) * 2 + right)}
    layers = [lax.rem(z + i, batch) for i in range(1, batch)]
    greet(
        [partner]
        + [chip(lax.rem(group + i, groups)) for i in range(1, groups)]
        + [(me, layer) for layer in layers]
    )

    swaps = []
    for m in range(matrices):
        depth = lefts[m].shape[0]
        width = rights[m].shape[1] // 2
        mine = pl.ds(pl.multiple_of(member * width, 128), width)
        theirs = pl.ds(pl.multiple_of((1 - member) * width, 128), width)
        here, there = pl.ds(0, depth), pl.ds(depth, depth)
        copies = [
            pltpu.make_async_copy(lefts[m], two_left[m].at[here], own_send.at[m, 0]),
            pltpu.make_async_copy(rights[m].at[:, mine], two_right[m].at[here], own_send.at[m, 1]),
            send(lefts[m], two_left[m].at[there], swap_send.at[m, 0], swap_recv.at[m, 0], partner),
            send(rights[m].at[:, theirs], two_right[m].at[there], swap_send.at[m, 1], swap_recv.at[m, 1], partner),
        ]
        for copy in copies:
            copy.start()
        swaps.append(copies)
    vector_copy = send(
        vectors.at[1 - member], other_vectors, swap_send.at[matrices, 0], swap_recv.at[matrices, 0], partner
    )
    vector_copy.start()
    ready = set()

    def need(m):
        if m not in ready:
            ready.add(m)
            for copy in swaps[m]:
                copy.wait()

    def spread(s, values, at, count, first):
        share = shares[s]
        rows = share.rows
        for layer in range(batch):
            for g in range(groups):
                start = (layer * groups + g) * rows
                sums[s][layer, g // 2, g % 2, :, pl.ds(at, count)] = values[start : start + rows].astype(BF16)

    def fill(s):
        share = shares[s]
        for piece in share.pieces:
            m = piece.matrix
            need(m)
            if share.part is None:
                tile = tile_of(piece.count)
                for t in range(piece.count // tile):
                    first = piece.first + t * tile
                    values = outer_sum(two_left[m][...], two_right[m][:, first : first + tile])
                    spread(s, values, piece.at + t * tile, tile, 0)
            else:
                rows = share.rows
                if share.part == 1:
                    continue
                deep = two_left[m].shape[1] // batch
                for layer in range(batch):
                    values = outer_sum(
                        two_left[m][:, layer * deep : (layer + 1) * deep], two_right[m][...]
                    ).astype(BF16)
                    for g in range(groups):
                        for part in range(2):
                            start = (g * 2 + part) * rows
                            sums[s + part][layer, g // 2, g % 2] = values[start : start + rows]
        if share.vectors is not None:
            vector_copy.wait()
            values = vectors[member].astype(F32) + other_vectors[...].astype(F32)
            spread(s, values, share.vectors, 128, 0)

    def add(a, b):
        return (a.astype(F32) + b.astype(F32)).astype(BF16)

    def steps(s):
        total = sums[s]
        sem = lambda k: (send_sems.at[s, k], recv_sems.at[s, k])
        fill(s)
        if s % 2 == 0:
            copy = send(total.at[:, :, 1 - right], firsts[s], *sem(0), across["x"])
        else:
            copy = send(total.at[:, 1 - down], firsts[s], *sem(0), across["y"])
        copy.start()
        yield
        copy.wait()
        if s % 2 == 0:
            total[:, :, right] = add(total[:, :, right], firsts[s][...])
            copy = send(total.at[:, 1 - down, right], seconds[s], *sem(1), across["y"])
        else:
            total[:, down] = add(total[:, down], firsts[s][...])
            copy = send(total.at[:, down, 1 - right], seconds[s], *sem(1), across["x"])
        copy.start()
        yield
        copy.wait()
        total[:, down, right] = add(total[:, down, right], seconds[s][...])
        copies = [
            send(total.at[layer, down, right], thirds[s].at[i], *sem(2 + i), (me, layer))
            for i, layer in enumerate(layers)
        ]
        for copy in copies:
            copy.start()
        yield
        for copy in copies:
            copy.wait()
        whole = total[z, down, right].astype(F32)
        for i in range(batch - 1):
            whole = whole + thirds[s][i].astype(F32)
        out = gathered[s]
        out[member, down, right] = whole.astype(BF16)
        copies = [
            send(
                out.at[member, down, right], out.at[member, down, right],
                *sem(1 + batch + i), chip(lax.rem(group + i, groups)),
            )
            for i in range(1, groups)
        ]
        for copy in copies:
            copy.start()
        yield
        for i, copy in enumerate(copies):
            copy.wait_send()
            source = lax.rem(group + groups - 1 - i, groups)
            spot = out.at[member, lax.div(source, 2), lax.rem(source, 2)]
            send(spot, spot, *sem(2 + batch + i), chip(group)).wait_recv()
        copy = send(out.at[member], out.at[member], *sem(1 + batch + groups), partner)
        copy.start()
        yield
        copy.wait_send()
        send(out.at[1 - member], out.at[1 - member], *sem(1 + batch + groups), partner).wait_recv()

    pairs = len(shares) // 2
    running = [(steps(2 * p), steps(2 * p + 1)) for p in range(pairs)]
    for time in range(pairs + 5):
        for p in range(min(time, pairs - 1), -1, -1):
            if time - p <= 5:
                for step in running[p]:
                    next(step, None)


def gather_weights(plan, batch, lefts, rights, vectors):
    ff = rights[1].shape[1]
    shares = shares_of(batch, plan.groups, ff)
    matrices = len(lefts)
    dma = pltpu.SemaphoreType.DMA
    out_shapes = [
        jax.ShapeDtypeStruct((2, 2, 2, s.rows, s.columns), BF16) for s in shares
    ]
    scratch = [VM((2 * left.shape[0], left.shape[1]), BF16) for left in lefts]
    scratch += [VM((2 * right.shape[0], right.shape[1] // 2), BF16) for right in rights]
    scratch += [VM((batch, 2, 2, s.rows, s.columns), BF16) for s in shares]
    scratch += [VM((batch, 2, s.rows, s.columns), BF16) for s in shares]
    scratch += [VM((batch, s.rows, s.columns), BF16) for s in shares]
    scratch += [VM((batch - 1, s.rows, s.columns), BF16) for s in shares]
    scratch += [
        VM((D, 128), BF16),
        dma((matrices, 2)),
        dma((matrices + 1, 2)),
        dma((matrices + 1, 2)),
        dma((len(shares), 2 + batch + plan.groups)),
        dma((len(shares), 2 + batch + plan.groups)),
    ]
    out = pl.pallas_call(
        partial(gather_kernel, plan, batch, shares, matrices),
        out_shape=out_shapes,
        in_specs=[pl.BlockSpec(memory_space=pl.ANY)] * (2 * matrices) + [pl.BlockSpec(memory_space=VM)],
        out_specs=[pl.BlockSpec(memory_space=VM)] * len(shares),
        scratch_shapes=scratch,
        compiler_params=pltpu.CompilerParams(
            collective_id=2, has_side_effects=True, vmem_limit_bytes=62 << 20
        ),
        name="gather_weights",
    )(*lefts, *rights, vectors)

    def joined(parts, width):
        columns = jnp.concatenate([out[s][..., first : first + count] for s, first, count in parts], axis=-1)
        core, _, _, rows, half = columns.shape
        return jnp.transpose(columns.reshape(core, 4 * rows, half), (1, 0, 2)).reshape(4 * rows, core * half).astype(F32)

    half = D // 2
    down = jnp.stack([out[0], out[1]], axis=3)
    down = jnp.transpose(down.reshape(2, 8 * shares[0].rows, half), (1, 0, 2)).reshape(-1, D).astype(F32)
    up = joined([(2, 0, ff // 4), (3, 0, ff // 4)], ff)
    memory = joined([(4, 0, 512), (5, 0, 256)], 2 * D)
    cross_out = joined([(5, 256, half)], D)
    query = joined([(6, 0, half)], D)
    self_out = joined([(7, 0, half)], D)
    self_weight = joined([(8, 0, 640), (9, 0, 512)], 3 * D)
    vector = out[9][..., 512:].reshape(2, 4 * shares[9].rows, 128)
    return down, up, cross_out, memory, query, self_out, self_weight, vector


def shifted(values, groups, top):
    rows = values.shape[0]
    pad = groups * STRETCH - rows - 1
    return jnp.pad(values, ((1, pad), (0, 0))).reshape(groups, STRETCH, D)


def on_device(devices, batch, tokens, segment_ids, neighbours, first_gain, first_shift, self_weight, self_output, second_gain,
    second_shift, query_weight, memory_weight, cross_output, third_gain, third_shift, up_weight, down_weight, cotangent,
):
    rows = tokens.shape[1]
    plan = Plan(devices, rows)
    seq_index = lax.axis_index("seq")
    stream = tokens[0].astype(F32)
    stretch_count = neighbours.shape[1]
    groups = stretch_count + 1
    neighbour_rows = neighbours[0].reshape(stretch_count * SPAN, D)
    segments = jnp.broadcast_to(segment_ids.astype(F32), (8, rows))
    normed_one_low, queries, pairs, outs, logs, segs, context_low, memory = attend(
        plan, tokens[0], first_gain, first_shift, self_weight, neighbour_rows, memory_weight, segments
    )
    stream_one = stream + matmul(context_low, self_output)
    normed_two, second_back = jax.vjp(full_norm, stream_one, second_gain, second_shift)
    normed_two_low = normed_two.astype(BF16)
    cross_queries = matmul(normed_two_low, query_weight).astype(BF16)
    padded_queries = shifted(cross_queries, groups, 1)
    keep = ((seq_index > 0) | (jnp.arange(rows, dtype=jnp.int32) >= STRETCH - 1)).astype(F32)[:, None]
    cross_context = cross(padded_queries, memory).reshape(groups * STRETCH, D)[1 : rows + 1]
    cross_low = (cross_context * keep).astype(BF16)
    stream_two = stream_one + matmul(cross_low, cross_output)
    normed_three, third_back = jax.vjp(full_norm, stream_two, third_gain, third_shift)
    normed_three_low = normed_three.astype(BF16)
    upper = matmul(normed_three_low, up_weight)
    active, gelu_back = jax.vjp(partial(jax.nn.gelu, approximate=False), upper)
    active_low = active.astype(BF16)
    result = (stream_two + matmul(active_low, down_weight)).astype(BF16)
    grad_low = cotangent[0]
    active_grad = back_product(grad_low, down_weight)
    upper_low = gelu_back(active_grad)[0].astype(BF16)
    stream_part, third_gain_grad, third_shift_grad = third_back(back_product(upper_low, up_weight))
    stream_two_grad = grad_low.astype(F32) + stream_part
    branch_low = stream_two_grad.astype(BF16)
    context_grad = (back_product(branch_low, cross_output) * keep).astype(BF16)
    query_part, memory_part = uncross(padded_queries, memory, shifted(context_grad, groups, 1))
    cross_query_low = query_part.reshape(groups * STRETCH, D)[1 : rows + 1].astype(BF16)
    returned = lax.ppermute(memory_part[0], "seq", [(i, i - 1) for i in range(1, devices)])
    last = (memory_part[stretch_count].astype(F32) + returned.astype(F32)).astype(BF16)
    memory_grad = jnp.concatenate([memory_part[1:stretch_count], last[None]], axis=0).reshape(stretch_count * SPAN, 2 * D)
    neighbour_grad = back_product(memory_grad, memory_weight).reshape(neighbours.shape)
    stream_part, second_gain_grad, second_shift_grad = second_back(back_product(cross_query_low, query_weight))
    stream_one_grad = stream_two_grad + stream_part
    self_low = stream_one_grad.astype(BF16)
    grad_out = back_product(self_low, self_output).astype(BF16)
    projected_grad = unattend(plan, grad_out, queries, pairs, outs, logs, segs)
    unused, first_back = jax.vjp(full_norm, stream, first_gain, first_shift)
    stream_part, first_gain_grad, first_shift_grad = first_back(back_product(projected_grad, self_weight))
    input_grad = stream_one_grad + stream_part
    gains = jnp.stack([first_gain_grad, second_gain_grad, third_gain_grad], axis=1)
    shifts = jnp.stack([first_shift_grad, second_shift_grad, third_shift_grad], axis=1)
    vectors = jnp.pad(jnp.stack([gains, shifts]), ((0, 0), (0, 0), (0, 125))).astype(BF16)
    down, up, cross_out, memory_w, query, self_out, self_w, vector = gather_weights(
        plan,
        batch,
        [active_low, normed_three_low, cross_low, neighbour_rows, normed_two_low, context_low, normed_one_low],
        [grad_low, upper_low, branch_low, memory_grad, cross_query_low, self_low, projected_grad],
        vectors,
    )
    vector = vector.astype(F32)
    return (
        result[None],
        input_grad[None],
        neighbour_grad,
        vector[0, :, 0],
        vector[1, :, 0],
        self_w,
        self_out,
        vector[0, :, 1],
        vector[1, :, 1],
        query,
        memory_w,
        cross_out,
        vector[0, :, 2],
        vector[1, :, 2],
        up,
        down,
    )


def from_behind(array, axis, by):
    devices = lax.axis_size(axis)
    pairs = [(i, i + by) for i in range(devices) if 0 <= i + by < devices]
    return lax.ppermute(array, axis, pairs)


def layer_norm(values, gain, shift):
    mean = jnp.mean(values, axis=-1, keepdims=True)
    centred = values - mean
    spread = jnp.mean(centred * centred, axis=-1, keepdims=True)
    return centred * lax.rsqrt(spread + EPSILON) * gain + shift


def block_rows():
    return 512


def causal_allowed(query_pos, query_seg, key_pos, key_seg):
    return (query_pos[:, None] >= key_pos[None, :]) & (query_seg[:, None] == key_seg[None, :])


def key_block_grads(
    queries, grad_out, log_total, delta, query_pos, query_seg, keys, values, key_pos, key_seg, scale
):
    allowed = causal_allowed(query_pos, query_seg, key_pos, key_seg)[None]
    scores = jnp.einsum("qhd,khd->hqk", queries, keys, preferred_element_type=jnp.float32) * scale
    chances = jnp.where(
        allowed, jnp.exp(jnp.where(allowed, scores, NEGATIVE) - log_total[..., None]), 0.0
    )
    prob_grad = jnp.einsum("qhd,khd->hqk", grad_out, values, preferred_element_type=jnp.float32)
    score_low = (chances * (prob_grad - delta[..., None])).astype(jnp.bfloat16)
    query_part = (
        jnp.einsum("hqk,khd->qhd", score_low, keys, preferred_element_type=jnp.float32) * scale
    )
    key_part = (
        jnp.einsum("hqk,qhd->khd", score_low, queries, preferred_element_type=jnp.float32) * scale
    )
    value_part = jnp.einsum(
        "hqk,qhd->khd", chances.astype(jnp.bfloat16), grad_out, preferred_element_type=jnp.float32
    )
    return (query_part, key_part, value_part)


def plain_on_device(
    tokens,
    segment_ids,
    neighbours,
    first_gain,
    first_shift,
    self_weight,
    self_output,
    second_gain,
    second_shift,
    query_weight,
    memory_weight,
    cross_output,
    third_gain,
    third_shift,
    up_weight,
    down_weight,
    cotangent,
):
    rows = tokens.shape[1]
    seq_index = lax.axis_index("seq")
    scale = HEAD ** (-0.5)
    stream = tokens[0].astype(jnp.float32)
    seg_local = segment_ids[0]
    positions = seq_index * rows + jnp.arange(rows, dtype=jnp.int32)
    normed_one, first_back = jax.vjp(layer_norm, stream, first_gain, first_shift)
    normed_one_low = normed_one.astype(jnp.bfloat16)
    projected = matmul(normed_one_low, self_weight).astype(jnp.bfloat16)
    queries = projected[:, :D].reshape(rows, HEADS, HEAD)
    keys_low = projected[:, D : 2 * D]
    values_low = projected[:, 2 * D :]
    start_state = (
        jnp.full((HEADS, rows), NEGATIVE, jnp.float32),
        jnp.zeros((HEADS, rows), jnp.float32),
        jnp.zeros((HEADS, rows, HEAD), jnp.float32),
    )
    carry = start_state
    piece_keys = lax.all_gather(keys_low, "seq", axis=0, tiled=True)
    piece_values = lax.all_gather(values_low, "seq", axis=0, tiled=True)
    piece_seg = lax.all_gather(seg_local, "seq", axis=0, tiled=True)
    count = piece_keys.shape[0]
    fold_size = block_rows()

    def step(state, index):
        maxes, totals, running = state
        first = index * fold_size
        keys = lax.dynamic_slice_in_dim(piece_keys, first, fold_size, 0).reshape(
            fold_size, HEADS, HEAD
        )
        values = lax.dynamic_slice_in_dim(piece_values, first, fold_size, 0).reshape(
            fold_size, HEADS, HEAD
        )
        key_seg = lax.dynamic_slice_in_dim(piece_seg, first, fold_size, 0)
        key_pos = first + jnp.arange(fold_size, dtype=jnp.int32)
        allowed = causal_allowed(positions, seg_local, key_pos, key_seg)[None]
        scores = (
            jnp.einsum("qhd,khd->hqk", queries, keys, preferred_element_type=jnp.float32) * scale
        )
        scores = jnp.where(allowed, scores, NEGATIVE)
        new_max = jnp.maximum(maxes, jnp.max(scores, axis=-1))
        factor = jnp.exp(maxes - new_max)
        weights = jnp.where(allowed, jnp.exp(scores - new_max[..., None]), 0.0)
        totals = totals * factor + jnp.sum(weights, axis=-1)
        running = running * factor[..., None] + jnp.einsum(
            "hqk,khd->hqd", weights.astype(jnp.bfloat16), values, preferred_element_type=jnp.float32
        )
        return ((new_max, totals, running), None)

    carry, unused = lax.scan(step, carry, jnp.arange(count // fold_size, dtype=jnp.int32))
    maxes, totals, running = carry
    log_total = maxes + jnp.log(totals)
    context = running / totals[..., None]
    context_low = jnp.transpose(context, (1, 0, 2)).reshape(rows, D).astype(jnp.bfloat16)
    stream_one = stream + matmul(context_low, self_output)
    normed_two, second_back = jax.vjp(layer_norm, stream_one, second_gain, second_shift)
    normed_two_low = normed_two.astype(jnp.bfloat16)
    cross_queries = matmul(normed_two_low, query_weight).astype(jnp.bfloat16)
    stretch_count = neighbours.shape[1]
    span = NEIGHBOURS * NEIGHBOUR_LEN
    groups = stretch_count + 1
    neighbour_rows = neighbours[0].reshape(stretch_count * span, D)
    memory = (
        matmul(neighbour_rows, memory_weight)
        .astype(jnp.bfloat16)
        .reshape(stretch_count, span, 2 * D)
    )
    previous = from_behind(memory[stretch_count - 1], "seq", 1)
    extended = jnp.concatenate([previous[None], memory], axis=0)
    memory_keys = extended[:, :, :D].reshape(groups, span, HEADS, HEAD)
    memory_values = extended[:, :, D:].reshape(groups, span, HEADS, HEAD)
    pad_top = jnp.zeros((1, D), jnp.bfloat16)
    pad_end = jnp.zeros((STRETCH - 1, D), jnp.bfloat16)
    padded_queries = jnp.concatenate([pad_top, cross_queries, pad_end], axis=0).reshape(
        groups, STRETCH, HEADS, HEAD
    )
    cross_probs = jax.nn.softmax(
        jnp.einsum(
            "gqhd,gkhd->ghqk", padded_queries, memory_keys, preferred_element_type=jnp.float32
        )
        * scale,
        axis=-1,
    )
    cross_probs_low = cross_probs.astype(jnp.bfloat16)
    keep = ((seq_index > 0) | (jnp.arange(rows, dtype=jnp.int32) >= STRETCH - 1)).astype(
        jnp.float32
    )[:, None]
    cross_context = jnp.einsum(
        "ghqk,gkhd->gqhd", cross_probs_low, memory_values, preferred_element_type=jnp.float32
    ).reshape(groups * STRETCH, D)[1 : rows + 1]
    cross_low = (cross_context * keep).astype(jnp.bfloat16)
    stream_two = stream_one + matmul(cross_low, cross_output)
    normed_three, third_back = jax.vjp(layer_norm, stream_two, third_gain, third_shift)
    normed_three_low = normed_three.astype(jnp.bfloat16)
    upper = matmul(normed_three_low, up_weight)
    active, gelu_back = jax.vjp(partial(jax.nn.gelu, approximate=False), upper)
    active_low = active.astype(jnp.bfloat16)
    result = (stream_two + matmul(active_low, down_weight)).astype(jnp.bfloat16)
    grad_low = cotangent[0]
    down_grad = outer_sum(active_low, grad_low)
    active_grad = back_product(grad_low, down_weight)
    upper_low = gelu_back(active_grad)[0].astype(jnp.bfloat16)
    up_grad = outer_sum(normed_three_low, upper_low)
    stream_part, third_gain_grad, third_shift_grad = third_back(back_product(upper_low, up_weight))
    stream_two_grad = grad_low.astype(jnp.float32) + stream_part
    branch_low = stream_two_grad.astype(jnp.bfloat16)
    cross_output_grad = outer_sum(cross_low, branch_low)
    context_grad = (back_product(branch_low, cross_output) * keep).astype(jnp.bfloat16)
    padded_grad = jnp.concatenate([pad_top, context_grad, pad_end], axis=0).reshape(
        groups, STRETCH, HEADS, HEAD
    )
    prob_grad = jnp.einsum(
        "gqhd,gkhd->ghqk", padded_grad, memory_values, preferred_element_type=jnp.float32
    )
    score_low = (
        cross_probs * (prob_grad - jnp.sum(cross_probs * prob_grad, axis=-1, keepdims=True))
    ).astype(jnp.bfloat16)
    cross_query_low = (
        (
            jnp.einsum(
                "ghqk,gkhd->gqhd", score_low, memory_keys, preferred_element_type=jnp.float32
            )
            * scale
        )
        .reshape(groups * STRETCH, D)[1 : rows + 1]
        .astype(jnp.bfloat16)
    )
    key_part = (
        jnp.einsum("ghqk,gqhd->gkhd", score_low, padded_queries, preferred_element_type=jnp.float32)
        * scale
    )
    value_part = jnp.einsum(
        "ghqk,gqhd->gkhd", cross_probs_low, padded_grad, preferred_element_type=jnp.float32
    )
    extended_grad = jnp.concatenate(
        [key_part.reshape(groups, span, D), value_part.reshape(groups, span, D)], axis=-1
    )
    returned = from_behind(extended_grad[0].astype(jnp.bfloat16), "seq", -1).astype(jnp.float32)
    memory_grad = jnp.concatenate(
        [extended_grad[1:stretch_count], (extended_grad[stretch_count] + returned)[None]], axis=0
    )
    memory_grad = memory_grad.astype(jnp.bfloat16).reshape(stretch_count * span, 2 * D)
    memory_weight_grad = outer_sum(neighbour_rows, memory_grad)
    neighbour_grad = back_product(memory_grad, memory_weight).reshape(neighbours.shape)
    query_weight_grad = outer_sum(normed_two_low, cross_query_low)
    stream_part, second_gain_grad, second_shift_grad = second_back(
        back_product(cross_query_low, query_weight)
    )
    stream_one_grad = stream_two_grad + stream_part
    self_low = stream_one_grad.astype(jnp.bfloat16)
    self_output_grad = outer_sum(context_low, self_low)
    grad_out = back_product(self_low, self_output).astype(jnp.bfloat16).reshape(rows, HEADS, HEAD)
    delta = jnp.sum(jnp.transpose(grad_out.astype(jnp.float32), (1, 0, 2)) * context, axis=-1)
    gathered_keys, gathered_values, gathered_seg = (
        lax.all_gather(keys_low, "seq", axis=0, tiled=True),
        lax.all_gather(values_low, "seq", axis=0, tiled=True),
        lax.all_gather(seg_local, "seq", axis=0, tiled=True),
    )
    total_rows = gathered_keys.shape[0]
    size = block_rows()

    def key_step(query_sum, index):
        first = index * size
        keys = lax.dynamic_slice_in_dim(gathered_keys, first, size, 0).reshape(size, HEADS, HEAD)
        values = lax.dynamic_slice_in_dim(gathered_values, first, size, 0).reshape(
            size, HEADS, HEAD
        )
        key_seg = lax.dynamic_slice_in_dim(gathered_seg, first, size, 0)
        key_pos = first + jnp.arange(size, dtype=jnp.int32)
        query_part, key_block, value_block = key_block_grads(
            queries,
            grad_out,
            log_total,
            delta,
            positions,
            seg_local,
            keys,
            values,
            key_pos,
            key_seg,
            scale,
        )
        pair = jnp.concatenate([key_block.reshape(size, D), value_block.reshape(size, D)], axis=1)
        return (query_sum + query_part, pair)

    query_grad, pairs = lax.scan(
        key_step,
        jnp.zeros((rows, HEADS, HEAD), jnp.float32),
        jnp.arange(total_rows // size, dtype=jnp.int32),
    )
    pair_grad = lax.psum_scatter(
        pairs.reshape(total_rows, 2 * D).astype(jnp.bfloat16),
        "seq",
        scatter_dimension=0,
        tiled=True,
    ).astype(jnp.float32)
    projected_grad = jnp.concatenate([query_grad.reshape(rows, D), pair_grad], axis=1).astype(
        jnp.bfloat16
    )
    self_weight_grad = outer_sum(normed_one_low, projected_grad)
    stream_part, first_gain_grad, first_shift_grad = first_back(
        back_product(projected_grad, self_weight)
    )
    input_grad = stream_one_grad + stream_part
    shares = (
        lax.psum_scatter(
            first_gain_grad.astype(jnp.bfloat16), "batch", scatter_dimension=0, tiled=True
        ).astype(jnp.float32),
        lax.psum_scatter(
            first_shift_grad.astype(jnp.bfloat16), "batch", scatter_dimension=0, tiled=True
        ).astype(jnp.float32),
        lax.psum_scatter(
            self_weight_grad.astype(jnp.bfloat16), "batch", scatter_dimension=0, tiled=True
        ).astype(jnp.float32),
        lax.psum_scatter(
            self_output_grad.astype(jnp.bfloat16), "batch", scatter_dimension=0, tiled=True
        ).astype(jnp.float32),
        lax.psum_scatter(
            second_gain_grad.astype(jnp.bfloat16), "batch", scatter_dimension=0, tiled=True
        ).astype(jnp.float32),
        lax.psum_scatter(
            second_shift_grad.astype(jnp.bfloat16), "batch", scatter_dimension=0, tiled=True
        ).astype(jnp.float32),
        lax.psum_scatter(
            query_weight_grad.astype(jnp.bfloat16), "batch", scatter_dimension=0, tiled=True
        ).astype(jnp.float32),
        lax.psum_scatter(
            memory_weight_grad.astype(jnp.bfloat16), "batch", scatter_dimension=0, tiled=True
        ).astype(jnp.float32),
        lax.psum_scatter(
            cross_output_grad.astype(jnp.bfloat16), "batch", scatter_dimension=0, tiled=True
        ).astype(jnp.float32),
        lax.psum_scatter(
            third_gain_grad.astype(jnp.bfloat16), "batch", scatter_dimension=0, tiled=True
        ).astype(jnp.float32),
        lax.psum_scatter(
            third_shift_grad.astype(jnp.bfloat16), "batch", scatter_dimension=0, tiled=True
        ).astype(jnp.float32),
        lax.psum_scatter(
            up_grad.astype(jnp.bfloat16), "batch", scatter_dimension=0, tiled=True
        ).astype(jnp.float32),
        lax.psum_scatter(
            down_grad.astype(jnp.bfloat16), "batch", scatter_dimension=0, tiled=True
        ).astype(jnp.float32),
    )
    sums = (
        lax.psum(shares[0].astype(jnp.bfloat16), "seq").astype(jnp.float32),
        lax.psum(shares[1].astype(jnp.bfloat16), "seq").astype(jnp.float32),
        lax.psum(shares[2].astype(jnp.bfloat16), "seq").astype(jnp.float32),
        lax.psum(shares[3].astype(jnp.bfloat16), "seq").astype(jnp.float32),
        lax.psum(shares[4].astype(jnp.bfloat16), "seq").astype(jnp.float32),
        lax.psum(shares[5].astype(jnp.bfloat16), "seq").astype(jnp.float32),
        lax.psum(shares[6].astype(jnp.bfloat16), "seq").astype(jnp.float32),
        lax.psum(shares[7].astype(jnp.bfloat16), "seq").astype(jnp.float32),
        lax.psum(shares[8].astype(jnp.bfloat16), "seq").astype(jnp.float32),
        lax.psum(shares[9].astype(jnp.bfloat16), "seq").astype(jnp.float32),
        lax.psum(shares[10].astype(jnp.bfloat16), "seq").astype(jnp.float32),
        lax.psum(shares[11].astype(jnp.bfloat16), "seq").astype(jnp.float32),
        lax.psum(shares[12].astype(jnp.bfloat16), "seq").astype(jnp.float32),
    )
    return (
        result[None],
        input_grad[None],
        neighbour_grad,
        sums[0],
        sums[1],
        sums[2],
        sums[3],
        sums[4],
        sums[5],
        sums[6],
        sums[7],
        sums[8],
        sums[9],
        sums[10],
        sums[11],
        sums[12],
    )


def solution(mesh):
    placed = (
        P("batch", "seq", None),
        P("batch", "seq"),
        P("batch", "seq", None, None, None),
        P(),
        P(),
        P(),
        P(),
        P(),
        P(),
        P(),
        P(),
        P(),
        P(),
        P(),
        P(),
        P(),
        P("batch", "seq", None),
    )
    sizes = mesh.shape
    if sizes["seq"] == 8 and sizes["batch"] == 4:
        body = partial(on_device, sizes["seq"], sizes["batch"])
    else:
        body = plain_on_device
    return jax.shard_map(
        body,
        mesh=mesh,
        in_specs=placed,
        out_specs=(
            P("batch", "seq", None),
            P("batch", "seq", None),
            P("batch", "seq", None, None, None),
            P("batch"),
            P("batch"),
            P("batch", None),
            P("batch", None),
            P("batch"),
            P("batch"),
            P("batch", None),
            P("batch", None),
            P("batch", None),
            P("batch"),
            P("batch"),
            P("batch", None),
            P("batch", None),
        ),
        check_vma=False,
    )
```

```python
import functools
from functools import partial

import jax
import jax.numpy as jnp
from jax import lax
from jax.experimental import pallas as pl
from jax.experimental.pallas import tpu as pltpu
from jax.sharding import PartitionSpec as P
import math

D = 768
HEADS = 12
HEAD = 64
STRETCH = 64
NEIGHBOURS = 2
NEIGHBOUR_LEN = 128
SPAN = NEIGHBOURS * NEIGHBOUR_LEN
EPSILON = 1e-05
NEGATIVE = -1e30
MESH = pl.DeviceIdType.MESH
VM = pltpu.VMEM
F32 = jnp.float32
BF16 = jnp.bfloat16


def matmul(left, right):
    return jnp.dot(left, right, preferred_element_type=F32)


def outer_sum(left, right):
    return lax.dot_general(left, right, (((0,), (0,)), ((), ())), preferred_element_type=F32)


def back_product(left, right):
    return lax.dot_general(left, right, (((1,), (1,)), ((), ())), preferred_element_type=F32)


def low_lanes(shape):
    return lax.broadcasted_iota(jnp.int32, shape, len(shape) - 1) < HEAD


def swap_lanes(values):
    return pltpu.roll(values, HEAD, 1)


def full_norm(values, gain, shift):
    mean = jnp.mean(values, axis=-1, keepdims=True)
    centred = values - mean
    spread = jnp.mean(centred * centred, axis=-1, keepdims=True)
    return centred * lax.rsqrt(spread + EPSILON) * gain + shift


class Plan:
    def __init__(self, devices, rows):
        self.devices = devices
        self.rows = rows
        self.groups = math.gcd(devices, HEADS)
        self.members = devices // self.groups
        self.slots = HEADS // self.groups

    def place(self):
        me = lax.axis_index("seq")
        return me, lax.div(me, self.members), lax.rem(me, self.members)


def seq_device(index):
    return (index, lax.axis_index("batch"))


def greet(devices):
    barrier = pltpu.get_barrier_semaphore()
    for device in devices:
        pl.semaphore_signal(barrier, inc=1, device_id=device, device_id_type=MESH)
    pl.semaphore_wait(barrier, len(devices))


def send(source, target, send_sem, recv_sem, device):
    return pltpu.make_async_remote_copy(
        src_ref=source,
        dst_ref=target,
        send_sem=send_sem,
        recv_sem=recv_sem,
        device_id=device,
        device_id_type=MESH,
    )


def pack_rows(values, head):
    half = values.shape[0] // 2
    top, bottom = values[:half], values[half:]
    low = low_lanes((half, 2 * HEAD))
    if head % 2 == 0:
        return jnp.where(low, top, swap_lanes(bottom))
    return jnp.where(low, swap_lanes(top), bottom)


def hide(plan, scores, k, g, member, start):
    causal = k == g
    if not (causal or k == 0 or g == plan.groups - 1):
        return scores
    at = lax.broadcasted_iota(jnp.int32, scores.shape, 0)
    allowed = at >= start - k * plan.members * plan.rows
    if causal:
        allowed = allowed & (at <= member * plan.rows + lax.broadcasted_iota(jnp.int32, scores.shape, 1))
    return jnp.where(allowed, scores, NEGATIVE)


def attend_kernel(plan, *refs):
    (
        tokens, gain, shift, weight, neighbours, memory_weight, segments,
        normed, queries, pairs, outs, logs, starts, context, memory,
        segs, projected, pack_pairs, pack_queries, got_queries, sent_context, got_context,
        pair_send, pair_recv, query_send, query_recv, pass_send, pass_recv,
        back_send, back_recv, seg_send, seg_recv, edge_send, edge_recv, edge,
    ) = refs
    me, group, member = plan.place()
    devices, groups, members, slots, rows = plan.devices, plan.groups, plan.members, plan.slots, plan.rows
    others = [lax.rem(me + i, devices) for i in range(1, devices)]
    greet([seq_device(o) for o in others])
    half = rows // 2
    stretches = neighbours.shape[0] // SPAN
    low = low_lanes((rows, 2 * HEAD))

    seg_copies = []
    segs[me] = segments[...]
    for i, o in enumerate(others):
        copy = send(segs.at[me], segs.at[me], seg_send.at[i], seg_recv.at[me], seq_device(o))
        copy.start()
        seg_copies.append(copy)
    last_rows = pl.ds((stretches - 1) * SPAN, SPAN)
    edge_copy = send(neighbours.at[last_rows], edge, edge_send, edge_recv, seq_device(jnp.minimum(me + 1, devices - 1)))

    @pl.when(me < devices - 1)
    def _():
        edge_copy.start()

    normed[...] = full_norm(tokens[...].astype(F32), gain[...], shift[...]).astype(BF16)

    @pl.loop(0, 3)
    def _(j):
        columns = pl.ds(pl.multiple_of(j * D, D), D)
        projected[:, columns] = matmul(normed[...], weight[:, columns])

    for head in range(HEADS):
        block = (head // 2) * 128
        key = projected[:, D + block : D + block + 128]
        value = projected[:, 2 * D + block : 2 * D + block + 128]
        if head % 2 == 0:
            pair = jnp.where(low, key, swap_lanes(value))
        else:
            pair = jnp.where(low, swap_lanes(key), value)
        pack_pairs[head] = pair.astype(BF16)
        query = projected[:, block : block + 128].astype(BF16).astype(F32) * (HEAD ** -0.5)
        pack_queries[head] = pack_rows(query, head).astype(BF16)

    def pair_copy(slot, away):
        to = lax.rem(group + away, groups)
        return send(
            pack_pairs.at[to * slots + slot], pairs.at[slot, me],
            pair_send.at[slot, away - 1], pair_recv.at[slot, group], seq_device(to * members + member),
        )

    def query_copy(slot, away):
        to = lax.rem(group + away, groups)
        return send(
            pack_queries.at[to * slots + slot], got_queries.at[slot, group],
            query_send.at[slot, away - 1], query_recv.at[slot, group], seq_device(to * members + member),
        )

    def arrived_pair(slot, origin):
        return send(
            pack_pairs.at[0], pairs.at[slot, origin * members + member],
            pair_send.at[slot, 0], pair_recv.at[slot, origin], seq_device(me),
        )

    def arrived_query(slot, origin):
        return send(
            pack_queries.at[0], got_queries.at[slot, origin],
            query_send.at[slot, 0], query_recv.at[slot, origin], seq_device(me),
        )

    def pass_copy(slot, origin, away):
        to = lax.rem(member + away, members)
        place = origin * members + member
        return send(
            pairs.at[slot, place], pairs.at[slot, place],
            pass_send.at[slot, origin, away - 1], pass_recv.at[slot, place], seq_device(group * members + to),
        )

    def passed(slot, origin, away):
        source = lax.rem(member + away, members)
        place = origin * members + source
        return send(
            pairs.at[slot, place], pairs.at[slot, place],
            pass_send.at[slot, origin, 0], pass_recv.at[slot, place], seq_device(me),
        )

    for slot in range(slots):
        for away in range(1, groups):
            pair_copy(slot, away).start()
            query_copy(slot, away).start()
    for slot in range(slots):
        pairs[slot, me] = pack_pairs[group * slots + slot]
        got_queries[slot, group] = pack_queries[group * slots + slot]
        for away in range(1, members):
            pass_copy(slot, group, away).start()

    @pl.loop(0, stretches)
    def _(s):
        some = pl.ds(pl.multiple_of(s * SPAN, SPAN), SPAN)
        memory[s + 1] = matmul(neighbours[some], memory_weight[...]).astype(BF16)

    for copy in seg_copies:
        copy.wait_send()
    for i in range(1, devices):
        source = lax.rem(me + i, devices)
        send(segs.at[source], segs.at[source], seg_send.at[0], seg_recv.at[source], seq_device(me)).wait_recv()

    counts = [
        jnp.sum(jnp.sum((segs[:, 0, :] == value).astype(F32), axis=1, keepdims=True), axis=0, keepdims=True)
        for value in (0.0, 1.0)
    ]
    for g in range(groups):
        mine = segs[g * members + member]
        starts[g] = jnp.where(mine == 0.0, 0.0, counts[0] + jnp.where(mine == 1.0, 0.0, counts[1])).astype(jnp.int32)

    def back_copy(slot, to):
        return send(
            sent_context.at[slot, to], got_context.at[group * slots + slot],
            back_send.at[slot, to], back_recv.at[group * slots + slot], seq_device(to * members + member),
        )

    def one_slot(slot, carry):
        for away in range(1, groups):
            origin = lax.rem(group + away, groups)
            arrived_pair(slot, origin).wait_recv()
            for beyond in range(1, members):
                pass_copy(slot, origin, beyond).start()
        for away in range(1, groups):
            origin = lax.rem(group + away, groups)
            arrived_query(slot, origin).wait_recv()
        for origin in range(groups):
            for beyond in range(1, members):
                passed(slot, origin, beyond).wait_recv()
        half_low = low_lanes((half, 2 * HEAD))
        for g in range(groups):
            packed = got_queries[slot, g].astype(F32)
            queries[slot, g, :half] = jnp.where(half_low, packed, 0.0).astype(BF16)
            queries[slot, g, half:] = jnp.where(half_low, swap_lanes(packed), 0.0).astype(BF16)
            query = queries[slot, g]
            scores = []
            for k in range(g + 1):
                tile = pairs[slot, k * members : (k + 1) * members].reshape(members * rows, 128)
                scores.append(hide(plan, back_product(tile, query), k, g, member, starts[g][:1]))
            top = functools.reduce(jnp.maximum, [jnp.max(s, axis=0, keepdims=True) for s in scores])
            total, out = 0.0, 0.0
            for k in range(g + 1):
                tile = pairs[slot, k * members : (k + 1) * members].reshape(members * rows, 128)
                chance = jnp.exp(scores[k] - top)
                total = total + jnp.sum(chance, axis=0, keepdims=True)
                out = out + outer_sum(tile, chance.astype(BF16))
            logs[slot, g] = jnp.broadcast_to(top + jnp.log(total), (8, rows))
            done = jnp.transpose(out / total)
            outs[slot, g] = done
            out_low = done.astype(BF16).astype(F32)
            packed_out = jnp.where(half_low, swap_lanes(out_low[:half]), out_low[half:]).astype(BF16)

            @pl.when(group != g)
            def _():
                sent_context[slot, g] = packed_out
                back_copy(slot, g).start()

            @pl.when(group == g)
            def _():
                got_context[group * slots + slot] = packed_out

        return carry

    lax.fori_loop(0, slots, one_slot, 0)

    @pl.when(me > 0)
    def _():
        edge_copy.wait_recv()
        memory[0] = matmul(edge[...], memory_weight[...]).astype(BF16)

    @pl.when(me == 0)
    def _():
        memory[0] = jnp.zeros_like(memory[0])

    @pl.when(me < devices - 1)
    def _():
        edge_copy.wait_send()

    for slot in range(slots):
        for away in range(1, groups):
            origin = lax.rem(group + away, groups)
            pair_copy(slot, away).wait_send()
            query_copy(slot, away).wait_send()
            send(
                sent_context.at[slot, 0], got_context.at[origin * slots + slot],
                back_send.at[slot, 0], back_recv.at[origin * slots + slot], seq_device(me),
            ).wait_recv()
            back_copy(slot, origin).wait_send()
        for origin in range(groups):
            for beyond in range(1, members):
                pass_copy(slot, origin, beyond).wait_send()

    for two in range(HEADS // 2):
        first = got_context[2 * two].astype(F32)
        second = got_context[2 * two + 1].astype(F32)
        half_low = low_lanes((half, 2 * HEAD))
        columns = slice(two * 128, two * 128 + 128)
        context[:half, columns] = jnp.where(half_low, first, swap_lanes(second)).astype(BF16)
        context[half:, columns] = jnp.where(half_low, swap_lanes(first), second).astype(BF16)


def attend(plan, tokens, gain, shift, weight, neighbours, memory_weight, segments):
    devices, groups, members, slots, rows = plan.devices, plan.groups, plan.members, plan.slots, plan.rows
    half = rows // 2
    stretches = neighbours.shape[0] // SPAN
    dma = pltpu.SemaphoreType.DMA
    shapes = [
        ((rows, D), BF16),
        ((slots, groups, rows, 128), BF16),
        ((slots, devices, rows, 128), BF16),
        ((slots, groups, rows, 128), F32),
        ((slots, groups, 8, rows), F32),
        ((groups, 8, rows), jnp.int32),
        ((rows, D), BF16),
        ((stretches + 1, SPAN, 2 * D), BF16),
    ]
    return pl.pallas_call(
        partial(attend_kernel, plan),
        out_shape=[jax.ShapeDtypeStruct(*s) for s in shapes],
        in_specs=[pl.BlockSpec(memory_space=VM)] * 7,
        out_specs=[pl.BlockSpec(memory_space=VM)] * len(shapes),
        scratch_shapes=[
            VM((devices, 8, rows), F32),
            VM((rows, 3 * D), F32),
            VM((HEADS, rows, 128), BF16),
            VM((HEADS, half, 128), BF16),
            VM((slots, groups, half, 128), BF16),
            VM((slots, groups, half, 128), BF16),
            VM((HEADS, half, 128), BF16),
            dma((slots, groups)),
            dma((slots, groups)),
            dma((slots, groups)),
            dma((slots, groups)),
            dma((slots, groups, members)),
            dma((slots, devices)),
            dma((slots, groups)),
            dma((HEADS,)),
            dma((devices,)),
            dma((devices,)),
            dma,
            dma,
            VM((SPAN, D), BF16),
        ],
        compiler_params=pltpu.CompilerParams(
            collective_id=0, has_side_effects=True, vmem_limit_bytes=60 << 20
        ),
        name="attend",
    )(tokens, gain.reshape(1, D), shift.reshape(1, D), weight, neighbours, memory_weight, segments)


class Grad:
    def __init__(self, matrix, first, count, at=0, part=None):
        self.matrix, self.first, self.count, self.at, self.part = matrix, first, count, at, part


class Product:
    def __init__(self, matrix, first, count, at=0):
        self.matrix, self.first, self.count, self.at = matrix, first, count, at


class Share:
    def __init__(self, rows, columns, order, pieces, vectors=None):
        self.rows, self.columns, self.order, self.pieces, self.vectors = rows, columns, order, pieces, vectors


def shares_of(batch, groups, ff):
    short, tall = D // (batch * groups), ff // (batch * groups * 2)
    half = D // 2
    return [
        Share(tall, half, "xyz", [Grad(0, 0, half, part=0)]),
        Share(tall, half, "yxz", [Grad(0, 0, half, part=1)]),
        Share(short, ff // 4, "xyz", [Product(0, 0, ff // 4)]),
        Share(short, ff // 4, "yxz", [Product(0, ff // 4, ff // 4)]),
        Share(short, 512, "xyz", [Grad(1, 0, 512)]),
        Share(short, 256 + half, "yxz", [Grad(1, 512, 256), Product(1, 0, half, 256)]),
        Share(short, half, "zxy", [Product(2, 0, half)]),
        Share(short, half, "zyx", [Product(3, 0, half)]),
        Share(short, 640, "xyz", [Product(4, 0, 640)]),
        Share(short, 640, "yxz", [Product(4, 640, 512)], vectors=512),
    ]


def step_shapes(share, batch):
    sizes = {"z": batch, "y": 2, "x": 2}
    shapes = []
    for axis in share.order:
        left = [sizes[a] for a in "zyx" if a in sizes and a != axis]
        sizes.pop(axis)
        lead = [batch - 1] if axis == "z" else []
        shapes.append(tuple(lead + left + [share.rows, share.columns]))
    return shapes


def add(a, b):
    return (a.astype(F32) + b.astype(F32)).astype(BF16)


class Engine:
    def __init__(self, plan, batch, shares, sums, arrivals, gathered, send_sems, recv_sems, keep_sems):
        self.plan, self.batch, self.shares = plan, batch, shares
        self.sums, self.arrivals, self.gathered = sums, arrivals, gathered
        self.send_sems, self.recv_sems, self.keep_sems = send_sems, recv_sems, keep_sems
        me, group, member = plan.place()
        self.me, self.group, self.member = me, group, member
        self.z = lax.axis_index("batch")
        self.x, self.y = lax.rem(group, 2), lax.div(group, 2)
        self.partner = seq_device(group * plan.members + 1 - member)
        chip = lambda g: seq_device(g * plan.members + member)
        self.across = {"x": chip(self.y * 2 + 1 - self.x), "y": chip((1 - self.y) * 2 + self.x)}
        self.diagonal = chip((1 - self.y) * 2 + 1 - self.x)
        self.layers = [lax.rem(self.z + i, batch) for i in range(1, batch)]

    def peers(self):
        return [self.partner, self.across["x"], self.across["y"], self.diagonal] + [
            (self.me, layer) for layer in self.layers
        ]

    def steps(self, s, fill):
        total, out, share = self.sums[s], self.gathered[s], self.shares[s]
        own = {"x": self.x, "y": self.y, "z": self.z}
        count = 0

        def sems():
            nonlocal count
            count += 1
            return self.send_sems.at[s, count - 1], self.recv_sems.at[s, count - 1]

        fill()
        done = {}
        for number, axis in enumerate(share.order):
            where = lambda spots: tuple(spots.get(a, slice(None)) for a in "zyx")
            arrived = self.arrivals[s][number]
            copies = []
            if axis == "z":
                for i, layer in enumerate(self.layers):
                    copies.append(
                        send(total.at[where({**done, "z": layer})], arrived.at[i], *sems(), (self.me, layer))
                    )
            else:
                copies.append(
                    send(total.at[where({**done, axis: 1 - own[axis]})], arrived, *sems(), self.across[axis])
                )
            for copy in copies:
                copy.start()
            yield
            for copy in copies:
                copy.wait()
            done[axis] = own[axis]
            spot = where(done)
            value = total[spot].astype(F32)
            if axis == "z":
                for i in range(self.batch - 1):
                    value = value + arrived[i].astype(F32)
            else:
                value = value + arrived[...].astype(F32)
            total[spot] = value.astype(BF16)
        block = total.at[self.z, self.y, self.x]
        first, second = share.order.replace("z", "")[::-1]
        home = out.at[self.member, self.y, self.x]
        keep = pltpu.make_async_copy(block, home, self.keep_sems.at[s])
        keep.start()
        copy = send(block, home, *sems(), self.across[first])
        copy.start()
        yield
        copy.wait()
        came = (self.member, 1 - self.y, self.x) if first == "y" else (self.member, self.y, 1 - self.x)
        copies = [send(block, home, *sems(), self.across[second])]
        copies.append(send(out.at[came], out.at[came], *sems(), self.across[second]))
        for copy in copies:
            copy.start()
        keep.wait()
        yield
        for copy in copies:
            copy.wait()
        copy = send(out.at[self.member], out.at[self.member], *sems(), self.partner)
        copy.start()
        yield
        copy.wait()


def tail_kernel(plan, batch, shares, arrival_counts, names, *refs):
    r = dict(zip(names, refs))
    refs = refs[len(names) :]
    takes = iter(refs)
    gathered = [next(takes) for _ in shares]
    two_left = [next(takes) for _ in range(5)]
    two_right = [next(takes) for _ in range(5)]
    sums = [next(takes) for _ in shares]
    arrivals = [[next(takes) for _ in range(n)] for n in arrival_counts]
    grad_pieces = [piece for share in shares for piece in share.pieces if isinstance(piece, Grad)]
    other_grads = [next(takes) for _ in grad_pieces]
    (
        queries, pairs, outs, pack_grads, got_grads, grads, deltas, pair_sum, query_sum,
        give, took, sent_pair, got_pair, sent_query, got_query, result, vector_rows, other_rows,
        load_sems, out_send, out_recv, give_send, give_recv, pair_send, pair_recv, query_send, query_recv,
        own_sems, swap_send, swap_recv, piece_own, piece_send, piece_recv, send_sems, recv_sems, keep_sems,
    ) = takes
    me, group, member = plan.place()
    devices, groups, members, slots, rows = plan.devices, plan.groups, plan.members, plan.slots, plan.rows
    half = rows // 2
    half_low = low_lanes((half, 2 * HEAD))
    low = low_lanes((rows, 2 * HEAD))
    engine = Engine(plan, batch, shares, sums, arrivals, gathered, send_sems, recv_sems, keep_sems)
    partner = engine.partner
    greet(engine.peers())

    def load(slot):
        spot = slot % 2
        return [
            pltpu.make_async_copy(r["queries"].at[slot], queries.at[spot], load_sems.at[spot, 0]),
            pltpu.make_async_copy(r["pairs"].at[slot], pairs.at[spot], load_sems.at[spot, 1]),
            pltpu.make_async_copy(r["outs"].at[slot], outs.at[spot], load_sems.at[spot, 2]),
        ]

    for copy in load(0):
        copy.start()
    for head in range(HEADS):
        block = (head // 2) * 128
        pack_grads[head] = pack_rows(r["grad_out"][:, block : block + 128].astype(F32), head).astype(BF16)

    def out_copy(slot, away):
        to = lax.rem(group + away, groups)
        return send(
            pack_grads.at[to * slots + slot], got_grads.at[slot, group],
            out_send.at[slot, away - 1], out_recv.at[slot, group], seq_device(to * members + member),
        )

    for slot in range(slots):
        for away in range(1, groups):
            out_copy(slot, away).start()
        got_grads[slot, group] = pack_grads[group * slots + slot]

    lefts = [r["left%d" % m] for m in range(5)]
    rights = [r["right%d" % m] for m in range(4)] + [result]
    here, there = pl.ds(0, rows), pl.ds(rows, rows)

    def left_swaps(m):
        return [
            pltpu.make_async_copy(lefts[m], two_left[m].at[here], own_sems.at[m, 0]),
            send(lefts[m], two_left[m].at[there], swap_send.at[m, 0], swap_recv.at[m, 0], partner),
        ]

    def right_swaps(m):
        width = rights[m].shape[1] // 2
        mine = pl.ds(pl.multiple_of(member * width, 128), width)
        theirs = pl.ds(pl.multiple_of((1 - member) * width, 128), width)
        return [
            pltpu.make_async_copy(rights[m].at[:, mine], two_right[m].at[here], own_sems.at[m, 1]),
            send(rights[m].at[:, theirs], two_right[m].at[there], swap_send.at[m, 1], swap_recv.at[m, 1], partner),
        ]

    pieces = {}
    swaps = {}
    for s, share in enumerate(shares):
        for piece in share.pieces:
            if isinstance(piece, Grad):
                n = len(pieces)
                source = r["whole%d" % piece.matrix]
                width = source.shape[-1] // 2
                lead = (slice(None),) * 3 + (() if piece.part is None else (piece.part,)) + (slice(None),)
                mine = pl.ds(pl.multiple_of(member * width + piece.first, 128), piece.count)
                theirs = pl.ds(pl.multiple_of((1 - member) * width + piece.first, 128), piece.count)
                pieces[piece] = (n, [
                    pltpu.make_async_copy(
                        source.at[lead + (mine,)],
                        sums[s].at[:, :, :, :, pl.ds(piece.at, piece.count)], piece_own.at[n],
                    ),
                    send(source.at[lead + (theirs,)], other_grads[n], piece_send.at[n], piece_recv.at[n], partner),
                ])
                for copy in pieces[piece][1]:
                    copy.start()
            else:
                m = piece.matrix
                if m not in swaps and m < 4:
                    swaps[m] = left_swaps(m) + right_swaps(m)
                    for copy in swaps[m]:
                        copy.start()
    last_left = left_swaps(4)
    for copy in last_left:
        copy.start()

    waited = set()

    def spread(s, values, at):
        share = shares[s]
        for layer in range(batch):
            for g in range(groups):
                start = (layer * groups + g) * share.rows
                sums[s][layer, g // 2, g % 2, :, pl.ds(at, values.shape[1])] = values[
                    start : start + share.rows
                ].astype(BF16)

    def fill(s):
        for piece in shares[s].pieces:
            if isinstance(piece, Grad):
                n, copies = pieces[piece]
                for copy in copies:
                    copy.wait()
                for layer in range(batch):
                    columns = pl.ds(piece.at, piece.count)
                    sums[s][layer, :, :, :, columns] = add(sums[s][layer, :, :, :, columns], other_grads[n][layer])
            else:
                m = piece.matrix
                if m not in waited:
                    waited.add(m)
                    for copy in swaps[m]:
                        copy.wait()
                tile = 384 if piece.count % 384 == 0 else 512 if piece.count % 512 == 0 else 128
                for t in range(piece.count // tile):
                    first = piece.first + t * tile
                    spread(s, outer_sum(two_left[m][...], two_right[m][:, first : first + tile]), piece.at + t * tile)
        if shares[s].vectors is not None:
            vector_copy.wait()
            mine = vector_rows[member] + other_rows[...]
            wide = jnp.concatenate([mine, jnp.zeros((120, D), F32)], axis=0)
            spread(s, jnp.transpose(wide), shares[s].vectors)

    running = [engine.steps(s, partial(fill, s)) for s in range(len(shares))]

    def advance(*numbers):
        for n in numbers:
            next(running[n], None)

    advance(0, 1, 2, 3)

    def give_copy(slot, away):
        to = lax.rem(member + away, members)
        return send(
            give.at[away - 1], took.at[slot, away - 1],
            give_send.at[slot, away - 1], give_recv.at[slot, away - 1], seq_device(group * members + to),
        )

    def pair_copy(slot, to):
        return send(
            sent_pair.at[to], got_pair.at[group * slots + slot],
            pair_send.at[slot, to], pair_recv.at[group * slots + slot], seq_device(to * members + member),
        )

    def query_copy(slot, to):
        return send(
            sent_query.at[slot, to], got_query.at[group * slots + slot],
            query_send.at[slot, to], query_recv.at[group * slots + slot], seq_device(to * members + member),
        )

    between = [(4, 5, 0, 1), (6, 7, 2, 3, 0, 1), (4, 5, 2, 3, 0, 1)]
    for slot in range(slots):
        spot = slot % 2
        for copy in load(slot):
            copy.wait()
        if slot + 1 < slots:
            for copy in load(slot + 1):
                copy.start()
        for away in range(1, groups):
            origin = lax.rem(group + away, groups)
            send(
                pack_grads.at[0], got_grads.at[slot, origin],
                out_send.at[slot, 0], out_recv.at[slot, origin], partner,
            ).wait_recv()
        for g in range(groups):
            packed = got_grads[slot, g].astype(F32)
            top = jnp.where(half_low, 0.0, swap_lanes(packed))
            bottom = jnp.where(half_low, 0.0, packed)
            grads[g, :half] = top.astype(BF16)
            grads[g, half:] = bottom.astype(BF16)
            product = jnp.concatenate([top, bottom], axis=0) * outs[spot, g]
            deltas[g] = jnp.broadcast_to(jnp.sum(jnp.transpose(product), axis=0, keepdims=True), (8, rows))
        for k in range(groups):
            total = 0.0
            tile = pairs[spot, k * members : (k + 1) * members].reshape(members * rows, 128)
            for g in range(k, groups):
                query, grad = queries[spot, g], grads[g]
                scores = hide(plan, back_product(tile, query), k, g, member, r["starts"][g][:1])
                chance = jnp.exp(scores - r["logs"][slot, g][:1])
                chance_grad = back_product(tile, grad)
                score_grad = (chance * (chance_grad - deltas[g][:1])).astype(BF16)
                total = total + matmul(score_grad, query) + matmul(chance.astype(BF16), grad)
                part = outer_sum(tile, score_grad)
                query_sum[g] = part if k == 0 else query_sum[g] + part
            pair_sum[k * members : (k + 1) * members] = total.reshape(members, rows, 128)
        for away in range(1, members):
            to = lax.rem(member + away, members)
            if slot > 0:
                give_copy(slot - 1, away).wait_send()
            for g in range(groups):
                give[away - 1, g] = pair_sum[g * members + to].astype(BF16)
            give_copy(slot, away).start()
        for g in range(groups):
            total = jnp.transpose(query_sum[g]) * (HEAD ** -0.5)
            packed = jnp.where(half_low, total[:half], swap_lanes(total[half:])).astype(BF16)

            @pl.when(group != g)
            def _():
                sent_query[slot, g] = packed
                query_copy(slot, g).start()

            @pl.when(group == g)
            def _():
                got_query[group * slots + slot] = packed

        for away in range(1, members):
            give_copy(slot, away).wait_recv()
        for g in range(groups):
            total = pair_sum[g * members + member]
            for away in range(1, members):
                total = total + took[slot, away - 1, g].astype(F32)
            total = total.astype(BF16)

            @pl.when(group != g)
            def _():
                if slot > 0:
                    pair_copy(slot - 1, g).wait_send()
                sent_pair[g] = total
                pair_copy(slot, g).start()

            @pl.when(group == g)
            def _():
                got_pair[group * slots + slot] = total

        advance(*between[slot])

    wide, narrow = two_right[0], two_left[0]
    weight_loads = [
        pltpu.make_async_copy(r["weight"].at[:, pl.ds(0, 2 * D)], wide, load_sems.at[0, 3]),
        pltpu.make_async_copy(r["weight"].at[:, pl.ds(2 * D, D)], narrow, load_sems.at[1, 3]),
    ]
    for copy in weight_loads:
        copy.start()
    for slot in range(slots):
        for away in range(1, groups):
            origin = lax.rem(group + away, groups)
            head = origin * slots + slot
            send(
                sent_query.at[slot, 0], got_query.at[head],
                query_send.at[slot, 0], query_recv.at[head], partner,
            ).wait_recv()
            send(
                sent_pair.at[0], got_pair.at[head], pair_send.at[slot, 0], pair_recv.at[head], partner,
            ).wait_recv()
    for two in range(HEADS // 2):
        columns = slice(two * 128, two * 128 + 128)
        first = got_query[2 * two].astype(F32)
        second = got_query[2 * two + 1].astype(F32)
        result[:half, columns] = jnp.where(half_low, first, swap_lanes(second)).astype(BF16)
        result[half:, columns] = jnp.where(half_low, swap_lanes(first), second).astype(BF16)
        first = got_pair[2 * two].astype(F32)
        second = got_pair[2 * two + 1].astype(F32)
        result[:, slice(D + two * 128, D + two * 128 + 128)] = jnp.where(low, first, swap_lanes(second)).astype(BF16)
        result[:, slice(2 * D + two * 128, 2 * D + two * 128 + 128)] = jnp.where(
            low, swap_lanes(first), second
        ).astype(BF16)
    swaps[4] = last_left + right_swaps(4)
    for copy in swaps[4][2:]:
        copy.start()
    for copy in weight_loads:
        copy.wait()
    normed_grad = back_product(result[:, : 2 * D], wide[...]) + back_product(result[:, 2 * D :], narrow[...])
    values = r["tokens"][...].astype(F32)
    centred = values - jnp.mean(values, axis=1, keepdims=True)
    inverse = lax.rsqrt(jnp.mean(centred * centred, axis=1, keepdims=True) + EPSILON)
    unit = centred * inverse
    vector_rows[0] = jnp.concatenate(
        [jnp.sum(normed_grad * unit, axis=0, keepdims=True), r["vectors"][0:2], jnp.zeros((5, D), F32)], axis=0
    )
    vector_rows[1] = jnp.concatenate(
        [jnp.sum(normed_grad, axis=0, keepdims=True), r["vectors"][2:4], jnp.zeros((5, D), F32)], axis=0
    )
    vector_copy = send(
        vector_rows.at[1 - member], other_rows, swap_send.at[5, 0], swap_recv.at[5, 0], partner
    )
    vector_copy.start()
    advance(8)
    scaled = normed_grad * r["gain"][...]
    r["input_grad"][...] = r["stream_grad"][...] + inverse * (
        scaled
        - jnp.mean(scaled, axis=1, keepdims=True)
        - unit * jnp.mean(scaled * unit, axis=1, keepdims=True)
    )
    advance(9)
    for _ in range(7):
        advance(6, 7, 4, 5, 2, 3, 0, 1, 8, 9)

    for slot in range(slots):
        for away in range(1, members):
            if slot == slots - 1:
                give_copy(slot, away).wait_send()
        for away in range(1, groups):
            origin = lax.rem(group + away, groups)
            out_copy(slot, away).wait_send()
            if slot == slots - 1:
                pair_copy(slot, origin).wait_send()
            query_copy(slot, origin).wait_send()


def tail(plan, batch, grad_out, queries, pairs, outs, logs, starts, lefts, rights, wholes, weight, tokens, gain, stream_grad, vectors):
    devices, groups, members, slots, rows = plan.devices, plan.groups, plan.members, plan.slots, plan.rows
    half = rows // 2
    shares = shares_of(batch, groups, rights[0].shape[1])
    dma = pltpu.SemaphoreType.DMA
    inputs = {"grad_out": grad_out, "logs": logs, "starts": starts, "tokens": tokens, "gain": gain.reshape(1, D)}
    inputs.update(stream_grad=stream_grad, vectors=vectors)
    near = len(inputs)
    inputs.update(queries=queries, pairs=pairs, outs=outs, weight=weight)
    inputs.update({"left%d" % m: left for m, left in enumerate(lefts)})
    inputs.update({"right%d" % m: right for m, right in enumerate(rights)})
    inputs.update({"whole%d" % m: whole for m, whole in enumerate(wholes)})
    widths = [right.shape[1] // 2 for right in rights] + [3 * D // 2]
    steps = [step_shapes(share, batch) for share in shares]
    scratch = [VM((2 * rows, left.shape[1]), BF16) for left in lefts]
    scratch += [VM((2 * rows, width), BF16) for width in widths]
    scratch += [VM((batch, 2, 2, share.rows, share.columns), BF16) for share in shares]
    scratch += [VM(shape, BF16) for shapes in steps for shape in shapes]
    scratch += [
        VM((batch, 2, 2, share.rows, piece.count), BF16)
        for share in shares
        for piece in share.pieces
        if isinstance(piece, Grad)
    ]
    scratch += [
        VM((2, groups, rows, 128), BF16),
        VM((2, devices, rows, 128), BF16),
        VM((2, groups, rows, 128), F32),
        VM((HEADS, half, 128), BF16),
        VM((slots, groups, half, 128), BF16),
        VM((groups, rows, 128), BF16),
        VM((groups, 8, rows), F32),
        VM((devices, rows, 128), F32),
        VM((groups, 128, rows), F32),
        VM((members - 1, groups, rows, 128), BF16),
        VM((slots, members - 1, groups, rows, 128), BF16),
        VM((groups, rows, 128), BF16),
        VM((HEADS, rows, 128), BF16),
        VM((slots, groups, half, 128), BF16),
        VM((HEADS, half, 128), BF16),
        VM((rows, 3 * D), BF16),
        VM((2, 8, D), F32),
        VM((8, D), F32),
        dma((2, 4)),
        dma((slots, groups)),
        dma((slots, groups)),
        dma((slots, members - 1)),
        dma((slots, members - 1)),
        dma((slots, groups)),
        dma((HEADS,)),
        dma((slots, groups)),
        dma((HEADS,)),
        dma((5, 2)),
        dma((6, 2)),
        dma((6, 2)),
        dma((4,)),
        dma((4,)),
        dma((4,)),
        dma((len(shares), 6 + batch)),
        dma((len(shares), 6 + batch)),
        dma((len(shares),)),
    ]
    names = list(inputs) + ["input_grad"]
    out = pl.pallas_call(
        partial(tail_kernel, plan, batch, shares, [len(s) for s in steps], names),
        out_shape=[jax.ShapeDtypeStruct((rows, D), F32)]
        + [jax.ShapeDtypeStruct((2, 2, 2, s.rows, s.columns), BF16) for s in shares],
        in_specs=[pl.BlockSpec(memory_space=VM)] * near + [pl.BlockSpec(memory_space=pl.ANY)] * (len(inputs) - near),
        out_specs=[pl.BlockSpec(memory_space=VM)] + [pl.BlockSpec(memory_space=pl.ANY)] * len(shares),
        scratch_shapes=scratch,
        compiler_params=pltpu.CompilerParams(
            collective_id=1, has_side_effects=True, vmem_limit_bytes=62 << 20
        ),
        name="tail",
    )(*inputs.values())
    return out[0], out[1:]


def widen_kernel(*refs):
    shares, outs = refs[:10], refs[10:]
    down, up, cross_out, memory, query, self_out, self_weight, vector = outs

    def put(out, s, at, first, count):
        for core in range(2):
            width = out.shape[1] // 2
            block = shares[s][core, 0, 0, :, first : first + count]
            out[:, core * width + at : core * width + at + count] = block.astype(F32)

    for part in range(2):
        for core in range(2):
            rows = shares[part].shape[3]
            out_rows = slice(part * rows, part * rows + rows)
            down[out_rows, core * (D // 2) : (core + 1) * (D // 2)] = shares[part][core, 0, 0].astype(F32)
    quarter = up.shape[1] // 4
    put(up, 2, 0, 0, quarter)
    put(up, 3, quarter, 0, quarter)
    put(memory, 4, 0, 0, 512)
    put(memory, 5, 512, 0, 256)
    put(cross_out, 5, 0, 256, D // 2)
    put(query, 6, 0, 0, D // 2)
    put(self_out, 7, 0, 0, D // 2)
    put(self_weight, 8, 0, 0, 640)
    put(self_weight, 9, 640, 0, 512)
    for core in range(2):
        vector[core] = shares[9][core, 0, 0, :, 512:].astype(F32)


def widen(batch, ff, shares):
    ins = [pl.BlockSpec((2, 1, 1) + s.shape[3:], lambda i: (0, i // 2, i % 2, 0, 0)) for s in shares]
    layout = [(ff, D), (D, ff), (D, D), (D, 2 * D), (D, D), (D, D), (D, 3 * D)]
    outs = [pl.BlockSpec((rows // batch // 4, columns), lambda i: (i, 0)) for rows, columns in layout]
    outs.append(pl.BlockSpec((2, D // batch // 4, 128), lambda i: (0, i, 0)))
    return pl.pallas_call(
        widen_kernel,
        grid=(4,),
        in_specs=ins,
        out_specs=outs,
        out_shape=[jax.ShapeDtypeStruct((rows // batch, columns), F32) for rows, columns in layout]
        + [jax.ShapeDtypeStruct((2, D // batch, 128), F32)],
        compiler_params=pltpu.CompilerParams(vmem_limit_bytes=60 << 20),
        name="widen",
    )(*shares)


FOLD = 256 // HEAD


def stack_heads(values):
    lane = lax.broadcasted_iota(jnp.int32, values.shape, 1) // HEAD
    return jnp.concatenate([jnp.where(lane == h, values, jnp.zeros_like(values)) for h in range(FOLD)], axis=0)


def unstack_heads(stacked):
    count = stacked.shape[0] // FOLD
    lane = lax.broadcasted_iota(jnp.int32, (count, stacked.shape[1]), 1) // HEAD
    total = jnp.where(lane == 0, stacked[:count], 0.0)
    for h in range(1, FOLD):
        total = total + jnp.where(lane == h, stacked[h * count : (h + 1) * count], 0.0)
    return total


def cross_chances(queries, keys):
    scores = back_product(queries, keys) * (HEAD ** -0.5)
    chance = jnp.exp(scores - jnp.max(scores, axis=1, keepdims=True))
    return chance / jnp.sum(chance, axis=1, keepdims=True)


def cross_kernel(queries, memory, out):
    for c in range(D // 256):
        columns = slice(c * 256, c * 256 + 256)
        values = slice(D + c * 256, D + c * 256 + 256)
        chances = cross_chances(stack_heads(queries[0, :, columns]), memory[0, :, columns])
        out[0, :, columns] = unstack_heads(matmul(chances.astype(BF16), memory[0, :, values]))


def cross(queries, memory):
    groups, count, _ = queries.shape
    block = lambda *shape: pl.BlockSpec((1,) + shape, lambda i: (i, 0, 0))
    return pl.pallas_call(
        cross_kernel,
        grid=(groups,),
        out_shape=jax.ShapeDtypeStruct((groups, count, D), F32),
        in_specs=[block(count, D), block(SPAN, 2 * D)],
        out_specs=block(count, D),
        compiler_params=pltpu.CompilerParams(vmem_limit_bytes=32 << 20),
        cost_estimate=pl.CostEstimate(flops=4 * groups * 4 * count * SPAN * D, bytes_accessed=8 << 20, transcendentals=0),
        name="cross",
    )(queries, memory)


def uncross_kernel(queries, memory, grads, query_grad, memory_grad):
    for c in range(D // 256):
        columns = slice(c * 256, c * 256 + 256)
        values = slice(D + c * 256, D + c * 256 + 256)
        stacked = stack_heads(queries[0, :, columns])
        stacked_grad = stack_heads(grads[0, :, columns])
        chances = cross_chances(stacked, memory[0, :, columns])
        chance_grad = back_product(stacked_grad, memory[0, :, values])
        total = jnp.sum(chances * chance_grad, axis=1, keepdims=True)
        score_grad = (chances * (chance_grad - total)).astype(BF16)
        query_grad[0, :, columns] = unstack_heads(matmul(score_grad, memory[0, :, columns])) * (HEAD ** -0.5)
        memory_grad[0, :, columns] = (outer_sum(score_grad, stacked) * (HEAD ** -0.5)).astype(BF16)
        memory_grad[0, :, values] = outer_sum(chances.astype(BF16), stacked_grad).astype(BF16)


def uncross(queries, memory, grads):
    groups, count, _ = queries.shape
    block = lambda *shape: pl.BlockSpec((1,) + shape, lambda i: (i, 0, 0))
    return pl.pallas_call(
        uncross_kernel,
        grid=(groups,),
        out_shape=[
            jax.ShapeDtypeStruct((groups, count, D), F32),
            jax.ShapeDtypeStruct((groups, SPAN, 2 * D), BF16),
        ],
        in_specs=[block(count, D), block(SPAN, 2 * D), block(count, D)],
        out_specs=[block(count, D), block(SPAN, 2 * D)],
        compiler_params=pltpu.CompilerParams(vmem_limit_bytes=32 << 20),
        cost_estimate=pl.CostEstimate(flops=10 * groups * 4 * count * SPAN * D, bytes_accessed=16 << 20, transcendentals=0),
        name="uncross",
    )(queries, memory, grads)


def shifted(values, groups, top):
    rows = values.shape[0]
    pad = groups * STRETCH - rows - 1
    return jnp.pad(values, ((1, pad), (0, 0))).reshape(groups, STRETCH, D)


def on_device(devices, batch, tokens, segment_ids, neighbours, first_gain, first_shift, self_weight, self_output, second_gain,
    second_shift, query_weight, memory_weight, cross_output, third_gain, third_shift, up_weight, down_weight, cotangent,
):
    rows = tokens.shape[1]
    plan = Plan(devices, rows)
    seq_index = lax.axis_index("seq")
    stream = tokens[0].astype(F32)
    stretch_count = neighbours.shape[1]
    groups = stretch_count + 1
    neighbour_rows = neighbours[0].reshape(stretch_count * SPAN, D)
    segments = jnp.broadcast_to(segment_ids.astype(F32), (8, rows))
    normed_one_low, queries, pairs, outs, logs, starts, context_low, memory = attend(
        plan, tokens[0], first_gain, first_shift, self_weight, neighbour_rows, memory_weight, segments
    )
    stream_one = stream + matmul(context_low, self_output)
    normed_two, second_back = jax.vjp(full_norm, stream_one, second_gain, second_shift)
    normed_two_low = normed_two.astype(BF16)
    cross_queries = matmul(normed_two_low, query_weight).astype(BF16)
    padded_queries = shifted(cross_queries, groups, 1)
    keep = ((seq_index > 0) | (jnp.arange(rows, dtype=jnp.int32) >= STRETCH - 1)).astype(F32)[:, None]
    cross_context = cross(padded_queries, memory).reshape(groups * STRETCH, D)[1 : rows + 1]
    cross_low = (cross_context * keep).astype(BF16)
    stream_two = stream_one + matmul(cross_low, cross_output)
    normed_three, third_back = jax.vjp(full_norm, stream_two, third_gain, third_shift)
    normed_three_low = normed_three.astype(BF16)
    upper = matmul(normed_three_low, up_weight)
    active, gelu_back = jax.vjp(partial(jax.nn.gelu, approximate=False), upper)
    active_low = active.astype(BF16)
    result = (stream_two + matmul(active_low, down_weight)).astype(BF16)
    grad_low = cotangent[0]
    active_grad = back_product(grad_low, down_weight)
    upper_low = gelu_back(active_grad)[0].astype(BF16)
    stream_part, third_gain_grad, third_shift_grad = third_back(back_product(upper_low, up_weight))
    stream_two_grad = grad_low.astype(F32) + stream_part
    branch_low = stream_two_grad.astype(BF16)
    context_grad = (back_product(branch_low, cross_output) * keep).astype(BF16)
    query_part, memory_part = uncross(padded_queries, memory, shifted(context_grad, groups, 1))
    cross_query_low = query_part.reshape(groups * STRETCH, D)[1 : rows + 1].astype(BF16)
    returned = lax.ppermute(memory_part[0], "seq", [(i, i - 1) for i in range(1, devices)])
    last = (memory_part[stretch_count].astype(F32) + returned.astype(F32)).astype(BF16)
    memory_grad = jnp.concatenate([memory_part[1:stretch_count], last[None]], axis=0).reshape(stretch_count * SPAN, 2 * D)
    neighbour_grad = back_product(memory_grad, memory_weight).reshape(neighbours.shape)
    stream_part, second_gain_grad, second_shift_grad = second_back(back_product(cross_query_low, query_weight))
    stream_one_grad = stream_two_grad + stream_part
    self_low = stream_one_grad.astype(BF16)
    grad_out = back_product(self_low, self_output).astype(BF16)
    vectors = jnp.stack([second_gain_grad, third_gain_grad, second_shift_grad, third_shift_grad])
    vectors = jnp.pad(vectors, ((0, 4), (0, 0)))
    ff = up_weight.shape[1]
    down_whole = outer_sum(active_low, grad_low).astype(BF16).reshape(batch, 2, 2, 2, ff // (batch * 8), D)
    memory_whole = outer_sum(neighbour_rows, memory_grad).astype(BF16).reshape(batch, 2, 2, D // (batch * 4), 2 * D)
    input_grad, shares = tail(
        plan,
        batch,
        grad_out,
        queries,
        pairs,
        outs,
        logs,
        starts,
        [normed_three_low, cross_low, normed_two_low, context_low, normed_one_low],
        [upper_low, branch_low, cross_query_low, self_low],
        [down_whole, memory_whole],
        self_weight,
        tokens[0],
        first_gain,
        stream_one_grad,
        vectors,
    )
    down, up, cross_out, memory_w, query, self_out, self_w, vector = widen(batch, ff, shares)
    return (
        result[None],
        input_grad[None],
        neighbour_grad,
        vector[0, :, 0],
        vector[1, :, 0],
        self_w,
        self_out,
        vector[0, :, 1],
        vector[1, :, 1],
        query,
        memory_w,
        cross_out,
        vector[0, :, 2],
        vector[1, :, 2],
        up,
        down,
    )


def from_behind(array, axis, by):
    devices = lax.axis_size(axis)
    pairs = [(i, i + by) for i in range(devices) if 0 <= i + by < devices]
    return lax.ppermute(array, axis, pairs)


def layer_norm(values, gain, shift):
    mean = jnp.mean(values, axis=-1, keepdims=True)
    centred = values - mean
    spread = jnp.mean(centred * centred, axis=-1, keepdims=True)
    return centred * lax.rsqrt(spread + EPSILON) * gain + shift


def block_rows():
    return 512


def causal_allowed(query_pos, query_seg, key_pos, key_seg):
    return (query_pos[:, None] >= key_pos[None, :]) & (query_seg[:, None] == key_seg[None, :])


def key_block_grads(
    queries, grad_out, log_total, delta, query_pos, query_seg, keys, values, key_pos, key_seg, scale
):
    allowed = causal_allowed(query_pos, query_seg, key_pos, key_seg)[None]
    scores = jnp.einsum("qhd,khd->hqk", queries, keys, preferred_element_type=jnp.float32) * scale
    chances = jnp.where(
        allowed, jnp.exp(jnp.where(allowed, scores, NEGATIVE) - log_total[..., None]), 0.0
    )
    prob_grad = jnp.einsum("qhd,khd->hqk", grad_out, values, preferred_element_type=jnp.float32)
    score_low = (chances * (prob_grad - delta[..., None])).astype(jnp.bfloat16)
    query_part = (
        jnp.einsum("hqk,khd->qhd", score_low, keys, preferred_element_type=jnp.float32) * scale
    )
    key_part = (
        jnp.einsum("hqk,qhd->khd", score_low, queries, preferred_element_type=jnp.float32) * scale
    )
    value_part = jnp.einsum(
        "hqk,qhd->khd", chances.astype(jnp.bfloat16), grad_out, preferred_element_type=jnp.float32
    )
    return (query_part, key_part, value_part)


def plain_on_device(
    tokens,
    segment_ids,
    neighbours,
    first_gain,
    first_shift,
    self_weight,
    self_output,
    second_gain,
    second_shift,
    query_weight,
    memory_weight,
    cross_output,
    third_gain,
    third_shift,
    up_weight,
    down_weight,
    cotangent,
):
    rows = tokens.shape[1]
    seq_index = lax.axis_index("seq")
    scale = HEAD ** (-0.5)
    stream = tokens[0].astype(jnp.float32)
    seg_local = segment_ids[0]
    positions = seq_index * rows + jnp.arange(rows, dtype=jnp.int32)
    normed_one, first_back = jax.vjp(layer_norm, stream, first_gain, first_shift)
    normed_one_low = normed_one.astype(jnp.bfloat16)
    projected = matmul(normed_one_low, self_weight).astype(jnp.bfloat16)
    queries = projected[:, :D].reshape(rows, HEADS, HEAD)
    keys_low = projected[:, D : 2 * D]
    values_low = projected[:, 2 * D :]
    start_state = (
        jnp.full((HEADS, rows), NEGATIVE, jnp.float32),
        jnp.zeros((HEADS, rows), jnp.float32),
        jnp.zeros((HEADS, rows, HEAD), jnp.float32),
    )
    carry = start_state
    piece_keys = lax.all_gather(keys_low, "seq", axis=0, tiled=True)
    piece_values = lax.all_gather(values_low, "seq", axis=0, tiled=True)
    piece_seg = lax.all_gather(seg_local, "seq", axis=0, tiled=True)
    count = piece_keys.shape[0]
    fold_size = block_rows()

    def step(state, index):
        maxes, totals, running = state
        first = index * fold_size
        keys = lax.dynamic_slice_in_dim(piece_keys, first, fold_size, 0).reshape(
            fold_size, HEADS, HEAD
        )
        values = lax.dynamic_slice_in_dim(piece_values, first, fold_size, 0).reshape(
            fold_size, HEADS, HEAD
        )
        key_seg = lax.dynamic_slice_in_dim(piece_seg, first, fold_size, 0)
        key_pos = first + jnp.arange(fold_size, dtype=jnp.int32)
        allowed = causal_allowed(positions, seg_local, key_pos, key_seg)[None]
        scores = (
            jnp.einsum("qhd,khd->hqk", queries, keys, preferred_element_type=jnp.float32) * scale
        )
        scores = jnp.where(allowed, scores, NEGATIVE)
        new_max = jnp.maximum(maxes, jnp.max(scores, axis=-1))
        factor = jnp.exp(maxes - new_max)
        weights = jnp.where(allowed, jnp.exp(scores - new_max[..., None]), 0.0)
        totals = totals * factor + jnp.sum(weights, axis=-1)
        running = running * factor[..., None] + jnp.einsum(
            "hqk,khd->hqd", weights.astype(jnp.bfloat16), values, preferred_element_type=jnp.float32
        )
        return ((new_max, totals, running), None)

    carry, unused = lax.scan(step, carry, jnp.arange(count // fold_size, dtype=jnp.int32))
    maxes, totals, running = carry
    log_total = maxes + jnp.log(totals)
    context = running / totals[..., None]
    context_low = jnp.transpose(context, (1, 0, 2)).reshape(rows, D).astype(jnp.bfloat16)
    stream_one = stream + matmul(context_low, self_output)
    normed_two, second_back = jax.vjp(layer_norm, stream_one, second_gain, second_shift)
    normed_two_low = normed_two.astype(jnp.bfloat16)
    cross_queries = matmul(normed_two_low, query_weight).astype(jnp.bfloat16)
    stretch_count = neighbours.shape[1]
    span = NEIGHBOURS * NEIGHBOUR_LEN
    groups = stretch_count + 1
    neighbour_rows = neighbours[0].reshape(stretch_count * span, D)
    memory = (
        matmul(neighbour_rows, memory_weight)
        .astype(jnp.bfloat16)
        .reshape(stretch_count, span, 2 * D)
    )
    previous = from_behind(memory[stretch_count - 1], "seq", 1)
    extended = jnp.concatenate([previous[None], memory], axis=0)
    memory_keys = extended[:, :, :D].reshape(groups, span, HEADS, HEAD)
    memory_values = extended[:, :, D:].reshape(groups, span, HEADS, HEAD)
    pad_top = jnp.zeros((1, D), jnp.bfloat16)
    pad_end = jnp.zeros((STRETCH - 1, D), jnp.bfloat16)
    padded_queries = jnp.concatenate([pad_top, cross_queries, pad_end], axis=0).reshape(
        groups, STRETCH, HEADS, HEAD
    )
    cross_probs = jax.nn.softmax(
        jnp.einsum(
            "gqhd,gkhd->ghqk", padded_queries, memory_keys, preferred_element_type=jnp.float32
        )
        * scale,
        axis=-1,
    )
    cross_probs_low = cross_probs.astype(jnp.bfloat16)
    keep = ((seq_index > 0) | (jnp.arange(rows, dtype=jnp.int32) >= STRETCH - 1)).astype(
        jnp.float32
    )[:, None]
    cross_context = jnp.einsum(
        "ghqk,gkhd->gqhd", cross_probs_low, memory_values, preferred_element_type=jnp.float32
    ).reshape(groups * STRETCH, D)[1 : rows + 1]
    cross_low = (cross_context * keep).astype(jnp.bfloat16)
    stream_two = stream_one + matmul(cross_low, cross_output)
    normed_three, third_back = jax.vjp(layer_norm, stream_two, third_gain, third_shift)
    normed_three_low = normed_three.astype(jnp.bfloat16)
    upper = matmul(normed_three_low, up_weight)
    active, gelu_back = jax.vjp(partial(jax.nn.gelu, approximate=False), upper)
    active_low = active.astype(jnp.bfloat16)
    result = (stream_two + matmul(active_low, down_weight)).astype(jnp.bfloat16)
    grad_low = cotangent[0]
    down_grad = outer_sum(active_low, grad_low)
    active_grad = back_product(grad_low, down_weight)
    upper_low = gelu_back(active_grad)[0].astype(jnp.bfloat16)
    up_grad = outer_sum(normed_three_low, upper_low)
    stream_part, third_gain_grad, third_shift_grad = third_back(back_product(upper_low, up_weight))
    stream_two_grad = grad_low.astype(jnp.float32) + stream_part
    branch_low = stream_two_grad.astype(jnp.bfloat16)
    cross_output_grad = outer_sum(cross_low, branch_low)
    context_grad = (back_product(branch_low, cross_output) * keep).astype(jnp.bfloat16)
    padded_grad = jnp.concatenate([pad_top, context_grad, pad_end], axis=0).reshape(
        groups, STRETCH, HEADS, HEAD
    )
    prob_grad = jnp.einsum(
        "gqhd,gkhd->ghqk", padded_grad, memory_values, preferred_element_type=jnp.float32
    )
    score_low = (
        cross_probs * (prob_grad - jnp.sum(cross_probs * prob_grad, axis=-1, keepdims=True))
    ).astype(jnp.bfloat16)
    cross_query_low = (
        (
            jnp.einsum(
                "ghqk,gkhd->gqhd", score_low, memory_keys, preferred_element_type=jnp.float32
            )
            * scale
        )
        .reshape(groups * STRETCH, D)[1 : rows + 1]
        .astype(jnp.bfloat16)
    )
    key_part = (
        jnp.einsum("ghqk,gqhd->gkhd", score_low, padded_queries, preferred_element_type=jnp.float32)
        * scale
    )
    value_part = jnp.einsum(
        "ghqk,gqhd->gkhd", cross_probs_low, padded_grad, preferred_element_type=jnp.float32
    )
    extended_grad = jnp.concatenate(
        [key_part.reshape(groups, span, D), value_part.reshape(groups, span, D)], axis=-1
    )
    returned = from_behind(extended_grad[0].astype(jnp.bfloat16), "seq", -1).astype(jnp.float32)
    memory_grad = jnp.concatenate(
        [extended_grad[1:stretch_count], (extended_grad[stretch_count] + returned)[None]], axis=0
    )
    memory_grad = memory_grad.astype(jnp.bfloat16).reshape(stretch_count * span, 2 * D)
    memory_weight_grad = outer_sum(neighbour_rows, memory_grad)
    neighbour_grad = back_product(memory_grad, memory_weight).reshape(neighbours.shape)
    query_weight_grad = outer_sum(normed_two_low, cross_query_low)
    stream_part, second_gain_grad, second_shift_grad = second_back(
        back_product(cross_query_low, query_weight)
    )
    stream_one_grad = stream_two_grad + stream_part
    self_low = stream_one_grad.astype(jnp.bfloat16)
    self_output_grad = outer_sum(context_low, self_low)
    grad_out = back_product(self_low, self_output).astype(jnp.bfloat16).reshape(rows, HEADS, HEAD)
    delta = jnp.sum(jnp.transpose(grad_out.astype(jnp.float32), (1, 0, 2)) * context, axis=-1)
    gathered_keys, gathered_values, gathered_seg = (
        lax.all_gather(keys_low, "seq", axis=0, tiled=True),
        lax.all_gather(values_low, "seq", axis=0, tiled=True),
        lax.all_gather(seg_local, "seq", axis=0, tiled=True),
    )
    total_rows = gathered_keys.shape[0]
    size = block_rows()

    def key_step(query_sum, index):
        first = index * size
        keys = lax.dynamic_slice_in_dim(gathered_keys, first, size, 0).reshape(size, HEADS, HEAD)
        values = lax.dynamic_slice_in_dim(gathered_values, first, size, 0).reshape(
            size, HEADS, HEAD
        )
        key_seg = lax.dynamic_slice_in_dim(gathered_seg, first, size, 0)
        key_pos = first + jnp.arange(size, dtype=jnp.int32)
        query_part, key_block, value_block = key_block_grads(
            queries,
            grad_out,
            log_total,
            delta,
            positions,
            seg_local,
            keys,
            values,
            key_pos,
            key_seg,
            scale,
        )
        pair = jnp.concatenate([key_block.reshape(size, D), value_block.reshape(size, D)], axis=1)
        return (query_sum + query_part, pair)

    query_grad, pairs = lax.scan(
        key_step,
        jnp.zeros((rows, HEADS, HEAD), jnp.float32),
        jnp.arange(total_rows // size, dtype=jnp.int32),
    )
    pair_grad = lax.psum_scatter(
        pairs.reshape(total_rows, 2 * D).astype(jnp.bfloat16),
        "seq",
        scatter_dimension=0,
        tiled=True,
    ).astype(jnp.float32)
    projected_grad = jnp.concatenate([query_grad.reshape(rows, D), pair_grad], axis=1).astype(
        jnp.bfloat16
    )
    self_weight_grad = outer_sum(normed_one_low, projected_grad)
    stream_part, first_gain_grad, first_shift_grad = first_back(
        back_product(projected_grad, self_weight)
    )
    input_grad = stream_one_grad + stream_part
    shares = (
        lax.psum_scatter(
            first_gain_grad.astype(jnp.bfloat16), "batch", scatter_dimension=0, tiled=True
        ).astype(jnp.float32),
        lax.psum_scatter(
            first_shift_grad.astype(jnp.bfloat16), "batch", scatter_dimension=0, tiled=True
        ).astype(jnp.float32),
        lax.psum_scatter(
            self_weight_grad.astype(jnp.bfloat16), "batch", scatter_dimension=0, tiled=True
        ).astype(jnp.float32),
        lax.psum_scatter(
            self_output_grad.astype(jnp.bfloat16), "batch", scatter_dimension=0, tiled=True
        ).astype(jnp.float32),
        lax.psum_scatter(
            second_gain_grad.astype(jnp.bfloat16), "batch", scatter_dimension=0, tiled=True
        ).astype(jnp.float32),
        lax.psum_scatter(
            second_shift_grad.astype(jnp.bfloat16), "batch", scatter_dimension=0, tiled=True
        ).astype(jnp.float32),
        lax.psum_scatter(
            query_weight_grad.astype(jnp.bfloat16), "batch", scatter_dimension=0, tiled=True
        ).astype(jnp.float32),
        lax.psum_scatter(
            memory_weight_grad.astype(jnp.bfloat16), "batch", scatter_dimension=0, tiled=True
        ).astype(jnp.float32),
        lax.psum_scatter(
            cross_output_grad.astype(jnp.bfloat16), "batch", scatter_dimension=0, tiled=True
        ).astype(jnp.float32),
        lax.psum_scatter(
            third_gain_grad.astype(jnp.bfloat16), "batch", scatter_dimension=0, tiled=True
        ).astype(jnp.float32),
        lax.psum_scatter(
            third_shift_grad.astype(jnp.bfloat16), "batch", scatter_dimension=0, tiled=True
        ).astype(jnp.float32),
        lax.psum_scatter(
            up_grad.astype(jnp.bfloat16), "batch", scatter_dimension=0, tiled=True
        ).astype(jnp.float32),
        lax.psum_scatter(
            down_grad.astype(jnp.bfloat16), "batch", scatter_dimension=0, tiled=True
        ).astype(jnp.float32),
    )
    sums = (
        lax.psum(shares[0].astype(jnp.bfloat16), "seq").astype(jnp.float32),
        lax.psum(shares[1].astype(jnp.bfloat16), "seq").astype(jnp.float32),
        lax.psum(shares[2].astype(jnp.bfloat16), "seq").astype(jnp.float32),
        lax.psum(shares[3].astype(jnp.bfloat16), "seq").astype(jnp.float32),
        lax.psum(shares[4].astype(jnp.bfloat16), "seq").astype(jnp.float32),
        lax.psum(shares[5].astype(jnp.bfloat16), "seq").astype(jnp.float32),
        lax.psum(shares[6].astype(jnp.bfloat16), "seq").astype(jnp.float32),
        lax.psum(shares[7].astype(jnp.bfloat16), "seq").astype(jnp.float32),
        lax.psum(shares[8].astype(jnp.bfloat16), "seq").astype(jnp.float32),
        lax.psum(shares[9].astype(jnp.bfloat16), "seq").astype(jnp.float32),
        lax.psum(shares[10].astype(jnp.bfloat16), "seq").astype(jnp.float32),
        lax.psum(shares[11].astype(jnp.bfloat16), "seq").astype(jnp.float32),
        lax.psum(shares[12].astype(jnp.bfloat16), "seq").astype(jnp.float32),
    )
    return (
        result[None],
        input_grad[None],
        neighbour_grad,
        sums[0],
        sums[1],
        sums[2],
        sums[3],
        sums[4],
        sums[5],
        sums[6],
        sums[7],
        sums[8],
        sums[9],
        sums[10],
        sums[11],
        sums[12],
    )


def solution(mesh):
    placed = (
        P("batch", "seq", None),
        P("batch", "seq"),
        P("batch", "seq", None, None, None),
        P(),
        P(),
        P(),
        P(),
        P(),
        P(),
        P(),
        P(),
        P(),
        P(),
        P(),
        P(),
        P(),
        P("batch", "seq", None),
    )
    sizes = mesh.shape
    if sizes["seq"] == 8 and sizes["batch"] == 4:
        body = partial(on_device, sizes["seq"], sizes["batch"])
    else:
        body = plain_on_device
    return jax.shard_map(
        body,
        mesh=mesh,
        in_specs=placed,
        out_specs=(
            P("batch", "seq", None),
            P("batch", "seq", None),
            P("batch", "seq", None, None, None),
            P("batch"),
            P("batch"),
            P("batch", None),
            P("batch", None),
            P("batch"),
            P("batch"),
            P("batch", None),
            P("batch", None),
            P("batch", None),
            P("batch"),
            P("batch"),
            P("batch", None),
            P("batch", None),
        ),
        check_vma=False,
    )
```

```python
import functools
from functools import partial

import jax
import jax.numpy as jnp
from jax import lax
from jax.experimental import pallas as pl
from jax.experimental.pallas import tpu as pltpu
from jax.sharding import PartitionSpec as P
import math

D = 768
HEADS = 12
HEAD = 64
STRETCH = 64
NEIGHBOURS = 2
NEIGHBOUR_LEN = 128
SPAN = NEIGHBOURS * NEIGHBOUR_LEN
EPSILON = 1e-05
NEGATIVE = -1e30
MESH = pl.DeviceIdType.MESH
VM = pltpu.VMEM
F32 = jnp.float32
BF16 = jnp.bfloat16


def matmul(left, right):
    return jnp.dot(left, right, preferred_element_type=F32)


def outer_sum(left, right):
    return lax.dot_general(left, right, (((0,), (0,)), ((), ())), preferred_element_type=F32)


def back_product(left, right):
    return lax.dot_general(left, right, (((1,), (1,)), ((), ())), preferred_element_type=F32)


def low_lanes(shape):
    return lax.broadcasted_iota(jnp.int32, shape, len(shape) - 1) < HEAD


def swap_lanes(values):
    return pltpu.roll(values, HEAD, 1)


def as_row(vector):
    return vector[...].reshape(1, D)


def full_norm(values, gain, shift):
    mean = jnp.mean(values, axis=-1, keepdims=True)
    centred = values - mean
    spread = jnp.mean(centred * centred, axis=-1, keepdims=True)
    return centred * lax.rsqrt(spread + EPSILON) * gain + shift


class Plan:
    def __init__(self, devices, rows):
        self.devices = devices
        self.rows = rows
        self.groups = math.gcd(devices, HEADS)
        self.members = devices // self.groups
        self.slots = HEADS // self.groups

    def place(self):
        me = lax.axis_index("seq")
        return me, lax.div(me, self.members), lax.rem(me, self.members)


def seq_device(index):
    return (index, lax.axis_index("batch"))


def greet(devices):
    barrier = pltpu.get_barrier_semaphore()
    for device in devices:
        pl.semaphore_signal(barrier, inc=1, device_id=device, device_id_type=MESH)
    pl.semaphore_wait(barrier, len(devices))


def send(source, target, send_sem, recv_sem, device):
    return pltpu.make_async_remote_copy(
        src_ref=source,
        dst_ref=target,
        send_sem=send_sem,
        recv_sem=recv_sem,
        device_id=device,
        device_id_type=MESH,
    )


def pack_rows(values, head):
    half = values.shape[0] // 2
    top, bottom = values[:half], values[half:]
    low = low_lanes((half, 2 * HEAD))
    if head % 2 == 0:
        return jnp.where(low, top, swap_lanes(bottom))
    return jnp.where(low, swap_lanes(top), bottom)


def hide(plan, scores, k, g, member, start):
    causal = k == g
    if not (causal or k == 0 or g == plan.groups - 1):
        return scores
    at = lax.broadcasted_iota(jnp.int32, scores.shape, 0)
    allowed = at >= start - k * plan.members * plan.rows
    if causal:
        allowed = allowed & (at <= member * plan.rows + lax.broadcasted_iota(jnp.int32, scores.shape, 1))
    return jnp.where(allowed, scores, NEGATIVE)


def attend_kernel(plan, *refs):
    (
        tokens, gain, shift, segments, far_weight, far_neighbours, far_memory_weight,
        normed, logs, starts, context, edge, far_queries, far_pairs, far_outs, far_memory,
        queries, pairs, outs, memory, weight, neighbours, memory_weight,
        segs, projected, pack_pairs, pack_queries, got_queries, sent_context, got_context,
        pair_send, pair_recv, query_send, query_recv, pass_send, pass_recv,
        back_send, back_recv, seg_send, seg_recv, edge_send, edge_recv, load_sems, memory_sems, store_sems,
    ) = refs
    me, group, member = plan.place()
    devices, groups, members, slots, rows = plan.devices, plan.groups, plan.members, plan.slots, plan.rows
    others = [lax.rem(me + i, devices) for i in range(1, devices)]
    loads = [
        pltpu.make_async_copy(far_weight, weight, load_sems.at[0]),
        pltpu.make_async_copy(far_neighbours, neighbours, load_sems.at[1]),
        pltpu.make_async_copy(far_memory_weight, memory_weight, load_sems.at[2]),
    ]
    for copy in loads:
        copy.start()
    greet([seq_device(o) for o in others])
    half = rows // 2
    stretches = neighbours.shape[0] // SPAN
    low = low_lanes((rows, 2 * HEAD))

    seg_copies = []
    segs[me] = jnp.broadcast_to(segments[...].astype(F32), (8, rows))
    for i, o in enumerate(others):
        copy = send(segs.at[me], segs.at[me], seg_send.at[i], seg_recv.at[me], seq_device(o))
        copy.start()
        seg_copies.append(copy)
    last_rows = pl.ds((stretches - 1) * SPAN, SPAN)
    edge_copy = send(far_neighbours.at[last_rows], edge, edge_send, edge_recv, seq_device(jnp.minimum(me + 1, devices - 1)))

    @pl.when(me < devices - 1)
    def _():
        edge_copy.start()

    normed[...] = full_norm(tokens[...].astype(F32), as_row(gain), as_row(shift)).astype(BF16)

    loads[0].wait()

    @pl.loop(0, 3)
    def _(j):
        columns = pl.ds(pl.multiple_of(j * D, D), D)
        projected[:, columns] = matmul(normed[...], weight[:, columns])

    def pair_copy(slot, away):
        to = lax.rem(group + away, groups)
        return send(
            pack_pairs.at[to * slots + slot], pairs.at[slot, me],
            pair_send.at[slot, away - 1], pair_recv.at[slot, group], seq_device(to * members + member),
        )

    def query_copy(slot, away):
        to = lax.rem(group + away, groups)
        return send(
            pack_queries.at[to * slots + slot], got_queries.at[slot, group],
            query_send.at[slot, away - 1], query_recv.at[slot, group], seq_device(to * members + member),
        )

    def arrived_pair(slot, origin):
        return send(
            pack_pairs.at[0], pairs.at[slot, origin * members + member],
            pair_send.at[slot, 0], pair_recv.at[slot, origin], seq_device(me),
        )

    def arrived_query(slot, origin):
        return send(
            pack_queries.at[0], got_queries.at[slot, origin],
            query_send.at[slot, 0], query_recv.at[slot, origin], seq_device(me),
        )

    def pass_copy(slot, origin, away):
        to = lax.rem(member + away, members)
        place = origin * members + member
        return send(
            pairs.at[slot, place], pairs.at[slot, place],
            pass_send.at[slot, origin, away - 1], pass_recv.at[slot, place], seq_device(group * members + to),
        )

    def passed(slot, origin, away):
        source = lax.rem(member + away, members)
        place = origin * members + source
        return send(
            pairs.at[slot, place], pairs.at[slot, place],
            pass_send.at[slot, origin, 0], pass_recv.at[slot, place], seq_device(me),
        )

    for slot in range(slots):
        for head in range(slot, HEADS, slots):
            block = (head // 2) * 128
            key = projected[:, D + block : D + block + 128]
            value = projected[:, 2 * D + block : 2 * D + block + 128]
            if head % 2 == 0:
                pair = jnp.where(low, key, swap_lanes(value))
            else:
                pair = jnp.where(low, swap_lanes(key), value)
            pack_pairs[head] = pair.astype(BF16)
            query = projected[:, block : block + 128].astype(BF16).astype(F32) * (HEAD ** -0.5)
            pack_queries[head] = pack_rows(query, head).astype(BF16)
        for away in range(1, groups):
            pair_copy(slot, away).start()
            query_copy(slot, away).start()
    for slot in range(slots):
        pairs[slot, me] = pack_pairs[group * slots + slot]
        got_queries[slot, group] = pack_queries[group * slots + slot]
        for away in range(1, members):
            pass_copy(slot, group, away).start()

    for copy in loads[1:]:
        copy.wait()

    def memory_copy(s):
        return pltpu.make_async_copy(memory.at[s], far_memory.at[s], memory_sems.at[s])

    @pl.loop(0, stretches)
    def _(s):
        some = pl.ds(pl.multiple_of(s * SPAN, SPAN), SPAN)
        memory[s + 1] = matmul(neighbours[some], memory_weight[...]).astype(BF16)
        memory_copy(s + 1).start()

    @pl.when(me > 0)
    def _():
        edge_copy.wait_recv()
        memory[0] = matmul(edge[...], memory_weight[...]).astype(BF16)

    @pl.when(me == 0)
    def _():
        memory[0] = jnp.zeros_like(memory[0])
        edge[...] = jnp.zeros_like(edge)

    memory_copy(0).start()

    for copy in seg_copies:
        copy.wait_send()
    for i in range(1, devices):
        source = lax.rem(me + i, devices)
        send(segs.at[source], segs.at[source], seg_send.at[0], seg_recv.at[source], seq_device(me)).wait_recv()

    counts = [
        jnp.sum(jnp.sum((segs[:, 0, :] == value).astype(F32), axis=1, keepdims=True), axis=0, keepdims=True)
        for value in (0.0, 1.0)
    ]
    for g in range(groups):
        mine = segs[g * members + member]
        starts[g] = jnp.where(mine == 0.0, 0.0, counts[0] + jnp.where(mine == 1.0, 0.0, counts[1])).astype(jnp.int32)

    def back_copy(slot, to):
        return send(
            sent_context.at[slot, to], got_context.at[group * slots + slot],
            back_send.at[slot, to], back_recv.at[group * slots + slot], seq_device(to * members + member),
        )

    def stores(slot):
        return [
            pltpu.make_async_copy(queries.at[slot], far_queries.at[slot], store_sems.at[slot, 0]),
            pltpu.make_async_copy(pairs.at[slot], far_pairs.at[slot], store_sems.at[slot, 1]),
            pltpu.make_async_copy(outs.at[slot], far_outs.at[slot], store_sems.at[slot, 2]),
        ]

    def one_slot(slot, carry):
        for away in range(1, groups):
            origin = lax.rem(group + away, groups)
            arrived_pair(slot, origin).wait_recv()
            for beyond in range(1, members):
                pass_copy(slot, origin, beyond).start()
        for away in range(1, groups):
            origin = lax.rem(group + away, groups)
            arrived_query(slot, origin).wait_recv()
        for origin in range(groups):
            for beyond in range(1, members):
                passed(slot, origin, beyond).wait_recv()
        half_low = low_lanes((half, 2 * HEAD))
        for g in range(groups):
            packed = got_queries[slot, g].astype(F32)
            queries[slot, g, :half] = jnp.where(half_low, packed, 0.0).astype(BF16)
            queries[slot, g, half:] = jnp.where(half_low, swap_lanes(packed), 0.0).astype(BF16)
            query = queries[slot, g]
            scores = []
            for k in range(g + 1):
                tile = pairs[slot, k * members : (k + 1) * members].reshape(members * rows, 128)
                scores.append(hide(plan, back_product(tile, query), k, g, member, starts[g][:1]))
            top = functools.reduce(jnp.maximum, [jnp.max(s, axis=0, keepdims=True) for s in scores])
            total, out = 0.0, 0.0
            for k in range(g + 1):
                tile = pairs[slot, k * members : (k + 1) * members].reshape(members * rows, 128)
                chance = jnp.exp(scores[k] - top)
                total = total + jnp.sum(chance, axis=0, keepdims=True)
                out = out + outer_sum(tile, chance.astype(BF16))
            logs[slot, g] = jnp.broadcast_to(top + jnp.log(total), (8, rows))
            done = jnp.transpose(out / total)
            outs[slot, g] = done
            out_low = done.astype(BF16).astype(F32)
            packed_out = jnp.where(half_low, swap_lanes(out_low[:half]), out_low[half:]).astype(BF16)

            @pl.when(group != g)
            def _():
                sent_context[slot, g] = packed_out
                back_copy(slot, g).start()

            @pl.when(group == g)
            def _():
                got_context[group * slots + slot] = packed_out

        for copy in stores(slot):
            copy.start()
        return carry

    lax.fori_loop(0, slots, one_slot, 0)

    @pl.when(me < devices - 1)
    def _():
        edge_copy.wait_send()

    for slot in range(slots):
        for copy in stores(slot):
            copy.wait()
        for away in range(1, groups):
            origin = lax.rem(group + away, groups)
            pair_copy(slot, away).wait_send()
            query_copy(slot, away).wait_send()
            send(
                sent_context.at[slot, 0], got_context.at[origin * slots + slot],
                back_send.at[slot, 0], back_recv.at[origin * slots + slot], seq_device(me),
            ).wait_recv()
            back_copy(slot, origin).wait_send()
        for origin in range(groups):
            for beyond in range(1, members):
                pass_copy(slot, origin, beyond).wait_send()

    @pl.loop(0, stretches + 1)
    def _(s):
        memory_copy(s).wait()

    for two in range(HEADS // 2):
        first = got_context[2 * two].astype(F32)
        second = got_context[2 * two + 1].astype(F32)
        half_low = low_lanes((half, 2 * HEAD))
        columns = slice(two * 128, two * 128 + 128)
        context[:half, columns] = jnp.where(half_low, first, swap_lanes(second)).astype(BF16)
        context[half:, columns] = jnp.where(half_low, swap_lanes(first), second).astype(BF16)


def attend(plan, tokens, gain, shift, segments, weight, neighbours, memory_weight):
    devices, groups, members, slots, rows = plan.devices, plan.groups, plan.members, plan.slots, plan.rows
    half = rows // 2
    stretches = neighbours.shape[0] // SPAN
    dma = pltpu.SemaphoreType.DMA
    near = [
        ((rows, D), BF16),
        ((slots, groups, 8, rows), F32),
        ((groups, 8, rows), jnp.int32),
        ((rows, D), BF16),
        ((SPAN, D), BF16),
    ]
    far = [
        ((slots, groups, rows, 128), BF16),
        ((slots, devices, rows, 128), BF16),
        ((slots, groups, rows, 128), F32),
        ((stretches + 1, SPAN, 2 * D), BF16),
    ]
    vmem, hbm = pl.BlockSpec(memory_space=VM), pl.BlockSpec(memory_space=pl.ANY)
    return pl.pallas_call(
        partial(attend_kernel, plan),
        out_shape=[jax.ShapeDtypeStruct(*s) for s in near + far],
        in_specs=[vmem] * 4 + [hbm] * 3,
        out_specs=[vmem] * len(near) + [hbm] * len(far),
        scratch_shapes=[VM(*s) for s in far]
        + [
            VM(weight.shape, BF16),
            VM(neighbours.shape, BF16),
            VM(memory_weight.shape, BF16),
            VM((devices, 8, rows), F32),
            VM((rows, 3 * D), F32),
            VM((HEADS, rows, 128), BF16),
            VM((HEADS, half, 128), BF16),
            VM((slots, groups, half, 128), BF16),
            VM((slots, groups, half, 128), BF16),
            VM((HEADS, half, 128), BF16),
            dma((slots, groups)),
            dma((slots, groups)),
            dma((slots, groups)),
            dma((slots, groups)),
            dma((slots, groups, members)),
            dma((slots, devices)),
            dma((slots, groups)),
            dma((HEADS,)),
            dma((devices,)),
            dma((devices,)),
            dma,
            dma,
            dma((3,)),
            dma((stretches + 1,)),
            dma((slots, 3)),
        ],
        compiler_params=pltpu.CompilerParams(
            collective_id=0, has_side_effects=True, vmem_limit_bytes=60 << 20
        ),
        name="attend",
    )(tokens, gain, shift, segments, weight, neighbours, memory_weight)


class Grad:
    def __init__(self, matrix, first, count, at=0):
        self.matrix, self.first, self.count, self.at = matrix, first, count, at


class Product:
    def __init__(self, matrix, first, count, at=0):
        self.matrix, self.first, self.count, self.at = matrix, first, count, at


class Share:
    def __init__(self, rows, columns, order, pieces, vectors=None):
        self.rows, self.columns, self.order, self.pieces, self.vectors = rows, columns, order, pieces, vectors


def shares_of(batch, groups, ff):
    short, tall = D // (batch * groups), ff // (batch * groups * 2)
    half = D // 2
    return [
        Share(tall, half, "xyz", []),
        Share(tall, half, "yxz", []),
        Share(short, ff // 4, "xyz", [Product(0, 0, ff // 4)]),
        Share(short, ff // 4, "zyx", [Product(0, ff // 4, ff // 4)]),
        Share(short, 512, "xyz", [Grad(0, 0, 512)]),
        Share(short, 256 + half, "yxz", [Grad(0, 512, 256), Product(0, 0, half, 256)]),
        Share(short, half, "zxy", [Product(1, 0, half)]),
        Share(short, half, "zyx", [Product(2, 0, half)]),
        Share(short, 640, "xyz", [Product(3, 0, 640)]),
        Share(short, 640, "yxz", [Product(3, 640, 512)], vectors=512),
    ]


EARLY = 4


def part_shape(share, batch, axes):
    sizes = {"z": batch, "y": 2, "x": 2}
    return tuple(sizes[a] for a in axes) + (share.rows, share.columns)


def step_shapes(share, batch, axes, order):
    shapes = []
    for axis in order:
        axes = axes.replace(axis, "")
        lead = (batch - 1,) if axis == "z" else ()
        shapes.append(lead + part_shape(share, batch, axes))
    return shapes


def add(a, b):
    return (a.astype(F32) + b.astype(F32)).astype(BF16)


class Engine:
    def __init__(self, plan, batch, shares, sums, arrivals, gathered, send_sems, recv_sems, keep_sems):
        self.plan, self.batch, self.shares = plan, batch, shares
        self.sums, self.arrivals, self.gathered = sums, arrivals, gathered
        self.send_sems, self.recv_sems, self.keep_sems = send_sems, recv_sems, keep_sems
        me, group, member = plan.place()
        self.me, self.group, self.member = me, group, member
        self.z = lax.axis_index("batch")
        self.x, self.y = lax.rem(group, 2), lax.div(group, 2)
        self.partner = seq_device(group * plan.members + 1 - member)
        chip = lambda g: seq_device(g * plan.members + member)
        self.across = {"x": chip(self.y * 2 + 1 - self.x), "y": chip((1 - self.y) * 2 + self.x)}
        self.diagonal = chip((1 - self.y) * 2 + 1 - self.x)
        self.layers = [lax.rem(self.z + i, batch) for i in range(1, batch)]

    def peers(self):
        return [self.partner, self.across["x"], self.across["y"], self.diagonal] + [
            (self.me, layer) for layer in self.layers
        ]

    def steps(self, s, fill, axes, order, stop=None):
        total, share = self.sums[s], self.shares[s]
        own = {"x": self.x, "y": self.y, "z": self.z}
        count = 0

        def sems():
            nonlocal count
            count += 1
            return self.send_sems.at[s, count - 1], self.recv_sems.at[s, count - 1]

        fill()
        done = {}
        for number, axis in enumerate(order):
            where = lambda spots: tuple(spots.get(a, slice(None)) for a in axes)
            arrived = self.arrivals[s][number]
            copies = []
            if axis == "z":
                for i, layer in enumerate(self.layers):
                    copies.append(
                        send(total.at[where({**done, "z": layer})], arrived.at[i], *sems(), (self.me, layer))
                    )
            else:
                copies.append(
                    send(total.at[where({**done, axis: 1 - own[axis]})], arrived, *sems(), self.across[axis])
                )
            for copy in copies:
                copy.start()
            yield
            for copy in copies:
                copy.wait()
            done[axis] = own[axis]
            spot = where(done)
            value = total[spot].astype(F32)
            if axis == "z":
                for i in range(self.batch - 1):
                    value = value + arrived[i].astype(F32)
            else:
                value = value + arrived[...].astype(F32)
            if stop is None:
                total[spot] = value.astype(BF16)
            else:
                stop[...] = value.astype(BF16)
        if stop is not None:
            return
        out = self.gathered[s]
        block = total.at[where(done)]
        first, second = share.order.replace("z", "")[::-1]
        home = out.at[self.member, self.y, self.x]
        keep = pltpu.make_async_copy(block, home, self.keep_sems.at[s])
        keep.start()
        copy = send(block, home, *sems(), self.across[first])
        copy.start()
        yield
        copy.wait()
        came = (self.member, 1 - self.y, self.x) if first == "y" else (self.member, self.y, 1 - self.x)
        copies = [send(block, home, *sems(), self.across[second])]
        copies.append(send(out.at[came], out.at[came], *sems(), self.across[second]))
        for copy in copies:
            copy.start()
        keep.wait()
        yield
        for copy in copies:
            copy.wait()
        copy = send(out.at[self.member], out.at[self.member], *sems(), self.partner)
        copy.start()
        yield
        copy.wait()


def spread_to(target, rows, values, at):
    layers, groups = target.shape[0], target.shape[1] * target.shape[2]
    for layer in range(layers):
        for g in range(groups):
            start = (layer * groups + g) * rows
            target[layer, g // 2, g % 2, :, pl.ds(at, values.shape[1])] = values[start : start + rows].astype(BF16)


def tail_kernel(plan, batch, shares, arrival_counts, names, *refs):
    r = dict(zip(names, refs))
    refs = refs[len(names) :]
    takes = iter(refs)
    neighbour_grad = next(takes)
    gathered = [next(takes) for _ in shares]
    two_left = [next(takes) for _ in range(4)]
    two_right = [next(takes) for _ in range(4)]
    sums = [next(takes) for _ in shares]
    arrivals = [[next(takes) for _ in range(n)] for n in arrival_counts]
    grad_pieces = [piece for share in shares for piece in share.pieces if isinstance(piece, Grad)]
    other_grads = [next(takes) for _ in grad_pieces]
    (
        queries, pairs, outs, pack_grads, got_grads, grads, deltas, pair_sum, query_sum,
        give, took, sent_pair, got_pair, sent_query, got_query, result, vector_rows, other_rows,
        near, slopes, memory_weight, give_grads, stage, edge_sent, edge_got,
        load_sems, out_send, out_recv, give_send, give_recv, pair_send, pair_recv, query_send, query_recv,
        own_sems, swap_send, swap_recv, piece_send, piece_recv, state_sems, near_sems, stage_sems, edge_send, edge_recv, send_sems, recv_sems, keep_sems,
    ) = takes
    me, group, member = plan.place()
    devices, groups, members, slots, rows = plan.devices, plan.groups, plan.members, plan.slots, plan.rows
    half = rows // 2
    half_low = low_lanes((half, 2 * HEAD))
    low = low_lanes((rows, 2 * HEAD))
    engine = Engine(plan, batch, shares, sums, arrivals, gathered, send_sems, recv_sems, keep_sems)
    partner = engine.partner
    before = jnp.maximum(me - 1, 0)
    greet(
        [seq_device(lax.rem(me + i, devices)) for i in range(1, devices)]
        + [(me, layer) for layer in engine.layers]
    )

    def load(slot):
        spot = slot % 2
        return [
            pltpu.make_async_copy(r["queries"].at[slot], queries.at[spot], load_sems.at[spot, 0]),
            pltpu.make_async_copy(r["pairs"].at[slot], pairs.at[spot], load_sems.at[spot, 1]),
            pltpu.make_async_copy(r["outs"].at[slot], outs.at[spot], load_sems.at[spot, 2]),
        ]

    for copy in load(0):
        copy.start()
    for head in range(HEADS):
        block = (head // 2) * 128
        pack_grads[head] = pack_rows(r["grad_out"][:, block : block + 128].astype(F32), head).astype(BF16)

    def out_copy(slot, away):
        to = lax.rem(group + away, groups)
        return send(
            pack_grads.at[to * slots + slot], got_grads.at[slot, group],
            out_send.at[slot, away - 1], out_recv.at[slot, group], seq_device(to * members + member),
        )

    for slot in range(slots):
        for away in range(1, groups):
            out_copy(slot, away).start()
        got_grads[slot, group] = pack_grads[group * slots + slot]

    state_loads = [
        pltpu.make_async_copy(r["state%d" % s], sums[s], state_sems.at[s]) for s in range(EARLY)
    ]
    stretches = r["neighbours"].shape[0] // SPAN
    near_loads = [
        pltpu.make_async_copy(r["edge"], near.at[pl.ds(0, SPAN)], near_sems.at[0]),
        pltpu.make_async_copy(r["neighbours"], near.at[pl.ds(SPAN, stretches * SPAN)], near_sems.at[1]),
        pltpu.make_async_copy(r["memory_grad"], slopes, near_sems.at[2]),
        pltpu.make_async_copy(r["memory_weight"], memory_weight, near_sems.at[3]),
    ]
    for copy in near_loads + state_loads:
        copy.start()

    lefts = [r["left%d" % m] for m in range(4)]
    rights = [r["right%d" % m] for m in range(3)] + [result]
    here, there = pl.ds(0, rows), pl.ds(rows, rows)

    def left_swaps(m):
        return [
            pltpu.make_async_copy(lefts[m], two_left[m].at[here], own_sems.at[m, 0]),
            send(lefts[m], two_left[m].at[there], swap_send.at[m, 0], swap_recv.at[m, 0], partner),
        ]

    def right_swaps(m):
        width = rights[m].shape[1] // 2
        mine = pl.ds(pl.multiple_of(member * width, 128), width)
        theirs = pl.ds(pl.multiple_of((1 - member) * width, 128), width)
        return [
            pltpu.make_async_copy(rights[m].at[:, mine], two_right[m].at[here], own_sems.at[m, 1]),
            send(rights[m].at[:, theirs], two_right[m].at[there], swap_send.at[m, 1], swap_recv.at[m, 1], partner),
        ]

    swaps = {}
    for m in range(3):
        swaps[m] = left_swaps(m) + right_swaps(m)
        for copy in swaps[m]:
            copy.start()
    last_left = left_swaps(3)
    for copy in last_left:
        copy.start()

    pieces = {}
    for s, share in enumerate(shares):
        for piece in share.pieces:
            if isinstance(piece, Grad):
                n = len(pieces)
                pieces[piece] = (n, s, send(
                    give_grads.at[:, :, :, :, pl.ds(piece.first, piece.count)], other_grads[n],
                    piece_send.at[n], piece_recv.at[n], partner,
                ))

    def memory_grads():
        for copy in near_loads:
            copy.wait()
        width = slopes.shape[1] // 2
        for piece, (n, s, copy) in pieces.items():
            for first in range(piece.first, piece.first + piece.count, 256):
                columns = pl.ds(pl.multiple_of((1 - member) * width + first, 256), 256)
                spread_to(give_grads, shares[s].rows, outer_sum(near[...], slopes[:, columns]), first)
            copy.start()
        for piece, (n, s, copy) in pieces.items():
            for first in range(piece.first, piece.first + piece.count, 256):
                columns = pl.ds(pl.multiple_of(member * width + first, 256), 256)
                spread(s, outer_sum(near[...], slopes[:, columns]), piece.at + first - piece.first)

    def edge_copy():
        return send(edge_sent, edge_got, edge_send, edge_recv, seq_device(before))

    def stage_copy(s):
        return pltpu.make_async_copy(
            stage.at[s % 2], neighbour_grad.at[pl.ds(s * SPAN, SPAN)], stage_sems.at[s % 2]
        )

    def neighbour_grads(numbers):
        for s in numbers:
            if s >= 2:
                stage_copy(s - 2).wait()
            part = back_product(slopes[(s + 1) * SPAN : (s + 2) * SPAN, :], memory_weight[...])
            stage[s % 2] = part.astype(BF16)
            if s == stretches - 1:

                @pl.when(me < devices - 1)
                def _():
                    edge_copy().wait_recv()
                    stage[s % 2] = (part + edge_got[...].astype(F32)).astype(BF16)

            stage_copy(s).start()

    waited = set()

    def spread(s, values, at):
        spread_to(sums[s], shares[s].rows, values, at)

    def fill(s):
        for piece in shares[s].pieces:
            if isinstance(piece, Grad):
                n, _, copy = pieces[piece]
                copy.wait()
                for layer in range(batch):
                    columns = pl.ds(piece.at, piece.count)
                    sums[s][layer, :, :, :, columns] = add(sums[s][layer, :, :, :, columns], other_grads[n][layer])
            else:
                m = piece.matrix
                if m not in waited:
                    waited.add(m)
                    for copy in swaps[m]:
                        copy.wait()
                tile = 384 if piece.count % 384 == 0 else 512 if piece.count % 512 == 0 else 128
                for t in range(piece.count // tile):
                    first = piece.first + t * tile
                    spread(s, outer_sum(two_left[m][...], two_right[m][:, first : first + tile]), piece.at + t * tile)
        if shares[s].vectors is not None:
            vector_copy.wait()
            mine = vector_rows[member] + other_rows[...]
            wide = jnp.concatenate([mine, jnp.zeros((120, D), F32)], axis=0)
            spread(s, jnp.transpose(wide), shares[s].vectors)

    def ready(s):
        state_loads[s].wait()

    running = []
    for s, share in enumerate(shares):
        if s < EARLY:
            axes = "zyx".replace(share.order[0], "")
            running.append(engine.steps(s, partial(ready, s), axes, share.order[1:]))
        else:
            running.append(engine.steps(s, partial(fill, s), "zyx", share.order))

    def advance(*numbers):
        for n in numbers:
            next(running[n], None)

    advance(0, 1, 2, 3)
    memory_grads()
    advance(4, 5)
    edge_sent[...] = back_product(slopes[0:SPAN, :], memory_weight[...]).astype(BF16)

    @pl.when(me > 0)
    def _():
        edge_copy().start()

    advance(6, 7)

    def give_copy(slot, away):
        to = lax.rem(member + away, members)
        return send(
            give.at[away - 1], took.at[slot, away - 1],
            give_send.at[slot, away - 1], give_recv.at[slot, away - 1], seq_device(group * members + to),
        )

    def pair_copy(slot, to):
        return send(
            sent_pair.at[to], got_pair.at[group * slots + slot],
            pair_send.at[slot, to], pair_recv.at[group * slots + slot], seq_device(to * members + member),
        )

    def query_copy(slot, to):
        return send(
            sent_query.at[slot, to], got_query.at[group * slots + slot],
            query_send.at[slot, to], query_recv.at[group * slots + slot], seq_device(to * members + member),
        )

    between = [(0, 1, 2, 3), (0, 1, 2, 3, 4, 5), (0, 1, 2, 3, 6, 7)]
    for slot in range(slots):
        spot = slot % 2
        for copy in load(slot):
            copy.wait()
        if slot + 1 < slots:
            for copy in load(slot + 1):
                copy.start()
        for away in range(1, groups):
            origin = lax.rem(group + away, groups)
            send(
                pack_grads.at[0], got_grads.at[slot, origin],
                out_send.at[slot, 0], out_recv.at[slot, origin], partner,
            ).wait_recv()
        for g in range(groups):
            packed = got_grads[slot, g].astype(F32)
            top = jnp.where(half_low, 0.0, swap_lanes(packed))
            bottom = jnp.where(half_low, 0.0, packed)
            grads[g, :half] = top.astype(BF16)
            grads[g, half:] = bottom.astype(BF16)
            product = jnp.concatenate([top, bottom], axis=0) * outs[spot, g]
            deltas[g] = jnp.broadcast_to(jnp.sum(jnp.transpose(product), axis=0, keepdims=True), (8, rows))
        for k in range(groups):
            total = 0.0
            tile = pairs[spot, k * members : (k + 1) * members].reshape(members * rows, 128)
            for g in range(k, groups):
                query, grad = queries[spot, g], grads[g]
                scores = hide(plan, back_product(tile, query), k, g, member, r["starts"][g][:1])
                chance = jnp.exp(scores - r["logs"][slot, g][:1])
                chance_grad = back_product(tile, grad)
                score_grad = (chance * (chance_grad - deltas[g][:1])).astype(BF16)
                total = total + matmul(score_grad, query) + matmul(chance.astype(BF16), grad)
                part = outer_sum(tile, score_grad)
                query_sum[g] = part if k == 0 else query_sum[g] + part
            pair_sum[k * members : (k + 1) * members] = total.reshape(members, rows, 128)
        for away in range(1, members):
            to = lax.rem(member + away, members)
            if slot > 0:
                give_copy(slot - 1, away).wait_send()
            for g in range(groups):
                give[away - 1, g] = pair_sum[g * members + to].astype(BF16)
            give_copy(slot, away).start()
        for g in range(groups):
            total = jnp.transpose(query_sum[g]) * (HEAD ** -0.5)
            packed = jnp.where(half_low, total[:half], swap_lanes(total[half:])).astype(BF16)

            @pl.when(group != g)
            def _():
                sent_query[slot, g] = packed
                query_copy(slot, g).start()

            @pl.when(group == g)
            def _():
                got_query[group * slots + slot] = packed

        for away in range(1, members):
            give_copy(slot, away).wait_recv()
        for g in range(groups):
            total = pair_sum[g * members + member]
            for away in range(1, members):
                total = total + took[slot, away - 1, g].astype(F32)
            total = total.astype(BF16)

            @pl.when(group != g)
            def _():
                if slot > 0:
                    pair_copy(slot - 1, g).wait_send()
                sent_pair[g] = total
                pair_copy(slot, g).start()

            @pl.when(group == g)
            def _():
                got_pair[group * slots + slot] = total

        advance(*between[slot])

    neighbour_grads(range(stretches))
    wide, narrow = slopes.at[pl.ds(0, D)], slopes.at[pl.ds(D, D), pl.ds(0, D)]
    weight_loads = [
        pltpu.make_async_copy(r["weight"].at[:, pl.ds(0, 2 * D)], wide, load_sems.at[0, 3]),
        pltpu.make_async_copy(r["weight"].at[:, pl.ds(2 * D, D)], narrow, load_sems.at[1, 3]),
    ]
    for copy in weight_loads:
        copy.start()
    for slot in range(slots):
        for away in range(1, groups):
            origin = lax.rem(group + away, groups)
            head = origin * slots + slot
            send(
                sent_query.at[slot, 0], got_query.at[head],
                query_send.at[slot, 0], query_recv.at[head], partner,
            ).wait_recv()
            send(
                sent_pair.at[0], got_pair.at[head], pair_send.at[slot, 0], pair_recv.at[head], partner,
            ).wait_recv()
    for two in range(HEADS // 2):
        columns = slice(two * 128, two * 128 + 128)
        first = got_query[2 * two].astype(F32)
        second = got_query[2 * two + 1].astype(F32)
        result[:half, columns] = jnp.where(half_low, first, swap_lanes(second)).astype(BF16)
        result[half:, columns] = jnp.where(half_low, swap_lanes(first), second).astype(BF16)
        first = got_pair[2 * two].astype(F32)
        second = got_pair[2 * two + 1].astype(F32)
        result[:, slice(D + two * 128, D + two * 128 + 128)] = jnp.where(low, first, swap_lanes(second)).astype(BF16)
        result[:, slice(2 * D + two * 128, 2 * D + two * 128 + 128)] = jnp.where(
            low, swap_lanes(first), second
        ).astype(BF16)
    swaps[3] = last_left + right_swaps(3)
    for copy in swaps[3][2:]:
        copy.start()
    for copy in weight_loads:
        copy.wait()
    normed_grad = back_product(result[:, : 2 * D], wide[...]) + back_product(result[:, 2 * D :], narrow[...])
    values = r["tokens"][...].astype(F32)
    centred = values - jnp.mean(values, axis=1, keepdims=True)
    inverse = lax.rsqrt(jnp.mean(centred * centred, axis=1, keepdims=True) + EPSILON)
    unit = centred * inverse
    vector_rows[0] = jnp.concatenate(
        [jnp.sum(normed_grad * unit, axis=0, keepdims=True), r["vectors"][0:2], jnp.zeros((5, D), F32)], axis=0
    )
    vector_rows[1] = jnp.concatenate(
        [jnp.sum(normed_grad, axis=0, keepdims=True), r["vectors"][2:4], jnp.zeros((5, D), F32)], axis=0
    )
    vector_copy = send(
        vector_rows.at[1 - member], other_rows, swap_send.at[4, 0], swap_recv.at[4, 0], partner
    )
    vector_copy.start()
    advance(8)
    scaled = normed_grad * as_row(r["gain"])
    input_grad = r["stream_grad"][...] + inverse * (
        scaled
        - jnp.mean(scaled, axis=1, keepdims=True)
        - unit * jnp.mean(scaled * unit, axis=1, keepdims=True)
    )
    r["input_grad"][...] = input_grad.astype(BF16)
    advance(9)
    for _ in range(7):
        advance(6, 7, 4, 5, 2, 3, 0, 1, 8, 9)

    for s in range(max(stretches - 2, 0), stretches):
        stage_copy(s).wait()

    @pl.when(me > 0)
    def _():
        edge_copy().wait_send()

    for slot in range(slots):
        for away in range(1, members):
            if slot == slots - 1:
                give_copy(slot, away).wait_send()
        for away in range(1, groups):
            origin = lax.rem(group + away, groups)
            out_copy(slot, away).wait_send()
            if slot == slots - 1:
                pair_copy(slot, origin).wait_send()
            query_copy(slot, origin).wait_send()


def tail(plan, batch, grad_out, queries, pairs, outs, logs, starts, lefts, rights, states,
    neighbours, edge, memory_grad, memory_weight, weight, tokens, gain, stream_grad, vectors, ff,
):
    devices, groups, members, slots, rows = plan.devices, plan.groups, plan.members, plan.slots, plan.rows
    half = rows // 2
    shares = shares_of(batch, groups, ff)
    dma = pltpu.SemaphoreType.DMA
    inputs = {"grad_out": grad_out, "logs": logs, "starts": starts, "tokens": tokens, "gain": gain}
    inputs.update(stream_grad=stream_grad, vectors=vectors)
    small = len(inputs)
    inputs.update(queries=queries, pairs=pairs, outs=outs, weight=weight)
    inputs.update({"left%d" % m: left for m, left in enumerate(lefts)})
    inputs.update({"right%d" % m: right for m, right in enumerate(rights)})
    inputs.update({"state%d" % m: state for m, state in enumerate(states)})
    inputs.update(neighbours=neighbours, edge=edge, memory_grad=memory_grad, memory_weight=memory_weight)
    widths = [right.shape[1] // 2 for right in rights] + [3 * D // 2]
    axes = ["zyx".replace(s.order[0], "") if n < EARLY else "zyx" for n, s in enumerate(shares)]
    orders = [s.order[1:] if n < EARLY else s.order for n, s in enumerate(shares)]
    steps = [step_shapes(share, batch, axes[n], orders[n]) for n, share in enumerate(shares)]
    scratch = [VM((2 * rows, left.shape[1]), BF16) for left in lefts]
    scratch += [VM((2 * rows, width), BF16) for width in widths]
    scratch += [VM(part_shape(share, batch, axes[n]), BF16) for n, share in enumerate(shares)]
    scratch += [VM(shape, BF16) for shapes in steps for shape in shapes]
    scratch += [
        VM((batch, 2, 2, share.rows, piece.count), BF16)
        for share in shares[EARLY:]
        for piece in share.pieces
        if isinstance(piece, Grad)
    ]
    span_rows = memory_grad.shape[0]
    scratch += [
        VM((2, groups, rows, 128), BF16),
        VM((2, devices, rows, 128), BF16),
        VM((2, groups, rows, 128), F32),
        VM((HEADS, half, 128), BF16),
        VM((slots, groups, half, 128), BF16),
        VM((groups, rows, 128), BF16),
        VM((groups, 8, rows), F32),
        VM((devices, rows, 128), F32),
        VM((groups, 128, rows), F32),
        VM((members - 1, groups, rows, 128), BF16),
        VM((slots, members - 1, groups, rows, 128), BF16),
        VM((groups, rows, 128), BF16),
        VM((HEADS, rows, 128), BF16),
        VM((slots, groups, half, 128), BF16),
        VM((HEADS, half, 128), BF16),
        VM((rows, 3 * D), BF16),
        VM((2, 8, D), F32),
        VM((8, D), F32),
        VM((span_rows, D), BF16),
        VM((span_rows, 2 * D), BF16),
        VM((D, 2 * D), BF16),
        VM((batch, 2, 2, shares[EARLY].rows, D), BF16),
        VM((2, SPAN, D), BF16),
        VM((SPAN, D), BF16),
        VM((SPAN, D), BF16),
        dma((2, 4)),
        dma((slots, groups)),
        dma((slots, groups)),
        dma((slots, members - 1)),
        dma((slots, members - 1)),
        dma((slots, groups)),
        dma((HEADS,)),
        dma((slots, groups)),
        dma((HEADS,)),
        dma((4, 2)),
        dma((5, 2)),
        dma((5, 2)),
        dma((2,)),
        dma((2,)),
        dma((EARLY,)),
        dma((4,)),
        dma((2,)),
        dma,
        dma,
        dma((len(shares), 6 + batch)),
        dma((len(shares), 6 + batch)),
        dma((len(shares),)),
    ]
    names = list(inputs) + ["input_grad"]
    out = pl.pallas_call(
        partial(tail_kernel, plan, batch, shares, [len(s) for s in steps], names),
        out_shape=[jax.ShapeDtypeStruct((rows, D), BF16), jax.ShapeDtypeStruct(neighbours.shape, BF16)]
        + [jax.ShapeDtypeStruct((2, 2, 2, s.rows, s.columns), BF16) for s in shares],
        in_specs=[pl.BlockSpec(memory_space=VM)] * small + [pl.BlockSpec(memory_space=pl.ANY)] * (len(inputs) - small),
        out_specs=[pl.BlockSpec(memory_space=VM)] + [pl.BlockSpec(memory_space=pl.ANY)] * (1 + len(shares)),
        scratch_shapes=scratch,
        compiler_params=pltpu.CompilerParams(
            collective_id=1, has_side_effects=True, vmem_limit_bytes=62 << 20
        ),
        name="tail",
    )(*inputs.values())
    return out[0], out[1], out[2:]


def widen_kernel(batch, *refs):
    shares, (low_result, low_input, low_neighbour) = refs[:10], refs[10:13]
    down, up, cross_out, memory, query, self_out, self_weight, result, input_grad, neighbour_grad = refs[13:23]
    vectors, kept = refs[23:29], refs[29]
    step = pl.program_id(0)

    def put(out, s, at, first, count):
        for core in range(2):
            width = out.shape[1] // 2
            block = shares[s][core, 0, 0, :, first : first + count]
            out[:, core * width + at : core * width + at + count] = block.astype(F32)

    for part in range(2):
        for core in range(2):
            rows = shares[part].shape[3]
            out_rows = slice(part * rows, part * rows + rows)
            down[out_rows, core * (D // 2) : (core + 1) * (D // 2)] = shares[part][core, 0, 0].astype(F32)
    quarter = up.shape[1] // 4
    put(up, 2, 0, 0, quarter)
    put(up, 3, quarter, 0, quarter)
    put(memory, 4, 0, 0, 512)
    put(memory, 5, 512, 0, 256)
    put(cross_out, 5, 0, 256, D // 2)
    put(query, 6, 0, 0, D // 2)
    put(self_out, 7, 0, 0, D // 2)
    put(self_weight, 8, 0, 0, 640)
    put(self_weight, 9, 640, 0, 512)
    result[...] = low_result[...]
    input_grad[...] = low_input[...].astype(F32)
    neighbour_grad[...] = low_neighbour[...].astype(F32)
    rows = shares[9].shape[3]
    for core in range(2):
        kept[core, pl.ds(pl.multiple_of(step * rows, 16), rows)] = shares[9][core, 0, 0, :, 512:].astype(F32)

    @pl.when(step == 3)
    def _():
        for core in range(2):
            turned = jnp.transpose(kept[core])
            for n in range(3):
                vectors[core * 3 + n][...] = turned[n]


def widen(plan, batch, ff, shares, result, input_grad, neighbour_grad):
    rows = plan.rows
    ins = [pl.BlockSpec((2, 1, 1) + s.shape[3:], lambda i: (0, i // 2, i % 2, 0, 0)) for s in shares]
    passed = [result, input_grad, neighbour_grad]
    ins += [pl.BlockSpec((a.shape[0] // 4, D), lambda i: (i, 0)) for a in passed]
    layout = [(ff, D), (D, ff), (D, D), (D, 2 * D), (D, D), (D, D), (D, 3 * D)]
    layout = [(r // batch, c) for r, c in layout] + [a.shape for a in passed]
    kinds = [F32] * 7 + [BF16, F32, F32]
    outs = [pl.BlockSpec((r // 4, c), lambda i: (i, 0)) for r, c in layout]
    outs += [pl.BlockSpec((D // batch,), lambda i: (0,))] * 6
    return pl.pallas_call(
        partial(widen_kernel, batch),
        grid=(4,),
        in_specs=ins,
        out_specs=outs,
        out_shape=[jax.ShapeDtypeStruct(shape, kind) for shape, kind in zip(layout, kinds)]
        + [jax.ShapeDtypeStruct((D // batch,), F32)] * 6,
        scratch_shapes=[VM((2, D // batch, 128), F32)],
        compiler_params=pltpu.CompilerParams(vmem_limit_bytes=60 << 20),
        name="widen",
    )(*shares, *passed)


FOLD = 256 // HEAD


def stack_heads(values):
    lane = lax.broadcasted_iota(jnp.int32, values.shape, 1) // HEAD
    return jnp.concatenate([jnp.where(lane == h, values, jnp.zeros_like(values)) for h in range(FOLD)], axis=0)


def unstack_heads(stacked):
    count = stacked.shape[0] // FOLD
    lane = lax.broadcasted_iota(jnp.int32, (count, stacked.shape[1]), 1) // HEAD
    total = jnp.where(lane == 0, stacked[:count], 0.0)
    for h in range(1, FOLD):
        total = total + jnp.where(lane == h, stacked[h * count : (h + 1) * count], 0.0)
    return total


def cross_chances(queries, keys):
    scores = back_product(queries, keys)
    chance = jnp.exp(scores - jnp.max(scores, axis=1, keepdims=True))
    return chance / jnp.sum(chance, axis=1, keepdims=True)


def norm_parts(values):
    centred = values - jnp.mean(values, axis=1, keepdims=True)
    inverse = lax.rsqrt(jnp.mean(centred * centred, axis=1, keepdims=True) + EPSILON)
    return centred * inverse, inverse


def norm_back(values, gain, grad):
    unit, inverse = norm_parts(values)
    scaled = grad * gain
    inner = inverse * (
        scaled - jnp.mean(scaled, axis=1, keepdims=True) - unit * jnp.mean(scaled * unit, axis=1, keepdims=True)
    )
    return jnp.sum(grad * unit, axis=0, keepdims=True), jnp.sum(grad, axis=0, keepdims=True), inner


def middle_kernel(plan, batch, shares, arrival_counts, names, *refs):
    r = dict(zip(names, refs))
    takes = iter(refs[len(names) :])
    sums = [next(takes) for _ in range(EARLY)]
    arrivals = [[next(takes) for _ in range(n)] for n in arrival_counts]
    (
        up, down, active, two_normed, give_upper, two_upper, two_grad, slopes,
        stream_one, stream_two, normed_grad, summed, moved_queries, moved_grads, moved,
        load_sems, own_sems, tile_send, tile_recv, swap_send, swap_recv, group_sems, send_sems, recv_sems,
    ) = takes
    me, group, member = plan.place()
    rows, groups = plan.rows, plan.groups
    states = [r["state%d" % s] for s in range(EARLY)]
    engine = Engine(plan, batch, shares, sums, arrivals, None, send_sems, recv_sems, None)
    partner = engine.partner
    greet(engine.peers())
    here, there = pl.ds(0, rows), pl.ds(rows, rows)
    ff = up.shape[1]
    loads = [
        pltpu.make_async_copy(r["memory"], slopes, load_sems.at[2]),
        pltpu.make_async_copy(r["up_weight"], up, load_sems.at[0]),
        pltpu.make_async_copy(r["down_weight"], down, load_sems.at[1]),
    ]
    for copy in loads:
        copy.start()
    half = D // 2
    mine = pl.ds(pl.multiple_of(member * half, 128), half)
    theirs = pl.ds(pl.multiple_of((1 - member) * half, 128), half)
    grad_swap = [
        pltpu.make_async_copy(r["cotangent"].at[:, mine], two_grad.at[here], own_sems.at[0]),
        send(r["cotangent"].at[:, theirs], two_grad.at[there], swap_send.at[0], swap_recv.at[0], partner),
    ]
    for copy in grad_swap:
        copy.start()
    at = lax.broadcasted_iota(jnp.int32, (rows, 1), 0)
    keep = ((me > 0) | (at >= STRETCH - 1)).astype(F32)
    stretches = slopes.shape[0]

    def move(values):
        wide = jnp.concatenate([values, jnp.zeros((STRETCH, D), F32)], axis=0)
        return pltpu.roll(wide, 1, 0).astype(BF16).reshape(stretches, STRETCH, D)

    def move_back():
        whole = moved[...].reshape(stretches * STRETCH, D)
        return pltpu.roll(whole, stretches * STRETCH - 1, 0)[:rows]

    stream_one[...] = r["tokens"][...].astype(F32) + matmul(r["context"][...], r["self_output"][...])
    normed_two = (norm_parts(stream_one[...])[0] * as_row(r["second_gain"]) + as_row(r["second_shift"])).astype(BF16)
    r["normed_two"][...] = normed_two
    cross_queries = matmul(normed_two, r["query_weight"][...]).astype(BF16).astype(F32) * (HEAD ** -0.5)
    moved_queries[...] = move(cross_queries)
    loads[0].wait()

    @pl.loop(0, stretches)
    def _(i):
        for c in range(D // 256):
            columns = slice(c * 256, c * 256 + 256)
            values = slice(D + c * 256, D + c * 256 + 256)
            chances = cross_chances(stack_heads(moved_queries[i, :, columns]), slopes[i, :, columns])
            moved[i, :, columns] = unstack_heads(matmul(chances.astype(BF16), slopes[i, :, values]))

    cross_low = (move_back() * keep).astype(BF16)
    r["cross_low"][...] = cross_low
    stream_two[...] = stream_one[...] + matmul(cross_low, r["cross_output"][...])
    two_normed[here] = (norm_parts(stream_two[...])[0] * as_row(r["third_gain"]) + as_row(r["third_shift"])).astype(BF16)
    normed_swap = send(two_normed.at[here], two_normed.at[there], swap_send.at[1], swap_recv.at[1], partner)
    normed_swap.start()
    normed_grad[...] = jnp.zeros_like(normed_grad)
    summed[...] = jnp.zeros_like(summed)
    for copy in loads[1:]:
        copy.wait()
    tile = 512
    tiles = ff // tile

    def tile_copy(t):
        columns = pl.ds(pl.multiple_of(t * tile, tile), tile)
        return send(
            active.at[here, columns], active.at[there, columns], tile_send.at[t], tile_recv.at[t], partner
        )

    @pl.loop(0, tiles)
    def _(t):
        columns = pl.ds(pl.multiple_of(t * tile, tile), tile)
        upper = matmul(two_normed[here], up[:, columns])
        density = jnp.exp(upper * upper * -0.5) * (2.0 * math.pi) ** -0.5
        below = 0.5 + 0.5 * lax.erf(upper * 0.5 ** 0.5)
        active_low = (upper * below).astype(BF16)
        active[here, columns] = active_low
        tile_copy(t).start()
        grad = back_product(r["cotangent"][...], down[columns])
        upper_low = (grad * (below + upper * density)).astype(BF16)
        spot = pl.ds(pl.multiple_of(lax.rem(t, tiles // 2) * tile, tile), tile)

        @pl.when(lax.div(t, tiles // 2) == member)
        def _():
            two_upper[here, spot] = upper_low

        @pl.when(lax.div(t, tiles // 2) != member)
        def _():
            give_upper[:, spot] = upper_low

        summed[...] += matmul(active_low, down[columns])
        normed_grad[...] += back_product(upper_low, up[:, columns])

    upper_swap = send(give_upper, two_upper.at[there], swap_send.at[2], swap_recv.at[2], partner)
    upper_swap.start()
    r["result"][...] = (stream_two[...] + summed[...]).astype(BF16)

    def fill_down(s):
        if s > 0:
            return
        for copy in grad_swap:
            copy.wait()

        @pl.loop(0, tiles)
        def _(t):
            tile_copy(t).wait()

        deep = ff // batch
        tall = shares[0].rows
        for layer in range(batch):
            values = outer_sum(active[:, layer * deep : (layer + 1) * deep], two_grad[...]).astype(BF16)
            for g in range(groups):
                for part in range(2):
                    start = (g * 2 + part) * tall
                    sums[part][layer, g // 2, g % 2] = values[start : start + tall]

    def fill_up(s):
        if s == 2:
            normed_swap.wait()
            upper_swap.wait()
        piece = shares[s].pieces[0]
        for first in range(0, piece.count, 384):
            tile_values = outer_sum(two_normed[...], two_upper[:, piece.first + first : piece.first + first + 384])
            spread_to(sums[s], shares[s].rows, tile_values, first)

    fills = [fill_down, fill_down, fill_up, fill_up]
    running = [
        engine.steps(s, partial(fills[s], s), "zyx", shares[s].order[:1], states[s]) for s in range(EARLY)
    ]
    for run in running:
        next(run, None)

    gain_grad, shift_grad, inner = norm_back(stream_two[...], as_row(r["third_gain"]), normed_grad[...])
    r["vectors"][1:2] = gain_grad
    r["vectors"][3:4] = shift_grad
    stream_two_grad = r["cotangent"][...].astype(F32) + inner
    normed_grad[...] = stream_two_grad
    branch_low = stream_two_grad.astype(BF16)
    r["branch"][...] = branch_low
    moved_grads[...] = move(back_product(branch_low, r["cross_output"][...]) * keep)

    def group_copy(i):
        return pltpu.make_async_copy(slopes.at[i], r["memory_grad"].at[i], group_sems.at[i])

    @pl.loop(0, stretches)
    def _(i):
        for c in range(D // 256):
            columns = slice(c * 256, c * 256 + 256)
            values = slice(D + c * 256, D + c * 256 + 256)
            stacked = stack_heads(moved_queries[i, :, columns])
            stacked_grad = stack_heads(moved_grads[i, :, columns])
            keys = slopes[i, :, columns]
            chances = cross_chances(stacked, keys)
            chance_grad = back_product(stacked_grad, slopes[i, :, values])
            total = jnp.sum(chances * chance_grad, axis=1, keepdims=True)
            score_grad = (chances * (chance_grad - total)).astype(BF16)
            moved[i, :, columns] = unstack_heads(matmul(score_grad, keys)) * (HEAD ** -0.5)
            slopes[i, :, columns] = outer_sum(score_grad, stacked).astype(BF16)
            slopes[i, :, values] = outer_sum(chances.astype(BF16), stacked_grad).astype(BF16)
        group_copy(i).start()

    query_grad = move_back().astype(BF16)
    r["query_grad"][...] = query_grad
    gain_grad, shift_grad, inner = norm_back(
        stream_one[...], as_row(r["second_gain"]), back_product(query_grad, r["query_weight"][...])
    )
    r["vectors"][0:1] = gain_grad
    r["vectors"][2:3] = shift_grad
    r["vectors"][4:8] = jnp.zeros((4, D), F32)
    stream_one_grad = normed_grad[...] + inner
    r["stream_grad"][...] = stream_one_grad
    self_low = stream_one_grad.astype(BF16)
    r["self_low"][...] = self_low
    r["grad_out"][...] = back_product(self_low, r["self_output"][...]).astype(BF16)
    for run in running:
        next(run, None)

    @pl.loop(0, stretches)
    def _(i):
        group_copy(i).wait()


def middle(plan, batch, tokens, context, self_output, second_gain, second_shift, third_gain, third_shift, query_weight, memory, cross_output, up_weight, down_weight, cotangent):
    rows = plan.rows
    ff = up_weight.shape[1]
    stretches = memory.shape[0]
    shares = shares_of(batch, plan.groups, ff)
    dma = pltpu.SemaphoreType.DMA
    inputs = dict(
        tokens=tokens, context=context, self_output=self_output, second_gain=second_gain, second_shift=second_shift,
        third_gain=third_gain, third_shift=third_shift, query_weight=query_weight,
        cross_output=cross_output, cotangent=cotangent,
    )
    near = len(inputs)
    inputs.update(memory=memory, up_weight=up_weight, down_weight=down_weight)
    low = ((rows, D), BF16)
    outputs = dict(
        result=low, normed_two=low, cross_low=low, branch=low, query_grad=low, self_low=low, grad_out=low,
        stream_grad=((rows, D), F32), vectors=((8, D), F32),
    )
    steps = [step_shapes(shares[s], batch, "zyx", shares[s].order[:1]) for s in range(EARLY)]
    for s in range(EARLY):
        outputs["state%d" % s] = (part_shape(shares[s], batch, "zyx".replace(shares[s].order[0], "")), BF16)
    far = len(outputs)
    outputs["memory_grad"] = (memory.shape, BF16)
    scratch = [VM(part_shape(shares[s], batch, "zyx"), BF16) for s in range(EARLY)]
    scratch += [VM(shape, BF16) for shapes in steps for shape in shapes]
    scratch += [
        VM((D, ff), BF16),
        VM((ff, D), BF16),
        VM((2 * rows, ff), BF16),
        VM((2 * rows, D), BF16),
        VM((rows, ff // 2), BF16),
        VM((2 * rows, ff // 2), BF16),
        VM((2 * rows, D // 2), BF16),
        VM(memory.shape, BF16),
        VM((rows, D), F32),
        VM((rows, D), F32),
        VM((rows, D), F32),
        VM((rows, D), F32),
        VM((stretches, STRETCH, D), BF16),
        VM((stretches, STRETCH, D), BF16),
        VM((stretches, STRETCH, D), F32),
        dma((3,)),
        dma((1,)),
        dma((ff // 512,)),
        dma((ff // 512,)),
        dma((3,)),
        dma((3,)),
        dma((stretches,)),
        dma((EARLY, batch - 1)),
        dma((EARLY, batch - 1)),
    ]
    names = list(inputs) + list(outputs)
    out = pl.pallas_call(
        partial(middle_kernel, plan, batch, shares, [len(s) for s in steps], names),
        out_shape=[jax.ShapeDtypeStruct(*shape) for shape in outputs.values()],
        in_specs=[pl.BlockSpec(memory_space=VM)] * near + [pl.BlockSpec(memory_space=pl.ANY)] * (len(inputs) - near),
        out_specs=[pl.BlockSpec(memory_space=VM)] * far + [pl.BlockSpec(memory_space=pl.ANY)],
        scratch_shapes=scratch,
        compiler_params=pltpu.CompilerParams(
            collective_id=2, has_side_effects=True, vmem_limit_bytes=62 << 20
        ),
        name="middle",
    )(*inputs.values())
    return dict(zip(outputs, out))


def on_device(devices, batch, tokens, segment_ids, neighbours, first_gain, first_shift, self_weight, self_output, second_gain,
    second_shift, query_weight, memory_weight, cross_output, third_gain, third_shift, up_weight, down_weight, cotangent,
):
    rows = tokens.shape[1]
    plan = Plan(devices, rows)
    stretch_count = neighbours.shape[1]
    ff = up_weight.shape[1]
    neighbour_rows = neighbours[0].reshape(stretch_count * SPAN, D)
    normed_one, logs, starts, context, edge, queries, pairs, outs, memory = attend(
        plan, tokens[0], first_gain, first_shift, segment_ids, self_weight, neighbour_rows, memory_weight
    )
    mid = middle(
        plan, batch, tokens[0], context, self_output, second_gain, second_shift, third_gain, third_shift, query_weight,
        memory, cross_output, up_weight, down_weight, cotangent[0],
    )
    input_grad, neighbour_grad, shares = tail(
        plan,
        batch,
        mid["grad_out"],
        queries,
        pairs,
        outs,
        logs,
        starts,
        [mid["cross_low"], mid["normed_two"], context, normed_one],
        [mid["branch"], mid["query_grad"], mid["self_low"]],
        [mid["state%d" % s] for s in range(EARLY)],
        neighbour_rows,
        edge,
        mid["memory_grad"].reshape((stretch_count + 1) * SPAN, 2 * D),
        memory_weight,
        self_weight,
        tokens[0],
        first_gain,
        mid["stream_grad"],
        mid["vectors"],
        ff,
    )
    wide = widen(plan, batch, ff, shares, mid["result"], input_grad, neighbour_grad)
    down, up, cross_out, memory_w, query, self_out, self_w, result, input_grad, neighbour_grad = wide[:10]
    vector = wide[10:]
    return (
        result[None],
        input_grad[None],
        neighbour_grad.reshape(neighbours.shape),
        vector[0],
        vector[3],
        self_w,
        self_out,
        vector[1],
        vector[4],
        query,
        memory_w,
        cross_out,
        vector[2],
        vector[5],
        up,
        down,
    )


def from_behind(array, axis, by):
    devices = lax.axis_size(axis)
    pairs = [(i, i + by) for i in range(devices) if 0 <= i + by < devices]
    return lax.ppermute(array, axis, pairs)


def layer_norm(values, gain, shift):
    mean = jnp.mean(values, axis=-1, keepdims=True)
    centred = values - mean
    spread = jnp.mean(centred * centred, axis=-1, keepdims=True)
    return centred * lax.rsqrt(spread + EPSILON) * gain + shift


def block_rows():
    return 512


def causal_allowed(query_pos, query_seg, key_pos, key_seg):
    return (query_pos[:, None] >= key_pos[None, :]) & (query_seg[:, None] == key_seg[None, :])


def key_block_grads(
    queries, grad_out, log_total, delta, query_pos, query_seg, keys, values, key_pos, key_seg, scale
):
    allowed = causal_allowed(query_pos, query_seg, key_pos, key_seg)[None]
    scores = jnp.einsum("qhd,khd->hqk", queries, keys, preferred_element_type=jnp.float32) * scale
    chances = jnp.where(
        allowed, jnp.exp(jnp.where(allowed, scores, NEGATIVE) - log_total[..., None]), 0.0
    )
    prob_grad = jnp.einsum("qhd,khd->hqk", grad_out, values, preferred_element_type=jnp.float32)
    score_low = (chances * (prob_grad - delta[..., None])).astype(jnp.bfloat16)
    query_part = (
        jnp.einsum("hqk,khd->qhd", score_low, keys, preferred_element_type=jnp.float32) * scale
    )
    key_part = (
        jnp.einsum("hqk,qhd->khd", score_low, queries, preferred_element_type=jnp.float32) * scale
    )
    value_part = jnp.einsum(
        "hqk,qhd->khd", chances.astype(jnp.bfloat16), grad_out, preferred_element_type=jnp.float32
    )
    return (query_part, key_part, value_part)


def plain_on_device(
    tokens,
    segment_ids,
    neighbours,
    first_gain,
    first_shift,
    self_weight,
    self_output,
    second_gain,
    second_shift,
    query_weight,
    memory_weight,
    cross_output,
    third_gain,
    third_shift,
    up_weight,
    down_weight,
    cotangent,
):
    rows = tokens.shape[1]
    seq_index = lax.axis_index("seq")
    scale = HEAD ** (-0.5)
    stream = tokens[0].astype(jnp.float32)
    seg_local = segment_ids[0]
    positions = seq_index * rows + jnp.arange(rows, dtype=jnp.int32)
    normed_one, first_back = jax.vjp(layer_norm, stream, first_gain, first_shift)
    normed_one_low = normed_one.astype(jnp.bfloat16)
    projected = matmul(normed_one_low, self_weight).astype(jnp.bfloat16)
    queries = projected[:, :D].reshape(rows, HEADS, HEAD)
    keys_low = projected[:, D : 2 * D]
    values_low = projected[:, 2 * D :]
    start_state = (
        jnp.full((HEADS, rows), NEGATIVE, jnp.float32),
        jnp.zeros((HEADS, rows), jnp.float32),
        jnp.zeros((HEADS, rows, HEAD), jnp.float32),
    )
    carry = start_state
    piece_keys = lax.all_gather(keys_low, "seq", axis=0, tiled=True)
    piece_values = lax.all_gather(values_low, "seq", axis=0, tiled=True)
    piece_seg = lax.all_gather(seg_local, "seq", axis=0, tiled=True)
    count = piece_keys.shape[0]
    fold_size = block_rows()

    def step(state, index):
        maxes, totals, running = state
        first = index * fold_size
        keys = lax.dynamic_slice_in_dim(piece_keys, first, fold_size, 0).reshape(
            fold_size, HEADS, HEAD
        )
        values = lax.dynamic_slice_in_dim(piece_values, first, fold_size, 0).reshape(
            fold_size, HEADS, HEAD
        )
        key_seg = lax.dynamic_slice_in_dim(piece_seg, first, fold_size, 0)
        key_pos = first + jnp.arange(fold_size, dtype=jnp.int32)
        allowed = causal_allowed(positions, seg_local, key_pos, key_seg)[None]
        scores = (
            jnp.einsum("qhd,khd->hqk", queries, keys, preferred_element_type=jnp.float32) * scale
        )
        scores = jnp.where(allowed, scores, NEGATIVE)
        new_max = jnp.maximum(maxes, jnp.max(scores, axis=-1))
        factor = jnp.exp(maxes - new_max)
        weights = jnp.where(allowed, jnp.exp(scores - new_max[..., None]), 0.0)
        totals = totals * factor + jnp.sum(weights, axis=-1)
        running = running * factor[..., None] + jnp.einsum(
            "hqk,khd->hqd", weights.astype(jnp.bfloat16), values, preferred_element_type=jnp.float32
        )
        return ((new_max, totals, running), None)

    carry, unused = lax.scan(step, carry, jnp.arange(count // fold_size, dtype=jnp.int32))
    maxes, totals, running = carry
    log_total = maxes + jnp.log(totals)
    context = running / totals[..., None]
    context_low = jnp.transpose(context, (1, 0, 2)).reshape(rows, D).astype(jnp.bfloat16)
    stream_one = stream + matmul(context_low, self_output)
    normed_two, second_back = jax.vjp(layer_norm, stream_one, second_gain, second_shift)
    normed_two_low = normed_two.astype(jnp.bfloat16)
    cross_queries = matmul(normed_two_low, query_weight).astype(jnp.bfloat16)
    stretch_count = neighbours.shape[1]
    span = NEIGHBOURS * NEIGHBOUR_LEN
    groups = stretch_count + 1
    neighbour_rows = neighbours[0].reshape(stretch_count * span, D)
    memory = (
        matmul(neighbour_rows, memory_weight)
        .astype(jnp.bfloat16)
        .reshape(stretch_count, span, 2 * D)
    )
    previous = from_behind(memory[stretch_count - 1], "seq", 1)
    extended = jnp.concatenate([previous[None], memory], axis=0)
    memory_keys = extended[:, :, :D].reshape(groups, span, HEADS, HEAD)
    memory_values = extended[:, :, D:].reshape(groups, span, HEADS, HEAD)
    pad_top = jnp.zeros((1, D), jnp.bfloat16)
    pad_end = jnp.zeros((STRETCH - 1, D), jnp.bfloat16)
    padded_queries = jnp.concatenate([pad_top, cross_queries, pad_end], axis=0).reshape(
        groups, STRETCH, HEADS, HEAD
    )
    cross_probs = jax.nn.softmax(
        jnp.einsum(
            "gqhd,gkhd->ghqk", padded_queries, memory_keys, preferred_element_type=jnp.float32
        )
        * scale,
        axis=-1,
    )
    cross_probs_low = cross_probs.astype(jnp.bfloat16)
    keep = ((seq_index > 0) | (jnp.arange(rows, dtype=jnp.int32) >= STRETCH - 1)).astype(
        jnp.float32
    )[:, None]
    cross_context = jnp.einsum(
        "ghqk,gkhd->gqhd", cross_probs_low, memory_values, preferred_element_type=jnp.float32
    ).reshape(groups * STRETCH, D)[1 : rows + 1]
    cross_low = (cross_context * keep).astype(jnp.bfloat16)
    stream_two = stream_one + matmul(cross_low, cross_output)
    normed_three, third_back = jax.vjp(layer_norm, stream_two, third_gain, third_shift)
    normed_three_low = normed_three.astype(jnp.bfloat16)
    upper = matmul(normed_three_low, up_weight)
    active, gelu_back = jax.vjp(partial(jax.nn.gelu, approximate=False), upper)
    active_low = active.astype(jnp.bfloat16)
    result = (stream_two + matmul(active_low, down_weight)).astype(jnp.bfloat16)
    grad_low = cotangent[0]
    down_grad = outer_sum(active_low, grad_low)
    active_grad = back_product(grad_low, down_weight)
    upper_low = gelu_back(active_grad)[0].astype(jnp.bfloat16)
    up_grad = outer_sum(normed_three_low, upper_low)
    stream_part, third_gain_grad, third_shift_grad = third_back(back_product(upper_low, up_weight))
    stream_two_grad = grad_low.astype(jnp.float32) + stream_part
    branch_low = stream_two_grad.astype(jnp.bfloat16)
    cross_output_grad = outer_sum(cross_low, branch_low)
    context_grad = (back_product(branch_low, cross_output) * keep).astype(jnp.bfloat16)
    padded_grad = jnp.concatenate([pad_top, context_grad, pad_end], axis=0).reshape(
        groups, STRETCH, HEADS, HEAD
    )
    prob_grad = jnp.einsum(
        "gqhd,gkhd->ghqk", padded_grad, memory_values, preferred_element_type=jnp.float32
    )
    score_low = (
        cross_probs * (prob_grad - jnp.sum(cross_probs * prob_grad, axis=-1, keepdims=True))
    ).astype(jnp.bfloat16)
    cross_query_low = (
        (
            jnp.einsum(
                "ghqk,gkhd->gqhd", score_low, memory_keys, preferred_element_type=jnp.float32
            )
            * scale
        )
        .reshape(groups * STRETCH, D)[1 : rows + 1]
        .astype(jnp.bfloat16)
    )
    key_part = (
        jnp.einsum("ghqk,gqhd->gkhd", score_low, padded_queries, preferred_element_type=jnp.float32)
        * scale
    )
    value_part = jnp.einsum(
        "ghqk,gqhd->gkhd", cross_probs_low, padded_grad, preferred_element_type=jnp.float32
    )
    extended_grad = jnp.concatenate(
        [key_part.reshape(groups, span, D), value_part.reshape(groups, span, D)], axis=-1
    )
    returned = from_behind(extended_grad[0].astype(jnp.bfloat16), "seq", -1).astype(jnp.float32)
    memory_grad = jnp.concatenate(
        [extended_grad[1:stretch_count], (extended_grad[stretch_count] + returned)[None]], axis=0
    )
    memory_grad = memory_grad.astype(jnp.bfloat16).reshape(stretch_count * span, 2 * D)
    memory_weight_grad = outer_sum(neighbour_rows, memory_grad)
    neighbour_grad = back_product(memory_grad, memory_weight).reshape(neighbours.shape)
    query_weight_grad = outer_sum(normed_two_low, cross_query_low)
    stream_part, second_gain_grad, second_shift_grad = second_back(
        back_product(cross_query_low, query_weight)
    )
    stream_one_grad = stream_two_grad + stream_part
    self_low = stream_one_grad.astype(jnp.bfloat16)
    self_output_grad = outer_sum(context_low, self_low)
    grad_out = back_product(self_low, self_output).astype(jnp.bfloat16).reshape(rows, HEADS, HEAD)
    delta = jnp.sum(jnp.transpose(grad_out.astype(jnp.float32), (1, 0, 2)) * context, axis=-1)
    gathered_keys, gathered_values, gathered_seg = (
        lax.all_gather(keys_low, "seq", axis=0, tiled=True),
        lax.all_gather(values_low, "seq", axis=0, tiled=True),
        lax.all_gather(seg_local, "seq", axis=0, tiled=True),
    )
    total_rows = gathered_keys.shape[0]
    size = block_rows()

    def key_step(query_sum, index):
        first = index * size
        keys = lax.dynamic_slice_in_dim(gathered_keys, first, size, 0).reshape(size, HEADS, HEAD)
        values = lax.dynamic_slice_in_dim(gathered_values, first, size, 0).reshape(
            size, HEADS, HEAD
        )
        key_seg = lax.dynamic_slice_in_dim(gathered_seg, first, size, 0)
        key_pos = first + jnp.arange(size, dtype=jnp.int32)
        query_part, key_block, value_block = key_block_grads(
            queries,
            grad_out,
            log_total,
            delta,
            positions,
            seg_local,
            keys,
            values,
            key_pos,
            key_seg,
            scale,
        )
        pair = jnp.concatenate([key_block.reshape(size, D), value_block.reshape(size, D)], axis=1)
        return (query_sum + query_part, pair)

    query_grad, pairs = lax.scan(
        key_step,
        jnp.zeros((rows, HEADS, HEAD), jnp.float32),
        jnp.arange(total_rows // size, dtype=jnp.int32),
    )
    pair_grad = lax.psum_scatter(
        pairs.reshape(total_rows, 2 * D).astype(jnp.bfloat16),
        "seq",
        scatter_dimension=0,
        tiled=True,
    ).astype(jnp.float32)
    projected_grad = jnp.concatenate([query_grad.reshape(rows, D), pair_grad], axis=1).astype(
        jnp.bfloat16
    )
    self_weight_grad = outer_sum(normed_one_low, projected_grad)
    stream_part, first_gain_grad, first_shift_grad = first_back(
        back_product(projected_grad, self_weight)
    )
    input_grad = stream_one_grad + stream_part
    shares = (
        lax.psum_scatter(
            first_gain_grad.astype(jnp.bfloat16), "batch", scatter_dimension=0, tiled=True
        ).astype(jnp.float32),
        lax.psum_scatter(
            first_shift_grad.astype(jnp.bfloat16), "batch", scatter_dimension=0, tiled=True
        ).astype(jnp.float32),
        lax.psum_scatter(
            self_weight_grad.astype(jnp.bfloat16), "batch", scatter_dimension=0, tiled=True
        ).astype(jnp.float32),
        lax.psum_scatter(
            self_output_grad.astype(jnp.bfloat16), "batch", scatter_dimension=0, tiled=True
        ).astype(jnp.float32),
        lax.psum_scatter(
            second_gain_grad.astype(jnp.bfloat16), "batch", scatter_dimension=0, tiled=True
        ).astype(jnp.float32),
        lax.psum_scatter(
            second_shift_grad.astype(jnp.bfloat16), "batch", scatter_dimension=0, tiled=True
        ).astype(jnp.float32),
        lax.psum_scatter(
            query_weight_grad.astype(jnp.bfloat16), "batch", scatter_dimension=0, tiled=True
        ).astype(jnp.float32),
        lax.psum_scatter(
            memory_weight_grad.astype(jnp.bfloat16), "batch", scatter_dimension=0, tiled=True
        ).astype(jnp.float32),
        lax.psum_scatter(
            cross_output_grad.astype(jnp.bfloat16), "batch", scatter_dimension=0, tiled=True
        ).astype(jnp.float32),
        lax.psum_scatter(
            third_gain_grad.astype(jnp.bfloat16), "batch", scatter_dimension=0, tiled=True
        ).astype(jnp.float32),
        lax.psum_scatter(
            third_shift_grad.astype(jnp.bfloat16), "batch", scatter_dimension=0, tiled=True
        ).astype(jnp.float32),
        lax.psum_scatter(
            up_grad.astype(jnp.bfloat16), "batch", scatter_dimension=0, tiled=True
        ).astype(jnp.float32),
        lax.psum_scatter(
            down_grad.astype(jnp.bfloat16), "batch", scatter_dimension=0, tiled=True
        ).astype(jnp.float32),
    )
    sums = (
        lax.psum(shares[0].astype(jnp.bfloat16), "seq").astype(jnp.float32),
        lax.psum(shares[1].astype(jnp.bfloat16), "seq").astype(jnp.float32),
        lax.psum(shares[2].astype(jnp.bfloat16), "seq").astype(jnp.float32),
        lax.psum(shares[3].astype(jnp.bfloat16), "seq").astype(jnp.float32),
        lax.psum(shares[4].astype(jnp.bfloat16), "seq").astype(jnp.float32),
        lax.psum(shares[5].astype(jnp.bfloat16), "seq").astype(jnp.float32),
        lax.psum(shares[6].astype(jnp.bfloat16), "seq").astype(jnp.float32),
        lax.psum(shares[7].astype(jnp.bfloat16), "seq").astype(jnp.float32),
        lax.psum(shares[8].astype(jnp.bfloat16), "seq").astype(jnp.float32),
        lax.psum(shares[9].astype(jnp.bfloat16), "seq").astype(jnp.float32),
        lax.psum(shares[10].astype(jnp.bfloat16), "seq").astype(jnp.float32),
        lax.psum(shares[11].astype(jnp.bfloat16), "seq").astype(jnp.float32),
        lax.psum(shares[12].astype(jnp.bfloat16), "seq").astype(jnp.float32),
    )
    return (
        result[None],
        input_grad[None],
        neighbour_grad,
        sums[0],
        sums[1],
        sums[2],
        sums[3],
        sums[4],
        sums[5],
        sums[6],
        sums[7],
        sums[8],
        sums[9],
        sums[10],
        sums[11],
        sums[12],
    )


def solution(mesh):
    placed = (
        P("batch", "seq", None),
        P("batch", "seq"),
        P("batch", "seq", None, None, None),
        P(),
        P(),
        P(),
        P(),
        P(),
        P(),
        P(),
        P(),
        P(),
        P(),
        P(),
        P(),
        P(),
        P("batch", "seq", None),
    )
    sizes = mesh.shape
    if sizes["seq"] == 8 and sizes["batch"] == 4:
        body = partial(on_device, sizes["seq"], sizes["batch"])
    else:
        body = plain_on_device
    return jax.shard_map(
        body,
        mesh=mesh,
        in_specs=placed,
        out_specs=(
            P("batch", "seq", None),
            P("batch", "seq", None),
            P("batch", "seq", None, None, None),
            P("batch"),
            P("batch"),
            P("batch", None),
            P("batch", None),
            P("batch"),
            P("batch"),
            P("batch", None),
            P("batch", None),
            P("batch", None),
            P("batch"),
            P("batch"),
            P("batch", None),
            P("batch", None),
        ),
        check_vma=False,
    )
```

```python
import functools
from functools import partial

import jax
import jax.numpy as jnp
from jax import lax
from jax.experimental import pallas as pl
from jax.experimental.pallas import tpu as pltpu
from jax.sharding import PartitionSpec as P
import math
from types import SimpleNamespace

D = 768
HEADS = 12
HEAD = 64
STRETCH = 64
NEIGHBOURS = 2
NEIGHBOUR_LEN = 128
SPAN = NEIGHBOURS * NEIGHBOUR_LEN
EPSILON = 1e-05
NEGATIVE = -1e30
MESH = pl.DeviceIdType.MESH
VM = pltpu.VMEM
F32 = jnp.float32
BF16 = jnp.bfloat16


def matmul(left, right):
    return jnp.dot(left, right, preferred_element_type=F32)


def outer_sum(left, right):
    return lax.dot_general(left, right, (((0,), (0,)), ((), ())), preferred_element_type=F32)


def back_product(left, right):
    return lax.dot_general(left, right, (((1,), (1,)), ((), ())), preferred_element_type=F32)


def low_lanes(shape):
    return lax.broadcasted_iota(jnp.int32, shape, len(shape) - 1) < HEAD


def swap_lanes(values):
    return pltpu.roll(values, HEAD, 1)


def as_row(vector):
    return vector[...].reshape(1, D)


def full_norm(values, gain, shift):
    mean = jnp.mean(values, axis=-1, keepdims=True)
    centred = values - mean
    spread = jnp.mean(centred * centred, axis=-1, keepdims=True)
    return centred * lax.rsqrt(spread + EPSILON) * gain + shift


class Plan:
    def __init__(self, devices, rows):
        self.devices = devices
        self.rows = rows
        self.groups = math.gcd(devices, HEADS)
        self.members = devices // self.groups
        self.slots = HEADS // self.groups

    def place(self):
        me = lax.axis_index("seq")
        return me, lax.div(me, self.members), lax.rem(me, self.members)


def seq_device(index):
    return (index, lax.axis_index("batch"))


def greet(devices):
    barrier = pltpu.get_barrier_semaphore()
    for device in devices:
        pl.semaphore_signal(barrier, inc=1, device_id=device, device_id_type=MESH)
    pl.semaphore_wait(barrier, len(devices))


def send(source, target, send_sem, recv_sem, device):
    return pltpu.make_async_remote_copy(
        src_ref=source,
        dst_ref=target,
        send_sem=send_sem,
        recv_sem=recv_sem,
        device_id=device,
        device_id_type=MESH,
    )


def pack_rows(values, head):
    half = values.shape[0] // 2
    top, bottom = values[:half], values[half:]
    low = low_lanes((half, 2 * HEAD))
    if head % 2 == 0:
        return jnp.where(low, top, swap_lanes(bottom))
    return jnp.where(low, swap_lanes(top), bottom)


def hide(plan, scores, k, g, member, start):
    causal = k == g
    if not (causal or k == 0 or g == plan.groups - 1):
        return scores
    at = lax.broadcasted_iota(jnp.int32, scores.shape, 0)
    allowed = at >= start - k * plan.members * plan.rows
    if causal:
        allowed = allowed & (at <= member * plan.rows + lax.broadcasted_iota(jnp.int32, scores.shape, 1))
    return jnp.where(allowed, scores, NEGATIVE)


def attend_kernel(plan, *refs):
    (
        tokens, gain, shift, segments, far_weight, far_neighbours, far_memory_weight,
        normed, logs, starts, context, edge, far_queries, far_pairs, far_outs, far_memory, far_packed,
        queries, pairs, outs, memory, packed, weight, neighbours, memory_weight,
        segs, projected, pack_pairs, pack_queries, got_queries, sent_context, got_context,
        pair_send, pair_recv, query_send, query_recv, pass_send, pass_recv,
        back_send, back_recv, seg_send, seg_recv, edge_send, edge_recv, load_sems, memory_sems, store_sems,
    ) = refs
    me, group, member = plan.place()
    devices, groups, members, slots, rows = plan.devices, plan.groups, plan.members, plan.slots, plan.rows
    others = [lax.rem(me + i, devices) for i in range(1, devices)]
    loads = [
        pltpu.make_async_copy(far_weight, weight, load_sems.at[0]),
        pltpu.make_async_copy(far_neighbours, neighbours, load_sems.at[1]),
        pltpu.make_async_copy(far_memory_weight, memory_weight, load_sems.at[2]),
    ]
    for copy in loads:
        copy.start()
    greet([seq_device(o) for o in others])
    half = rows // 2
    stretches = neighbours.shape[0] // SPAN
    low = low_lanes((rows, 2 * HEAD))

    seg_copies = []
    segs[me] = jnp.broadcast_to(segments[...].astype(F32), (8, rows))
    for i, o in enumerate(others):
        copy = send(segs.at[me], segs.at[me], seg_send.at[i], seg_recv.at[me], seq_device(o))
        copy.start()
        seg_copies.append(copy)
    last_rows = pl.ds((stretches - 1) * SPAN, SPAN)
    edge_copy = send(far_neighbours.at[last_rows], edge, edge_send, edge_recv, seq_device(jnp.minimum(me + 1, devices - 1)))

    @pl.when(me < devices - 1)
    def _():
        edge_copy.start()

    normed[...] = full_norm(tokens[...].astype(F32), as_row(gain), as_row(shift)).astype(BF16)

    loads[0].wait()

    @pl.loop(0, 3)
    def _(j):
        columns = pl.ds(pl.multiple_of(j * D, D), D)
        projected[:, columns] = matmul(normed[...], weight[:, columns])

    def pair_copy(slot, away):
        to = lax.rem(group + away, groups)
        return send(
            pack_pairs.at[to * slots + slot], pairs.at[slot, me],
            pair_send.at[slot, away - 1], pair_recv.at[slot, group], seq_device(to * members + member),
        )

    def query_copy(slot, away):
        to = lax.rem(group + away, groups)
        return send(
            pack_queries.at[to * slots + slot], got_queries.at[slot, group],
            query_send.at[slot, away - 1], query_recv.at[slot, group], seq_device(to * members + member),
        )

    def arrived_pair(slot, origin):
        return send(
            pack_pairs.at[0], pairs.at[slot, origin * members + member],
            pair_send.at[slot, 0], pair_recv.at[slot, origin], seq_device(me),
        )

    def arrived_query(slot, origin):
        return send(
            pack_queries.at[0], got_queries.at[slot, origin],
            query_send.at[slot, 0], query_recv.at[slot, origin], seq_device(me),
        )

    def pass_copy(slot, origin, away):
        to = lax.rem(member + away, members)
        place = origin * members + member
        return send(
            pairs.at[slot, place], pairs.at[slot, place],
            pass_send.at[slot, origin, away - 1], pass_recv.at[slot, place], seq_device(group * members + to),
        )

    def passed(slot, origin, away):
        source = lax.rem(member + away, members)
        place = origin * members + source
        return send(
            pairs.at[slot, place], pairs.at[slot, place],
            pass_send.at[slot, origin, 0], pass_recv.at[slot, place], seq_device(me),
        )

    for slot in range(slots):
        for head in range(slot, HEADS, slots):
            block = (head // 2) * 128
            key = projected[:, D + block : D + block + 128]
            value = projected[:, 2 * D + block : 2 * D + block + 128]
            if head % 2 == 0:
                pair = jnp.where(low, key, swap_lanes(value))
            else:
                pair = jnp.where(low, swap_lanes(key), value)
            pack_pairs[head] = pair.astype(BF16)
            query = projected[:, block : block + 128].astype(BF16).astype(F32) * (HEAD ** -0.5)
            pack_queries[head] = pack_rows(query, head).astype(BF16)
        for away in range(1, groups):
            pair_copy(slot, away).start()
            query_copy(slot, away).start()
    for slot in range(slots):
        pairs[slot, me] = pack_pairs[group * slots + slot]
        got_queries[slot, group] = pack_queries[group * slots + slot]
        for away in range(1, members):
            pass_copy(slot, group, away).start()

    for copy in loads[1:]:
        copy.wait()

    def memory_copy(s):
        return pltpu.make_async_copy(memory.at[s], far_memory.at[s], memory_sems.at[s])

    @pl.loop(0, stretches)
    def _(s):
        some = pl.ds(pl.multiple_of(s * SPAN, SPAN), SPAN)
        memory[s + 1] = matmul(neighbours[some], memory_weight[...]).astype(BF16)
        memory_copy(s + 1).start()

    @pl.when(me > 0)
    def _():
        edge_copy.wait_recv()
        memory[0] = matmul(edge[...], memory_weight[...]).astype(BF16)

    @pl.when(me == 0)
    def _():
        memory[0] = jnp.zeros_like(memory[0])
        edge[...] = jnp.zeros_like(edge)

    memory_copy(0).start()

    per = groups // members
    wide_low = low_lanes((D, 2 * HEAD))

    def columns_of(part, head):
        first = part * D + head // 2 * 128
        return weight[:, first : first + 128].astype(F32), head % 2

    for slot in range(slots):
        for owner in range(members):
            heads = [(owner * per + i) * slots + slot for i in range(per)]
            first = (slot * members + owner) * per * 3 * HEAD
            for i, head in enumerate(heads):
                (key, odd), (value, _) = columns_of(1, head), columns_of(2, head)
                pair = jnp.where(wide_low, swap_lanes(key), value) if odd else jnp.where(wide_low, key, swap_lanes(value))
                packed[:, first + i * 128 : first + i * 128 + 128] = pair.astype(BF16)
            (one, odd), (two, other) = columns_of(0, heads[0]), columns_of(0, heads[1])
            pair = jnp.where(wide_low, swap_lanes(one) if odd else one, two if other else swap_lanes(two))
            packed[:, first + per * 128 : first + per * 128 + 128] = pair.astype(BF16)
    packed_copy = pltpu.make_async_copy(packed, far_packed, memory_sems.at[stretches + 1])
    packed_copy.start()

    for copy in seg_copies:
        copy.wait_send()
    for i in range(1, devices):
        source = lax.rem(me + i, devices)
        send(segs.at[source], segs.at[source], seg_send.at[0], seg_recv.at[source], seq_device(me)).wait_recv()

    counts = [
        jnp.sum(jnp.sum((segs[:, 0, :] == value).astype(F32), axis=1, keepdims=True), axis=0, keepdims=True)
        for value in (0.0, 1.0)
    ]
    for g in range(groups):
        mine = segs[g * members + member]
        starts[g] = jnp.where(mine == 0.0, 0.0, counts[0] + jnp.where(mine == 1.0, 0.0, counts[1])).astype(jnp.int32)

    def back_copy(slot, to):
        return send(
            sent_context.at[slot, to], got_context.at[group * slots + slot],
            back_send.at[slot, to], back_recv.at[group * slots + slot], seq_device(to * members + member),
        )

    def stores(slot):
        return [
            pltpu.make_async_copy(queries.at[slot], far_queries.at[slot], store_sems.at[slot, 0]),
            pltpu.make_async_copy(pairs.at[slot], far_pairs.at[slot], store_sems.at[slot, 1]),
            pltpu.make_async_copy(outs.at[slot], far_outs.at[slot], store_sems.at[slot, 2]),
        ]

    def one_slot(slot, carry):
        for away in range(1, groups):
            origin = lax.rem(group + away, groups)
            arrived_pair(slot, origin).wait_recv()
            for beyond in range(1, members):
                pass_copy(slot, origin, beyond).start()
        for away in range(1, groups):
            origin = lax.rem(group + away, groups)
            arrived_query(slot, origin).wait_recv()
        for origin in range(groups):
            for beyond in range(1, members):
                passed(slot, origin, beyond).wait_recv()
        half_low = low_lanes((half, 2 * HEAD))
        for g in range(groups):
            packed = got_queries[slot, g].astype(F32)
            queries[slot, g, :half] = jnp.where(half_low, packed, 0.0).astype(BF16)
            queries[slot, g, half:] = jnp.where(half_low, swap_lanes(packed), 0.0).astype(BF16)
            query = queries[slot, g]
            scores = []
            for k in range(g + 1):
                tile = pairs[slot, k * members : (k + 1) * members].reshape(members * rows, 128)
                scores.append(hide(plan, back_product(tile, query), k, g, member, starts[g][:1]))
            top = functools.reduce(jnp.maximum, [jnp.max(s, axis=0, keepdims=True) for s in scores])
            total, out = 0.0, 0.0
            for k in range(g + 1):
                tile = pairs[slot, k * members : (k + 1) * members].reshape(members * rows, 128)
                chance = jnp.exp(scores[k] - top)
                total = total + jnp.sum(chance, axis=0, keepdims=True)
                out = out + outer_sum(tile, chance.astype(BF16))
            logs[slot, g] = jnp.broadcast_to(top + jnp.log(total), (8, rows))
            done = jnp.transpose(out / total)
            outs[slot, g] = done
            out_low = done.astype(BF16).astype(F32)
            packed_out = jnp.where(half_low, swap_lanes(out_low[:half]), out_low[half:]).astype(BF16)

            @pl.when(group != g)
            def _():
                sent_context[slot, g] = packed_out
                back_copy(slot, g).start()

            @pl.when(group == g)
            def _():
                got_context[group * slots + slot] = packed_out

        for copy in stores(slot):
            copy.start()
        return carry

    lax.fori_loop(0, slots, one_slot, 0)

    @pl.when(me < devices - 1)
    def _():
        edge_copy.wait_send()

    for slot in range(slots):
        for copy in stores(slot):
            copy.wait()
        for away in range(1, groups):
            origin = lax.rem(group + away, groups)
            pair_copy(slot, away).wait_send()
            query_copy(slot, away).wait_send()
            send(
                sent_context.at[slot, 0], got_context.at[origin * slots + slot],
                back_send.at[slot, 0], back_recv.at[origin * slots + slot], seq_device(me),
            ).wait_recv()
            back_copy(slot, origin).wait_send()
        for origin in range(groups):
            for beyond in range(1, members):
                pass_copy(slot, origin, beyond).wait_send()

    packed_copy.wait()

    @pl.loop(0, stretches + 1)
    def _(s):
        memory_copy(s).wait()

    for two in range(HEADS // 2):
        first = got_context[2 * two].astype(F32)
        second = got_context[2 * two + 1].astype(F32)
        half_low = low_lanes((half, 2 * HEAD))
        columns = slice(two * 128, two * 128 + 128)
        context[:half, columns] = jnp.where(half_low, first, swap_lanes(second)).astype(BF16)
        context[half:, columns] = jnp.where(half_low, swap_lanes(first), second).astype(BF16)


def attend(plan, tokens, gain, shift, segments, weight, neighbours, memory_weight):
    devices, groups, members, slots, rows = plan.devices, plan.groups, plan.members, plan.slots, plan.rows
    half = rows // 2
    stretches = neighbours.shape[0] // SPAN
    dma = pltpu.SemaphoreType.DMA
    near = [
        ((rows, D), BF16),
        ((slots, groups, 8, rows), F32),
        ((groups, 8, rows), jnp.int32),
        ((rows, D), BF16),
        ((SPAN, D), BF16),
    ]
    far = [
        ((slots, groups, rows, 128), BF16),
        ((slots, devices, rows, 128), BF16),
        ((slots, groups, rows, 128), F32),
        ((stretches + 1, SPAN, 2 * D), BF16),
        ((D, 3 * D), BF16),
    ]
    vmem, hbm = pl.BlockSpec(memory_space=VM), pl.BlockSpec(memory_space=pl.ANY)
    return pl.pallas_call(
        partial(attend_kernel, plan),
        out_shape=[jax.ShapeDtypeStruct(*s) for s in near + far],
        in_specs=[vmem] * 4 + [hbm] * 3,
        out_specs=[vmem] * len(near) + [hbm] * len(far),
        scratch_shapes=[VM(*s) for s in far]
        + [
            VM(weight.shape, BF16),
            VM(neighbours.shape, BF16),
            VM(memory_weight.shape, BF16),
            VM((devices, 8, rows), F32),
            VM((rows, 3 * D), F32),
            VM((HEADS, rows, 128), BF16),
            VM((HEADS, half, 128), BF16),
            VM((slots, groups, half, 128), BF16),
            VM((slots, groups, half, 128), BF16),
            VM((HEADS, half, 128), BF16),
            dma((slots, groups)),
            dma((slots, groups)),
            dma((slots, groups)),
            dma((slots, groups)),
            dma((slots, groups, members)),
            dma((slots, devices)),
            dma((slots, groups)),
            dma((HEADS,)),
            dma((devices,)),
            dma((devices,)),
            dma,
            dma,
            dma((3,)),
            dma((stretches + 2,)),
            dma((slots, 3)),
        ],
        compiler_params=pltpu.CompilerParams(
            collective_id=0, has_side_effects=True, vmem_limit_bytes=60 << 20
        ),
        name="attend",
    )(tokens, gain, shift, segments, weight, neighbours, memory_weight)


class Product:
    def __init__(self, matrix, first, count, at=0):
        self.matrix, self.first, self.count, self.at = matrix, first, count, at


class Share:
    def __init__(self, rows, columns, order, pieces, vectors=None):
        self.rows, self.columns, self.order, self.pieces, self.vectors = rows, columns, order, pieces, vectors


def shares_of(batch, groups, ff):
    short, tall = D // (batch * groups), ff // (batch * groups * 2)
    half = D // 2
    return [
        Share(tall, half, "xzy", []),
        Share(tall, half, "yxz", []),
        Share(short, ff // 4, "xzy", [Product(0, 0, ff // 4)]),
        Share(short, ff // 4, "zyx", [Product(0, ff // 4, ff // 4)]),
        Share(short, 512, "xyz", []),
        Share(short, 256 + half, "yxz", [Product(0, 0, half, 256)]),
        Share(short, half, "yzx", [Product(1, 0, half)]),
        Share(short, half, "zyx", [Product(2, 0, half)]),
        Share(short, half, "xyz", [Product(3, 0, half)]),
        Share(short, half, "zyx", [Product(4, 0, half)]),
        Share(short, 256, "xzy", [Product(5, 0, 256)]),
        Share(short, 256, "yxz", [Product(5, 256, 128)], vectors=128),
    ]


EARLY = 4

SCHEDULE = (
    (), (), (), (), (), (), (-1, 5, 4, 3), (8,), (1, 6), (0, 2), (-2, 8, 0, 3), (9, 5, 1, 2), (),
    (7, 0, 1, 2), (10, 4, 3), (11, 1), (5, 0), (8, 2, 3, 1), (9, 6, 7, 0), (10, 11, 4, 5, 2, 3), (9, 6, 8),
    (11, 7, 4), (9,), (10,), (6,), (8,), (5,), (7,), (11,), (10,), (5,), (9,), (6,), (10,), (11,), (4,), (8,),
    (7,), (6,), (9,), (4,), (10,), (11,), (7,), (8,), (9,), (10,), (11,),
)


def part_shape(share, batch, axes):
    sizes = {"z": batch, "y": 2, "x": 2}
    return tuple(sizes[a] for a in axes) + (share.rows, share.columns)


def step_shapes(share, batch, axes, order):
    shapes = []
    for axis in order:
        axes = axes.replace(axis, "")
        lead = (batch - 1,) if axis == "z" else ()
        shapes.append(lead + part_shape(share, batch, axes))
    return shapes


def add(a, b):
    return (a.astype(F32) + b.astype(F32)).astype(BF16)


class Engine:
    def __init__(self, plan, batch, shares, sums, arrivals, gathered, send_sems, recv_sems, keep_sems):
        self.plan, self.batch, self.shares = plan, batch, shares
        self.sums, self.arrivals, self.gathered = sums, arrivals, gathered
        self.send_sems, self.recv_sems, self.keep_sems = send_sems, recv_sems, keep_sems
        me, group, member = plan.place()
        self.me, self.group, self.member = me, group, member
        self.z = lax.axis_index("batch")
        self.x, self.y = lax.rem(group, 2), lax.div(group, 2)
        self.partner = seq_device(group * plan.members + 1 - member)
        chip = lambda g: seq_device(g * plan.members + member)
        self.across = {"x": chip(self.y * 2 + 1 - self.x), "y": chip((1 - self.y) * 2 + self.x)}
        self.diagonal = chip((1 - self.y) * 2 + 1 - self.x)
        self.layers = [lax.rem(self.z + i, batch) for i in range(1, batch)]

    def peers(self):
        return [self.partner, self.across["x"], self.across["y"], self.diagonal] + [
            (self.me, layer) for layer in self.layers
        ]

    def steps(self, s, fill, axes, order, stop=None):
        total, share = self.sums[s], self.shares[s]
        own = {"x": self.x, "y": self.y, "z": self.z}
        count = 0

        def sems():
            nonlocal count
            count += 1
            return self.send_sems.at[s, count - 1], self.recv_sems.at[s, count - 1]

        fill()
        done = {}
        for number, axis in enumerate(order):
            where = lambda spots: tuple(spots.get(a, slice(None)) for a in axes)
            arrived = self.arrivals[s][number]
            copies = []
            if axis == "z":
                for i, layer in enumerate(self.layers):
                    copies.append(
                        send(total.at[where({**done, "z": layer})], arrived.at[i], *sems(), (self.me, layer))
                    )
            else:
                copies.append(
                    send(total.at[where({**done, axis: 1 - own[axis]})], arrived, *sems(), self.across[axis])
                )
            for copy in copies:
                copy.start()
            yield
            for copy in copies:
                copy.wait()
            done[axis] = own[axis]
            spot = where(done)
            value = total[spot].astype(F32)
            if axis == "z":
                for i in range(self.batch - 1):
                    value = value + arrived[i].astype(F32)
            else:
                value = value + arrived[...].astype(F32)
            if stop is None:
                total[spot] = value.astype(BF16)
            else:
                stop[...] = value.astype(BF16)
        if stop is not None:
            return
        out = self.gathered[s]
        block = total.at[where(done)]
        first, second = share.order.replace("z", "")[::-1]
        home = out.at[self.member, self.y, self.x]
        keep = pltpu.make_async_copy(block, home, self.keep_sems.at[s])
        keep.start()
        copy = send(block, home, *sems(), self.across[first])
        copy.start()
        yield
        copy.wait()
        came = (self.member, 1 - self.y, self.x) if first == "y" else (self.member, self.y, 1 - self.x)
        copies = [send(block, home, *sems(), self.across[second])]
        copies.append(send(out.at[came], out.at[came], *sems(), self.across[second]))
        for copy in copies:
            copy.start()
        keep.wait()
        yield
        for copy in copies:
            copy.wait()
        copy = send(out.at[self.member], out.at[self.member], *sems(), self.partner)
        copy.start()
        yield
        copy.wait()


def spread_to(target, rows, values, at):
    layers, groups = target.shape[0], target.shape[1] * target.shape[2]
    for layer in range(layers):
        for g in range(groups):
            start = (layer * groups + g) * rows
            target[layer, g // 2, g % 2, :, pl.ds(at, values.shape[1])] = values[start : start + rows].astype(BF16)


def tail_kernel(plan, batch, shares, arrival_counts, names, *refs):
    r = SimpleNamespace(**dict(zip(names, refs)))
    refs = refs[len(names) :]
    takes = iter(refs)
    neighbour_grad = next(takes)
    gathered = [next(takes) for _ in shares]
    two_left = [next(takes) for _ in range(4)]
    two_right = [next(takes) for _ in range(3 + plan.slots)]
    give_right = [next(takes) for _ in range(plan.slots)]
    sums = [next(takes) for _ in shares]
    arrivals = [[next(takes) for _ in range(n)] for n in arrival_counts]
    (
        queries, pairs, outs, got_grads, grads, deltas, pair_sum, query_sum,
        give, took, sent_pair, got_pair, sent_query, got_query, vector_rows, other_rows,
        turned_weight, slopes, memory_weight, stage, edge_sent, edge_got,
        load_sems, out_send, out_recv, give_send, give_recv, pair_send, pair_recv, query_send, query_recv,
        own_sems, swap_send, swap_recv, state_sems, near_sems, stage_sems, edge_send, edge_recv, send_sems, recv_sems, keep_sems,
    ) = takes
    me, group, member = plan.place()
    devices, groups, members, slots, rows = plan.devices, plan.groups, plan.members, plan.slots, plan.rows
    half = rows // 2
    half_low = low_lanes((half, 2 * HEAD))
    low = low_lanes((rows, 2 * HEAD))
    engine = Engine(plan, batch, shares, sums, arrivals, gathered, send_sems, recv_sems, keep_sems)
    partner = engine.partner
    before = jnp.maximum(me - 1, 0)
    greet(
        [seq_device(lax.rem(me + i, devices)) for i in range(1, devices)]
        + [(me, layer) for layer in engine.layers]
    )

    def load(slot):
        spot = slot % 2
        return [
            pltpu.make_async_copy(r.queries.at[slot], queries.at[spot], load_sems.at[spot, 0]),
            pltpu.make_async_copy(r.pairs.at[slot], pairs.at[spot], load_sems.at[spot, 1]),
            pltpu.make_async_copy(r.outs.at[slot], outs.at[spot], load_sems.at[spot, 2]),
        ]

    for copy in load(0):
        copy.start()

    def out_copy(slot, away):
        to = lax.rem(group + away, groups)
        return send(
            r.packed_grads.at[to * slots + slot], got_grads.at[slot, group],
            out_send.at[slot, away - 1], out_recv.at[slot, group], seq_device(to * members + member),
        )

    for slot in range(slots):
        for away in range(1, groups):
            out_copy(slot, away).start()
        got_grads[slot, group] = r.packed_grads[group * slots + slot]

    state_loads = [
        pltpu.make_async_copy(getattr(r, "state%d" % s), sums[s], state_sems.at[s]) for s in range(EARLY)
    ]
    stretches = slopes.shape[0] // SPAN - 1
    near_loads = [
        pltpu.make_async_copy(r.memory_grad, slopes, near_sems.at[0]),
        pltpu.make_async_copy(r.memory_weight, memory_weight, near_sems.at[1]),
    ]
    first = sums[EARLY].shape[-1]
    rest = r.memory_part.shape[-1] - first
    memory_loads = [
        pltpu.make_async_copy(r.memory_part.at[:, :, :, :, pl.ds(0, first)], sums[EARLY], near_sems.at[2]),
        pltpu.make_async_copy(
            r.memory_part.at[:, :, :, :, pl.ds(first, rest)],
            sums[EARLY + 1].at[:, :, :, :, pl.ds(0, rest)],
            near_sems.at[3],
        ),
    ]
    packed_load = pltpu.make_async_copy(r.weight, turned_weight, near_sems.at[4])
    for copy in state_loads + memory_loads + near_loads + [packed_load]:
        copy.start()

    lefts = [getattr(r, "left%d" % m) for m in range(4)]
    rights = [getattr(r, "right%d" % m) for m in range(3)]
    here, there = pl.ds(0, rows), pl.ds(rows, rows)

    def left_swaps(m):
        return [
            pltpu.make_async_copy(lefts[m], two_left[m].at[here], own_sems.at[m, 0]),
            send(lefts[m], two_left[m].at[there], swap_send.at[m, 0], swap_recv.at[m, 0], partner),
        ]

    def right_swaps(m):
        width = rights[m].shape[1] // 2
        mine = pl.ds(pl.multiple_of(member * width, 128), width)
        theirs = pl.ds(pl.multiple_of((1 - member) * width, 128), width)
        return [
            pltpu.make_async_copy(rights[m].at[:, mine], two_right[m].at[here], own_sems.at[m, 1]),
            send(rights[m].at[:, theirs], two_right[m].at[there], swap_send.at[m, 1], swap_recv.at[m, 1], partner),
        ]

    swaps = {}
    for m in range(3):
        swaps[m] = left_swaps(m) + right_swaps(m)
        for copy in swaps[m]:
            copy.start()
    last_left = left_swaps(3)
    for copy in last_left:
        copy.start()

    def edge_copy():
        return send(edge_sent, edge_got, edge_send, edge_recv, seq_device(before))

    def stage_copy(s):
        return pltpu.make_async_copy(
            stage.at[s % 2], neighbour_grad.at[pl.ds(s * SPAN, SPAN)], stage_sems.at[s % 2]
        )

    def neighbour_grads(numbers):
        for s in numbers:
            if s >= 2:
                stage_copy(s - 2).wait()
            part = back_product(slopes[(s + 1) * SPAN : (s + 2) * SPAN, :], memory_weight[...])
            stage[s % 2] = part.astype(BF16)
            if s == stretches - 1:

                @pl.when(me < devices - 1)
                def _():
                    edge_copy().wait_recv()
                    stage[s % 2] = (part + edge_got[...].astype(F32)).astype(BF16)

            stage_copy(s).start()

    def slot_swap(slot):
        return send(
            give_right[slot], two_right[3 + slot].at[there], swap_send.at[4 + slot, 1], swap_recv.at[4 + slot, 1], partner
        )

    def arrive(slot):
        for away in range(1, groups):
            origin = lax.rem(group + away, groups)
            head = origin * slots + slot
            send(
                sent_query.at[slot, 0], got_query.at[head],
                query_send.at[slot, 0], query_recv.at[head], partner,
            ).wait_recv()
            send(
                sent_pair.at[0], got_pair.at[head], pair_send.at[slot, 0], pair_recv.at[head], partner,
            ).wait_recv()
        for owner, target in ((1 - member, give_right[slot]), (member, two_right[3 + slot].at[here])):
            heads = [(owner * 2 + i) * slots + slot for i in range(2)]
            for i in range(2):
                target[:, i * 128 : (i + 1) * 128] = got_pair[heads[i]]
            first, second = [got_query[head].astype(F32) for head in heads]
            target[:half, 256:384] = jnp.where(half_low, first, swap_lanes(second)).astype(BF16)
            target[half:, 256:384] = jnp.where(half_low, swap_lanes(first), second).astype(BF16)
            if target is give_right[slot]:
                slot_swap(slot).start()

    waited = set()
    last_left_done = []

    def spread(s, values, at):
        spread_to(sums[s], shares[s].rows, values, at)

    def fill(s):
        if EARLY <= s < EARLY + 2:
            memory_loads[s - EARLY].wait()
        for piece in shares[s].pieces:
            m = piece.matrix
            if m not in waited:
                waited.add(m)
                if m < 3:
                    for copy in swaps[m]:
                        copy.wait()
                else:
                    slot_swap(m - 3).wait()
            if m >= 3 and not last_left_done:
                last_left_done.append(m)
                for copy in last_left:
                    copy.wait()
            tile = piece.count if piece.count <= 512 else 384
            for t in range(piece.count // tile):
                first = piece.first + t * tile
                spread(s, outer_sum(two_left[min(m, 3)][...], two_right[m][:, first : first + tile]), piece.at + t * tile)
        if shares[s].vectors is not None:
            vector_copy.wait()
            mine = vector_rows[member] + other_rows[...]
            wide = jnp.concatenate([mine, jnp.zeros((120, D), F32)], axis=0)
            spread(s, jnp.transpose(wide), shares[s].vectors)

    def ready(s):
        state_loads[s].wait()

    running = []
    for s, share in enumerate(shares):
        if s < EARLY:
            axes = "zyx".replace(share.order[0], "")
            running.append(engine.steps(s, partial(ready, s), axes, share.order[1:]))
        else:
            running.append(engine.steps(s, partial(fill, s), "zyx", share.order))

    def advance(*numbers):
        for n in numbers:
            next(running[n], None)

    advance(0, 1, 2, 3, 4, 5)
    advance(6, 7)

    def give_copy(slot, away):
        to = lax.rem(member + away, members)
        return send(
            give.at[away - 1], took.at[slot, away - 1],
            give_send.at[slot, away - 1], give_recv.at[slot, away - 1], seq_device(group * members + to),
        )

    def pair_copy(slot, to):
        return send(
            sent_pair.at[to], got_pair.at[group * slots + slot],
            pair_send.at[slot, to], pair_recv.at[group * slots + slot], seq_device(to * members + member),
        )

    def query_copy(slot, to):
        return send(
            sent_query.at[slot, to], got_query.at[group * slots + slot],
            query_send.at[slot, to], query_recv.at[group * slots + slot], seq_device(to * members + member),
        )

    def tick():
        for action in next(schedule, ()):
            if action < 0:
                arrive(-1 - action)
            else:
                advance(action)

    schedule = iter(SCHEDULE)
    for slot in range(slots):
        spot = slot % 2
        for copy in load(slot):
            copy.wait()
        if slot + 1 < slots:
            for copy in load(slot + 1):
                copy.start()
        for away in range(1, groups):
            origin = lax.rem(group + away, groups)
            out_copy(slot, away).wait_send()
            send(
                r.packed_grads.at[0], got_grads.at[slot, origin],
                out_send.at[slot, 0], out_recv.at[slot, origin], partner,
            ).wait_recv()
        for g in range(groups):
            part = got_grads[slot, g].astype(F32)
            top = jnp.where(half_low, 0.0, swap_lanes(part))
            bottom = jnp.where(half_low, 0.0, part)
            grads[g, :half] = top.astype(BF16)
            grads[g, half:] = bottom.astype(BF16)
            product = jnp.concatenate([top, bottom], axis=0) * outs[spot, g]
            deltas[g] = jnp.broadcast_to(jnp.sum(jnp.transpose(product), axis=0, keepdims=True), (8, rows))
        for k in range(groups):
            total = 0.0
            tile = pairs[spot, k * members : (k + 1) * members].reshape(members * rows, 128)
            for g in range(k, groups):
                query, grad = queries[spot, g], grads[g]
                scores = hide(plan, back_product(tile, query), k, g, member, r.starts[g][:1])
                chance = jnp.exp(scores - r.logs[slot, g][:1])
                chance_grad = back_product(tile, grad)
                score_grad = (chance * (chance_grad - deltas[g][:1])).astype(BF16)
                total = total + matmul(score_grad, query) + matmul(chance.astype(BF16), grad)
                part = outer_sum(tile, score_grad)
                query_sum[g] = part if k == 0 else query_sum[g] + part
            pair_sum[k * members : (k + 1) * members] = total.reshape(members, rows, 128)
            if k < groups - 1:
                tick()
        for away in range(1, members):
            to = lax.rem(member + away, members)
            if slot > 0:
                give_copy(slot - 1, away).wait_send()
            for g in range(groups):
                give[away - 1, g] = pair_sum[g * members + to].astype(BF16)
            give_copy(slot, away).start()
        for g in range(groups):
            total = jnp.transpose(query_sum[g]) * (HEAD ** -0.5)
            packed = jnp.where(half_low, total[:half], swap_lanes(total[half:])).astype(BF16)

            @pl.when(group != g)
            def _():
                sent_query[slot, g] = packed
                query_copy(slot, g).start()

            @pl.when(group == g)
            def _():
                got_query[group * slots + slot] = packed

        for away in range(1, members):
            give_copy(slot, away).wait_recv()
        for g in range(groups):
            total = pair_sum[g * members + member]
            for away in range(1, members):
                total = total + took[slot, away - 1, g].astype(F32)
            total = total.astype(BF16)

            @pl.when(group != g)
            def _():
                if slot > 0:
                    pair_copy(slot - 1, g).wait_send()
                sent_pair[g] = total
                pair_copy(slot, g).start()

            @pl.when(group == g)
            def _():
                got_pair[group * slots + slot] = total

        if slot == 0:
            for copy in near_loads:
                copy.wait()
            edge_sent[...] = back_product(slopes[0:SPAN, :], memory_weight[...]).astype(BF16)

            @pl.when(me > 0)
            def _():
                edge_copy().start()

        tick()

    tick()
    arrive(slots - 1)
    tick()
    packed_load.wait()
    normed_grad = 0.0
    for slot in range(slots):
        for owner, part in ((member, two_right[3 + slot][here]), (1 - member, give_right[slot][...])):
            columns = pl.ds(pl.multiple_of(slot * D + owner * (D // 2), 128), D // 2)
            normed_grad = normed_grad + back_product(part, turned_weight[:, columns])
    values = r.tokens[...].astype(F32)
    centred = values - jnp.mean(values, axis=1, keepdims=True)
    inverse = lax.rsqrt(jnp.mean(centred * centred, axis=1, keepdims=True) + EPSILON)
    unit = centred * inverse
    vector_rows[0] = jnp.concatenate(
        [jnp.sum(normed_grad * unit, axis=0, keepdims=True), r.vectors[0:2], jnp.zeros((5, D), F32)], axis=0
    )
    vector_rows[1] = jnp.concatenate(
        [jnp.sum(normed_grad, axis=0, keepdims=True), r.vectors[2:4], jnp.zeros((5, D), F32)], axis=0
    )
    vector_copy = send(
        vector_rows.at[1 - member], other_rows, swap_send.at[3, 1], swap_recv.at[3, 1], partner
    )
    vector_copy.start()
    tick()
    scaled = normed_grad * as_row(r.gain)
    input_grad = r.stream_grad[...] + inverse * (
        scaled
        - jnp.mean(scaled, axis=1, keepdims=True)
        - unit * jnp.mean(scaled * unit, axis=1, keepdims=True)
    )
    r.input_grad[...] = input_grad.astype(BF16)
    tick()
    for s in range(stretches):
        neighbour_grads([s])
        tick()
    for _ in range(40):
        tick()
    for _ in range(8):
        advance(*range(len(shares)))

    for s in range(max(stretches - 2, 0), stretches):
        stage_copy(s).wait()

    @pl.when(me > 0)
    def _():
        edge_copy().wait_send()

    for slot in range(slots):
        for away in range(1, members):
            if slot == slots - 1:
                give_copy(slot, away).wait_send()
        for away in range(1, groups):
            origin = lax.rem(group + away, groups)
            if slot == slots - 1:
                pair_copy(slot, origin).wait_send()
            query_copy(slot, origin).wait_send()


def tail(plan, batch, packed_grads, queries, pairs, outs, logs, starts, lefts, rights, states,
    memory_part, memory_grad, memory_weight, weight, tokens, gain, stream_grad, vectors, ff,
):
    devices, groups, members, slots, rows = plan.devices, plan.groups, plan.members, plan.slots, plan.rows
    half = rows // 2
    shares = shares_of(batch, groups, ff)
    dma = pltpu.SemaphoreType.DMA
    inputs = dict(packed_grads=packed_grads, logs=logs, starts=starts, tokens=tokens, gain=gain)
    inputs.update(stream_grad=stream_grad, vectors=vectors)
    small = len(inputs)
    inputs.update(queries=queries, pairs=pairs, outs=outs, weight=weight)
    inputs.update({"left%d" % m: left for m, left in enumerate(lefts)})
    inputs.update({"right%d" % m: right for m, right in enumerate(rights)})
    inputs.update({"state%d" % m: state for m, state in enumerate(states)})
    inputs.update(memory_part=memory_part, memory_grad=memory_grad, memory_weight=memory_weight)
    widths = [right.shape[1] // 2 for right in rights] + [D // 2] * slots
    axes = ["zyx".replace(s.order[0], "") if n < EARLY else "zyx" for n, s in enumerate(shares)]
    orders = [s.order[1:] if n < EARLY else s.order for n, s in enumerate(shares)]
    steps = [step_shapes(share, batch, axes[n], orders[n]) for n, share in enumerate(shares)]
    scratch = [VM((2 * rows, left.shape[1]), BF16) for left in lefts]
    scratch += [VM((2 * rows, width), BF16) for width in widths]
    scratch += [VM((rows, D // 2), BF16)] * slots
    scratch += [VM(part_shape(share, batch, axes[n]), BF16) for n, share in enumerate(shares)]
    scratch += [VM(shape, BF16) for shapes in steps for shape in shapes]
    span_rows = memory_grad.shape[0]
    scratch += [
        VM((2, groups, rows, 128), BF16),
        VM((2, devices, rows, 128), BF16),
        VM((2, groups, rows, 128), F32),
        VM((slots, groups, half, 128), BF16),
        VM((groups, rows, 128), BF16),
        VM((groups, 8, rows), F32),
        VM((devices, rows, 128), F32),
        VM((groups, 128, rows), F32),
        VM((members - 1, groups, rows, 128), BF16),
        VM((slots, members - 1, groups, rows, 128), BF16),
        VM((groups, rows, 128), BF16),
        VM((HEADS, rows, 128), BF16),
        VM((slots, groups, half, 128), BF16),
        VM((HEADS, half, 128), BF16),
        VM((2, 8, D), F32),
        VM((8, D), F32),
        VM((D, 3 * D), BF16),
        VM((span_rows, 2 * D), BF16),
        VM((D, 2 * D), BF16),
        VM((2, SPAN, D), BF16),
        VM((SPAN, D), BF16),
        VM((SPAN, D), BF16),
        dma((2, 3)),
        dma((slots, groups)),
        dma((slots, groups)),
        dma((slots, members - 1)),
        dma((slots, members - 1)),
        dma((slots, groups)),
        dma((HEADS,)),
        dma((slots, groups)),
        dma((HEADS,)),
        dma((4, 2)),
        dma((4 + slots, 2)),
        dma((4 + slots, 2)),
        dma((EARLY,)),
        dma((5,)),
        dma((2,)),
        dma,
        dma,
        dma((len(shares), 6 + batch)),
        dma((len(shares), 6 + batch)),
        dma((len(shares),)),
    ]
    names = list(inputs) + ["input_grad"]
    out = pl.pallas_call(
        partial(tail_kernel, plan, batch, shares, [len(s) for s in steps], names),
        out_shape=[jax.ShapeDtypeStruct((rows, D), BF16), jax.ShapeDtypeStruct((span_rows - SPAN, D), BF16)]
        + [jax.ShapeDtypeStruct((2, 2, 2, s.rows, s.columns), BF16) for s in shares],
        in_specs=[pl.BlockSpec(memory_space=VM)] * small + [pl.BlockSpec(memory_space=pl.ANY)] * (len(inputs) - small),
        out_specs=[pl.BlockSpec(memory_space=VM)] + [pl.BlockSpec(memory_space=pl.ANY)] * (1 + len(shares)),
        scratch_shapes=scratch,
        compiler_params=pltpu.CompilerParams(
            collective_id=1, has_side_effects=True, vmem_limit_bytes=62 << 20
        ),
        name="tail",
    )(*inputs.values())
    return out[0], out[1], out[2:]


def widen_kernel(plan, *refs):
    shares, (low_result, low_input, low_neighbour) = refs[:12], refs[12:15]
    down, up, cross_out, memory, query, self_out, self_weight, result, input_grad, neighbour_grad = refs[15:25]
    vectors, kept = refs[25:31], refs[31]
    step = pl.program_id(0)

    def put(out, s, at, first, count):
        for core in range(2):
            width = out.shape[1] // 2
            block = shares[s][core, 0, 0, :, first : first + count]
            out[:, core * width + at : core * width + at + count] = block.astype(F32)

    for part in range(2):
        for core in range(2):
            tall = shares[part].shape[3]
            out_rows = slice(part * tall, part * tall + tall)
            down[out_rows, core * (D // 2) : (core + 1) * (D // 2)] = shares[part][core, 0, 0].astype(F32)
    quarter = up.shape[1] // 4
    put(up, 2, 0, 0, quarter)
    put(up, 3, quarter, 0, quarter)
    put(memory, 4, 0, 0, 512)
    put(memory, 5, 512, 0, 256)
    put(cross_out, 5, 0, 256, D // 2)
    put(query, 6, 0, 0, D // 2)
    put(self_out, 7, 0, 0, D // 2)
    rows = shares[8].shape[3]
    low = low_lanes((rows, 2 * HEAD))

    def block(head, spot):
        g, slot = head // plan.slots, head % plan.slots
        core, i = g // 2, g % 2
        spot = i if spot is None else spot
        s, first = (8 + slot, spot * 128) if slot < 2 else (10, spot * 128) if spot < 2 else (11, 0)
        return shares[s][core, 0, 0, :, first : first + 128].astype(F32), i

    for two in range(HEADS // 2):
        heads = (2 * two, 2 * two + 1)
        columns = slice(two * 128, two * 128 + 128)
        (one, i), (other, j) = [block(head, 2) for head in heads]
        self_weight[:, columns] = jnp.where(low, swap_lanes(one) if i else one, other if j else swap_lanes(other))
        one, other = [block(head, None)[0] for head in heads]
        self_weight[:, slice(D + two * 128, D + two * 128 + 128)] = jnp.where(low, one, swap_lanes(other))
        self_weight[:, slice(2 * D + two * 128, 2 * D + two * 128 + 128)] = jnp.where(low, swap_lanes(one), other)
    result[...] = low_result[...]
    input_grad[...] = low_input[...].astype(F32)
    neighbour_grad[...] = low_neighbour[...].astype(F32)
    for core in range(2):
        kept[core, pl.ds(pl.multiple_of(step * rows, 16), rows)] = shares[11][core, 0, 0, :, 128:].astype(F32)

    @pl.when(step == 3)
    def _():
        for core in range(2):
            turned = jnp.transpose(kept[core])
            for n in range(3):
                vectors[core * 3 + n][...] = turned[n]


def widen(plan, batch, ff, shares, result, input_grad, neighbour_grad):
    rows = plan.rows
    ins = [pl.BlockSpec((2, 1, 1) + s.shape[3:], lambda i: (0, i // 2, i % 2, 0, 0)) for s in shares]
    passed = [result, input_grad, neighbour_grad]
    ins += [pl.BlockSpec((a.shape[0] // 4, D), lambda i: (i, 0)) for a in passed]
    layout = [(ff, D), (D, ff), (D, D), (D, 2 * D), (D, D), (D, D), (D, 3 * D)]
    layout = [(r // batch, c) for r, c in layout] + [a.shape for a in passed]
    kinds = [F32] * 7 + [BF16, F32, F32]
    outs = [pl.BlockSpec((r // 4, c), lambda i: (i, 0)) for r, c in layout]
    outs += [pl.BlockSpec((D // batch,), lambda i: (0,))] * 6
    return pl.pallas_call(
        partial(widen_kernel, plan),
        grid=(4,),
        in_specs=ins,
        out_specs=outs,
        out_shape=[jax.ShapeDtypeStruct(shape, kind) for shape, kind in zip(layout, kinds)]
        + [jax.ShapeDtypeStruct((D // batch,), F32)] * 6,
        scratch_shapes=[VM((2, D // batch, 128), F32)],
        compiler_params=pltpu.CompilerParams(vmem_limit_bytes=60 << 20),
        name="widen",
    )(*shares, *passed)


FOLD = 256 // HEAD


def stack_heads(values):
    lane = lax.broadcasted_iota(jnp.int32, values.shape, 1) // HEAD
    return jnp.concatenate([jnp.where(lane == h, values, jnp.zeros_like(values)) for h in range(FOLD)], axis=0)


def unstack_heads(stacked):
    count = stacked.shape[0] // FOLD
    lane = lax.broadcasted_iota(jnp.int32, (count, stacked.shape[1]), 1) // HEAD
    total = jnp.where(lane == 0, stacked[:count], 0.0)
    for h in range(1, FOLD):
        total = total + jnp.where(lane == h, stacked[h * count : (h + 1) * count], 0.0)
    return total


def cross_chances(queries, keys):
    scores = back_product(queries, keys)
    chance = jnp.exp(scores - jnp.max(scores, axis=1, keepdims=True))
    return chance / jnp.sum(chance, axis=1, keepdims=True)


def norm_parts(values):
    centred = values - jnp.mean(values, axis=1, keepdims=True)
    inverse = lax.rsqrt(jnp.mean(centred * centred, axis=1, keepdims=True) + EPSILON)
    return centred * inverse, inverse


def norm_back(values, gain, grad):
    unit, inverse = norm_parts(values)
    scaled = grad * gain
    inner = inverse * (
        scaled - jnp.mean(scaled, axis=1, keepdims=True) - unit * jnp.mean(scaled * unit, axis=1, keepdims=True)
    )
    return jnp.sum(grad * unit, axis=0, keepdims=True), jnp.sum(grad, axis=0, keepdims=True), inner


def middle_kernel(plan, batch, shares, arrival_counts, names, *refs):
    r = SimpleNamespace(**dict(zip(names, refs)))
    takes = iter(refs[len(names) :])
    sums = [next(takes) for _ in range(EARLY)]
    arrivals = [[next(takes) for _ in range(n)] for n in arrival_counts]
    (
        up, down, active, two_normed, give_upper, two_upper, two_grad, slopes,
        stream_one, stream_two, normed_grad, summed, moved_queries, moved_grads, moved,
        load_sems, own_sems, tile_send, tile_recv, swap_send, swap_recv, group_sems, near_sems, send_sems, recv_sems,
    ) = takes
    me, group, member = plan.place()
    rows, groups = plan.rows, plan.groups
    states = [getattr(r, "state%d" % s) for s in range(EARLY)]
    engine = Engine(plan, batch, shares, sums, arrivals, None, send_sems, recv_sems, None)
    partner = engine.partner
    greet(engine.peers())
    here, there = pl.ds(0, rows), pl.ds(rows, rows)
    ff = up.shape[1]
    loads = [
        pltpu.make_async_copy(r.memory, slopes, load_sems.at[2]),
        pltpu.make_async_copy(r.up_weight, up, load_sems.at[0]),
        pltpu.make_async_copy(r.down_weight, down, load_sems.at[1]),
    ]
    for copy in loads:
        copy.start()
    half = D // 2
    mine = pl.ds(pl.multiple_of(member * half, 128), half)
    theirs = pl.ds(pl.multiple_of((1 - member) * half, 128), half)
    grad_swap = [
        pltpu.make_async_copy(r.cotangent.at[:, mine], two_grad.at[here], own_sems.at[0]),
        send(r.cotangent.at[:, theirs], two_grad.at[there], swap_send.at[0], swap_recv.at[0], partner),
    ]
    for copy in grad_swap:
        copy.start()
    at = lax.broadcasted_iota(jnp.int32, (rows, 1), 0)
    keep = ((me > 0) | (at >= STRETCH - 1)).astype(F32)
    stretches = slopes.shape[0]

    def move(values):
        wide = jnp.concatenate([values, jnp.zeros((STRETCH, D), F32)], axis=0)
        return pltpu.roll(wide, 1, 0).astype(BF16).reshape(stretches, STRETCH, D)

    def move_back():
        whole = moved[...].reshape(stretches * STRETCH, D)
        return pltpu.roll(whole, stretches * STRETCH - 1, 0)[:rows]

    stream_one[...] = r.tokens[...].astype(F32) + matmul(r.context[...], r.self_output[...])
    normed_two = (norm_parts(stream_one[...])[0] * as_row(r.second_gain) + as_row(r.second_shift)).astype(BF16)
    r.normed_two[...] = normed_two
    cross_queries = matmul(normed_two, r.query_weight[...]).astype(BF16).astype(F32) * (HEAD ** -0.5)
    moved_queries[...] = move(cross_queries)
    loads[0].wait()

    @pl.loop(0, stretches)
    def _(i):
        for c in range(D // 256):
            columns = slice(c * 256, c * 256 + 256)
            values = slice(D + c * 256, D + c * 256 + 256)
            chances = cross_chances(stack_heads(moved_queries[i, :, columns]), slopes[i, :, columns])
            moved[i, :, columns] = unstack_heads(matmul(chances.astype(BF16), slopes[i, :, values]))

    cross_low = (move_back() * keep).astype(BF16)
    r.cross_low[...] = cross_low
    stream_two[...] = stream_one[...] + matmul(cross_low, r.cross_output[...])
    two_normed[here] = (norm_parts(stream_two[...])[0] * as_row(r.third_gain) + as_row(r.third_shift)).astype(BF16)
    normed_swap = send(two_normed.at[here], two_normed.at[there], swap_send.at[1], swap_recv.at[1], partner)
    normed_swap.start()
    normed_grad[...] = jnp.zeros_like(normed_grad)
    summed[...] = jnp.zeros_like(summed)
    for copy in loads[1:]:
        copy.wait()
    tile = 512
    tiles = ff // tile

    def tile_copy(t):
        columns = pl.ds(pl.multiple_of(t * tile, tile), tile)
        return send(
            active.at[here, columns], active.at[there, columns], tile_send.at[t], tile_recv.at[t], partner
        )

    @pl.loop(0, tiles)
    def _(t):
        columns = pl.ds(pl.multiple_of(t * tile, tile), tile)
        upper = matmul(two_normed[here], up[:, columns])
        density = jnp.exp(upper * upper * -0.5) * (2.0 * math.pi) ** -0.5
        below = 0.5 + 0.5 * lax.erf(upper * 0.5 ** 0.5)
        active_low = (upper * below).astype(BF16)
        active[here, columns] = active_low
        tile_copy(t).start()
        grad = back_product(r.cotangent[...], down[columns])
        upper_low = (grad * (below + upper * density)).astype(BF16)
        spot = pl.ds(pl.multiple_of(lax.rem(t, tiles // 2) * tile, tile), tile)

        @pl.when(lax.div(t, tiles // 2) == member)
        def _():
            two_upper[here, spot] = upper_low

        @pl.when(lax.div(t, tiles // 2) != member)
        def _():
            give_upper[:, spot] = upper_low

        summed[...] += matmul(active_low, down[columns])
        normed_grad[...] += back_product(upper_low, up[:, columns])

    near = down.at[pl.ds(0, stretches * SPAN)]
    near_loads = [
        pltpu.make_async_copy(r.edge, down.at[pl.ds(0, SPAN)], near_sems.at[0]),
        pltpu.make_async_copy(r.neighbours, down.at[pl.ds(SPAN, (stretches - 1) * SPAN)], near_sems.at[1]),
    ]
    for copy in near_loads:
        copy.start()
    upper_swap = send(give_upper, two_upper.at[there], swap_send.at[2], swap_recv.at[2], partner)
    upper_swap.start()
    r.result[...] = (stream_two[...] + summed[...]).astype(BF16)

    def fill_down(s):
        if s > 0:
            return
        for copy in grad_swap:
            copy.wait()

        @pl.loop(0, tiles)
        def _(t):
            tile_copy(t).wait()

        deep = ff // batch
        tall = shares[0].rows
        for layer in range(batch):
            values = outer_sum(active[:, layer * deep : (layer + 1) * deep], two_grad[...]).astype(BF16)
            for g in range(groups):
                for part in range(2):
                    start = (g * 2 + part) * tall
                    sums[part][layer, g // 2, g % 2] = values[start : start + tall]

    def fill_up(s):
        if s == 2:
            normed_swap.wait()
            upper_swap.wait()
        piece = shares[s].pieces[0]
        for first in range(0, piece.count, 384):
            tile_values = outer_sum(two_normed[...], two_upper[:, piece.first + first : piece.first + first + 384])
            spread_to(sums[s], shares[s].rows, tile_values, first)

    fills = [fill_down, fill_down, fill_up, fill_up]
    running = [
        engine.steps(s, partial(fills[s], s), "zyx", shares[s].order[:1], states[s]) for s in range(EARLY)
    ]
    for run in running:
        next(run, None)

    gain_grad, shift_grad, inner = norm_back(stream_two[...], as_row(r.third_gain), normed_grad[...])
    r.vectors[1:2] = gain_grad
    r.vectors[3:4] = shift_grad
    stream_two_grad = r.cotangent[...].astype(F32) + inner
    normed_grad[...] = stream_two_grad
    branch_low = stream_two_grad.astype(BF16)
    r.branch[...] = branch_low
    moved_grads[...] = move(back_product(branch_low, r.cross_output[...]) * keep)

    def group_copy(i):
        return pltpu.make_async_copy(slopes.at[i], r.memory_grad.at[i], group_sems.at[i])

    @pl.loop(0, stretches)
    def _(i):
        for c in range(D // 256):
            columns = slice(c * 256, c * 256 + 256)
            values = slice(D + c * 256, D + c * 256 + 256)
            stacked = stack_heads(moved_queries[i, :, columns])
            stacked_grad = stack_heads(moved_grads[i, :, columns])
            keys = slopes[i, :, columns]
            chances = cross_chances(stacked, keys)
            chance_grad = back_product(stacked_grad, slopes[i, :, values])
            total = jnp.sum(chances * chance_grad, axis=1, keepdims=True)
            score_grad = (chances * (chance_grad - total)).astype(BF16)
            moved[i, :, columns] = unstack_heads(matmul(score_grad, keys)) * (HEAD ** -0.5)
            slopes[i, :, columns] = outer_sum(score_grad, stacked).astype(BF16)
            slopes[i, :, values] = outer_sum(chances.astype(BF16), stacked_grad).astype(BF16)
        group_copy(i).start()

    query_grad = move_back().astype(BF16)
    r.query_grad[...] = query_grad
    gain_grad, shift_grad, inner = norm_back(
        stream_one[...], as_row(r.second_gain), back_product(query_grad, r.query_weight[...])
    )
    r.vectors[0:1] = gain_grad
    r.vectors[2:3] = shift_grad
    r.vectors[4:8] = jnp.zeros((4, D), F32)
    stream_one_grad = normed_grad[...] + inner
    r.stream_grad[...] = stream_one_grad
    self_low = stream_one_grad.astype(BF16)
    r.self_low[...] = self_low
    grad_out = back_product(self_low, r.self_output[...]).astype(BF16).astype(F32)

    for head in range(HEADS):
        block = (head // 2) * 128
        r.packed_grads[head] = pack_rows(grad_out[:, block : block + 128], head).astype(BF16)

    for copy in near_loads:
        copy.wait()
    span_rows = stretches * SPAN

    def memory_tile(owner, t):
        columns = pl.ds(pl.multiple_of(owner * D + t * 256, 256), 256)
        return outer_sum(near[...], slopes[:, :, columns].reshape(span_rows, 256)).astype(BF16)

    for t in range(D // 256):
        up[:, t * 256 : t * 256 + 256] = memory_tile(1 - member, t)
    memory_swap = send(
        up.at[:, pl.ds(0, D)], up.at[:, pl.ds(D, D)], swap_send.at[3], swap_recv.at[3], partner
    )
    memory_swap.start()
    for t in range(D // 256):
        up[:, 2 * D + t * 256 : 2 * D + t * 256 + 256] = memory_tile(member, t)
    for run in running:
        next(run, None)
    memory_swap.wait()
    r.memory_part[...] = add(up[:, 2 * D : 3 * D], up[:, D : 2 * D])

    @pl.loop(0, stretches)
    def _(i):
        group_copy(i).wait()


def middle(plan, batch, tokens, context, self_output, second_gain, second_shift, third_gain, third_shift, query_weight, memory, neighbours, edge, cross_output, up_weight, down_weight, cotangent):
    rows = plan.rows
    ff = up_weight.shape[1]
    stretches = memory.shape[0]
    shares = shares_of(batch, plan.groups, ff)
    dma = pltpu.SemaphoreType.DMA
    inputs = dict(
        tokens=tokens, context=context, self_output=self_output, second_gain=second_gain, second_shift=second_shift,
        third_gain=third_gain, third_shift=third_shift, query_weight=query_weight,
        cross_output=cross_output, cotangent=cotangent,
    )
    near = len(inputs)
    inputs.update(memory=memory, up_weight=up_weight, down_weight=down_weight, neighbours=neighbours, edge=edge)
    low = ((rows, D), BF16)
    outputs = dict(
        result=low, normed_two=low, cross_low=low, branch=low, query_grad=low, self_low=low,
        packed_grads=((HEADS, rows // 2, 128), BF16), memory_part=((D, D), BF16),
        stream_grad=((rows, D), F32), vectors=((8, D), F32),
    )
    steps = [step_shapes(shares[s], batch, "zyx", shares[s].order[:1]) for s in range(EARLY)]
    for s in range(EARLY):
        outputs["state%d" % s] = (part_shape(shares[s], batch, "zyx".replace(shares[s].order[0], "")), BF16)
    far = len(outputs)
    outputs.update(memory_grad=(memory.shape, BF16))
    scratch = [VM(part_shape(shares[s], batch, "zyx"), BF16) for s in range(EARLY)]
    scratch += [VM(shape, BF16) for shapes in steps for shape in shapes]
    scratch += [
        VM((D, ff), BF16),
        VM((ff, D), BF16),
        VM((2 * rows, ff), BF16),
        VM((2 * rows, D), BF16),
        VM((rows, ff // 2), BF16),
        VM((2 * rows, ff // 2), BF16),
        VM((2 * rows, D // 2), BF16),
        VM(memory.shape, BF16),
        VM((rows, D), F32),
        VM((rows, D), F32),
        VM((rows, D), F32),
        VM((rows, D), F32),
        VM((stretches, STRETCH, D), BF16),
        VM((stretches, STRETCH, D), BF16),
        VM((stretches, STRETCH, D), F32),
        dma((3,)),
        dma((1,)),
        dma((ff // 512,)),
        dma((ff // 512,)),
        dma((4,)),
        dma((4,)),
        dma((stretches,)),
        dma((2,)),
        dma((EARLY, batch - 1)),
        dma((EARLY, batch - 1)),
    ]
    names = list(inputs) + list(outputs)
    out = pl.pallas_call(
        partial(middle_kernel, plan, batch, shares, [len(s) for s in steps], names),
        out_shape=[jax.ShapeDtypeStruct(*shape) for shape in outputs.values()],
        in_specs=[pl.BlockSpec(memory_space=VM)] * near + [pl.BlockSpec(memory_space=pl.ANY)] * (len(inputs) - near),
        out_specs=[pl.BlockSpec(memory_space=VM)] * far + [pl.BlockSpec(memory_space=pl.ANY)],
        scratch_shapes=scratch,
        compiler_params=pltpu.CompilerParams(
            collective_id=2, has_side_effects=True, vmem_limit_bytes=62 << 20
        ),
        name="middle",
    )(*inputs.values())
    return SimpleNamespace(**dict(zip(outputs, out)))


def on_device(devices, batch, tokens, segment_ids, neighbours, first_gain, first_shift, self_weight, self_output, second_gain,
    second_shift, query_weight, memory_weight, cross_output, third_gain, third_shift, up_weight, down_weight, cotangent,
):
    rows = tokens.shape[1]
    plan = Plan(devices, rows)
    stretch_count = neighbours.shape[1]
    ff = up_weight.shape[1]
    neighbour_rows = neighbours[0].reshape(stretch_count * SPAN, D)
    normed_one, logs, starts, context, edge, queries, pairs, outs, memory, packed = attend(
        plan, tokens[0], first_gain, first_shift, segment_ids, self_weight, neighbour_rows, memory_weight
    )
    mid = middle(
        plan, batch, tokens[0], context, self_output, second_gain, second_shift, third_gain, third_shift, query_weight,
        memory, neighbour_rows, edge, cross_output, up_weight, down_weight, cotangent[0],
    )
    input_grad, neighbour_grad, shares = tail(
        plan,
        batch,
        mid.packed_grads,
        queries,
        pairs,
        outs,
        logs,
        starts,
        [mid.cross_low, mid.normed_two, context, normed_one],
        [mid.branch, mid.query_grad, mid.self_low],
        [getattr(mid, "state%d" % s) for s in range(EARLY)],
        mid.memory_part.reshape(batch, 2, 2, D // (batch * 4), D),
        mid.memory_grad.reshape((stretch_count + 1) * SPAN, 2 * D),
        memory_weight,
        packed,
        tokens[0],
        first_gain,
        mid.stream_grad,
        mid.vectors,
        ff,
    )
    wide = widen(plan, batch, ff, shares, mid.result, input_grad, neighbour_grad)
    down, up, cross_out, memory_w, query, self_out, self_w, result, input_grad, neighbour_grad = wide[:10]
    vector = wide[10:]
    return (
        result[None],
        input_grad[None],
        neighbour_grad.reshape(neighbours.shape),
        vector[0],
        vector[3],
        self_w,
        self_out,
        vector[1],
        vector[4],
        query,
        memory_w,
        cross_out,
        vector[2],
        vector[5],
        up,
        down,
    )


def from_behind(array, axis, by):
    devices = lax.axis_size(axis)
    pairs = [(i, i + by) for i in range(devices) if 0 <= i + by < devices]
    return lax.ppermute(array, axis, pairs)


def layer_norm(values, gain, shift):
    mean = jnp.mean(values, axis=-1, keepdims=True)
    centred = values - mean
    spread = jnp.mean(centred * centred, axis=-1, keepdims=True)
    return centred * lax.rsqrt(spread + EPSILON) * gain + shift


def block_rows():
    return 512


def causal_allowed(query_pos, query_seg, key_pos, key_seg):
    return (query_pos[:, None] >= key_pos[None, :]) & (query_seg[:, None] == key_seg[None, :])


def key_block_grads(
    queries, grad_out, log_total, delta, query_pos, query_seg, keys, values, key_pos, key_seg, scale
):
    allowed = causal_allowed(query_pos, query_seg, key_pos, key_seg)[None]
    scores = jnp.einsum("qhd,khd->hqk", queries, keys, preferred_element_type=jnp.float32) * scale
    chances = jnp.where(
        allowed, jnp.exp(jnp.where(allowed, scores, NEGATIVE) - log_total[..., None]), 0.0
    )
    prob_grad = jnp.einsum("qhd,khd->hqk", grad_out, values, preferred_element_type=jnp.float32)
    score_low = (chances * (prob_grad - delta[..., None])).astype(jnp.bfloat16)
    query_part = (
        jnp.einsum("hqk,khd->qhd", score_low, keys, preferred_element_type=jnp.float32) * scale
    )
    key_part = (
        jnp.einsum("hqk,qhd->khd", score_low, queries, preferred_element_type=jnp.float32) * scale
    )
    value_part = jnp.einsum(
        "hqk,qhd->khd", chances.astype(jnp.bfloat16), grad_out, preferred_element_type=jnp.float32
    )
    return (query_part, key_part, value_part)


def plain_on_device(
    tokens,
    segment_ids,
    neighbours,
    first_gain,
    first_shift,
    self_weight,
    self_output,
    second_gain,
    second_shift,
    query_weight,
    memory_weight,
    cross_output,
    third_gain,
    third_shift,
    up_weight,
    down_weight,
    cotangent,
):
    rows = tokens.shape[1]
    seq_index = lax.axis_index("seq")
    scale = HEAD ** (-0.5)
    stream = tokens[0].astype(jnp.float32)
    seg_local = segment_ids[0]
    positions = seq_index * rows + jnp.arange(rows, dtype=jnp.int32)
    normed_one, first_back = jax.vjp(layer_norm, stream, first_gain, first_shift)
    normed_one_low = normed_one.astype(jnp.bfloat16)
    projected = matmul(normed_one_low, self_weight).astype(jnp.bfloat16)
    queries = projected[:, :D].reshape(rows, HEADS, HEAD)
    keys_low = projected[:, D : 2 * D]
    values_low = projected[:, 2 * D :]
    start_state = (
        jnp.full((HEADS, rows), NEGATIVE, jnp.float32),
        jnp.zeros((HEADS, rows), jnp.float32),
        jnp.zeros((HEADS, rows, HEAD), jnp.float32),
    )
    carry = start_state
    piece_keys = lax.all_gather(keys_low, "seq", axis=0, tiled=True)
    piece_values = lax.all_gather(values_low, "seq", axis=0, tiled=True)
    piece_seg = lax.all_gather(seg_local, "seq", axis=0, tiled=True)
    count = piece_keys.shape[0]
    fold_size = block_rows()

    def step(state, index):
        maxes, totals, running = state
        first = index * fold_size
        keys = lax.dynamic_slice_in_dim(piece_keys, first, fold_size, 0).reshape(
            fold_size, HEADS, HEAD
        )
        values = lax.dynamic_slice_in_dim(piece_values, first, fold_size, 0).reshape(
            fold_size, HEADS, HEAD
        )
        key_seg = lax.dynamic_slice_in_dim(piece_seg, first, fold_size, 0)
        key_pos = first + jnp.arange(fold_size, dtype=jnp.int32)
        allowed = causal_allowed(positions, seg_local, key_pos, key_seg)[None]
        scores = (
            jnp.einsum("qhd,khd->hqk", queries, keys, preferred_element_type=jnp.float32) * scale
        )
        scores = jnp.where(allowed, scores, NEGATIVE)
        new_max = jnp.maximum(maxes, jnp.max(scores, axis=-1))
        factor = jnp.exp(maxes - new_max)
        weights = jnp.where(allowed, jnp.exp(scores - new_max[..., None]), 0.0)
        totals = totals * factor + jnp.sum(weights, axis=-1)
        running = running * factor[..., None] + jnp.einsum(
            "hqk,khd->hqd", weights.astype(jnp.bfloat16), values, preferred_element_type=jnp.float32
        )
        return ((new_max, totals, running), None)

    carry, unused = lax.scan(step, carry, jnp.arange(count // fold_size, dtype=jnp.int32))
    maxes, totals, running = carry
    log_total = maxes + jnp.log(totals)
    context = running / totals[..., None]
    context_low = jnp.transpose(context, (1, 0, 2)).reshape(rows, D).astype(jnp.bfloat16)
    stream_one = stream + matmul(context_low, self_output)
    normed_two, second_back = jax.vjp(layer_norm, stream_one, second_gain, second_shift)
    normed_two_low = normed_two.astype(jnp.bfloat16)
    cross_queries = matmul(normed_two_low, query_weight).astype(jnp.bfloat16)
    stretch_count = neighbours.shape[1]
    span = NEIGHBOURS * NEIGHBOUR_LEN
    groups = stretch_count + 1
    neighbour_rows = neighbours[0].reshape(stretch_count * span, D)
    memory = (
        matmul(neighbour_rows, memory_weight)
        .astype(jnp.bfloat16)
        .reshape(stretch_count, span, 2 * D)
    )
    previous = from_behind(memory[stretch_count - 1], "seq", 1)
    extended = jnp.concatenate([previous[None], memory], axis=0)
    memory_keys = extended[:, :, :D].reshape(groups, span, HEADS, HEAD)
    memory_values = extended[:, :, D:].reshape(groups, span, HEADS, HEAD)
    pad_top = jnp.zeros((1, D), jnp.bfloat16)
    pad_end = jnp.zeros((STRETCH - 1, D), jnp.bfloat16)
    padded_queries = jnp.concatenate([pad_top, cross_queries, pad_end], axis=0).reshape(
        groups, STRETCH, HEADS, HEAD
    )
    cross_probs = jax.nn.softmax(
        jnp.einsum(
            "gqhd,gkhd->ghqk", padded_queries, memory_keys, preferred_element_type=jnp.float32
        )
        * scale,
        axis=-1,
    )
    cross_probs_low = cross_probs.astype(jnp.bfloat16)
    keep = ((seq_index > 0) | (jnp.arange(rows, dtype=jnp.int32) >= STRETCH - 1)).astype(
        jnp.float32
    )[:, None]
    cross_context = jnp.einsum(
        "ghqk,gkhd->gqhd", cross_probs_low, memory_values, preferred_element_type=jnp.float32
    ).reshape(groups * STRETCH, D)[1 : rows + 1]
    cross_low = (cross_context * keep).astype(jnp.bfloat16)
    stream_two = stream_one + matmul(cross_low, cross_output)
    normed_three, third_back = jax.vjp(layer_norm, stream_two, third_gain, third_shift)
    normed_three_low = normed_three.astype(jnp.bfloat16)
    upper = matmul(normed_three_low, up_weight)
    active, gelu_back = jax.vjp(partial(jax.nn.gelu, approximate=False), upper)
    active_low = active.astype(jnp.bfloat16)
    result = (stream_two + matmul(active_low, down_weight)).astype(jnp.bfloat16)
    grad_low = cotangent[0]
    down_grad = outer_sum(active_low, grad_low)
    active_grad = back_product(grad_low, down_weight)
    upper_low = gelu_back(active_grad)[0].astype(jnp.bfloat16)
    up_grad = outer_sum(normed_three_low, upper_low)
    stream_part, third_gain_grad, third_shift_grad = third_back(back_product(upper_low, up_weight))
    stream_two_grad = grad_low.astype(jnp.float32) + stream_part
    branch_low = stream_two_grad.astype(jnp.bfloat16)
    cross_output_grad = outer_sum(cross_low, branch_low)
    context_grad = (back_product(branch_low, cross_output) * keep).astype(jnp.bfloat16)
    padded_grad = jnp.concatenate([pad_top, context_grad, pad_end], axis=0).reshape(
        groups, STRETCH, HEADS, HEAD
    )
    prob_grad = jnp.einsum(
        "gqhd,gkhd->ghqk", padded_grad, memory_values, preferred_element_type=jnp.float32
    )
    score_low = (
        cross_probs * (prob_grad - jnp.sum(cross_probs * prob_grad, axis=-1, keepdims=True))
    ).astype(jnp.bfloat16)
    cross_query_low = (
        (
            jnp.einsum(
                "ghqk,gkhd->gqhd", score_low, memory_keys, preferred_element_type=jnp.float32
            )
            * scale
        )
        .reshape(groups * STRETCH, D)[1 : rows + 1]
        .astype(jnp.bfloat16)
    )
    key_part = (
        jnp.einsum("ghqk,gqhd->gkhd", score_low, padded_queries, preferred_element_type=jnp.float32)
        * scale
    )
    value_part = jnp.einsum(
        "ghqk,gqhd->gkhd", cross_probs_low, padded_grad, preferred_element_type=jnp.float32
    )
    extended_grad = jnp.concatenate(
        [key_part.reshape(groups, span, D), value_part.reshape(groups, span, D)], axis=-1
    )
    returned = from_behind(extended_grad[0].astype(jnp.bfloat16), "seq", -1).astype(jnp.float32)
    memory_grad = jnp.concatenate(
        [extended_grad[1:stretch_count], (extended_grad[stretch_count] + returned)[None]], axis=0
    )
    memory_grad = memory_grad.astype(jnp.bfloat16).reshape(stretch_count * span, 2 * D)
    memory_weight_grad = outer_sum(neighbour_rows, memory_grad)
    neighbour_grad = back_product(memory_grad, memory_weight).reshape(neighbours.shape)
    query_weight_grad = outer_sum(normed_two_low, cross_query_low)
    stream_part, second_gain_grad, second_shift_grad = second_back(
        back_product(cross_query_low, query_weight)
    )
    stream_one_grad = stream_two_grad + stream_part
    self_low = stream_one_grad.astype(jnp.bfloat16)
    self_output_grad = outer_sum(context_low, self_low)
    grad_out = back_product(self_low, self_output).astype(jnp.bfloat16).reshape(rows, HEADS, HEAD)
    delta = jnp.sum(jnp.transpose(grad_out.astype(jnp.float32), (1, 0, 2)) * context, axis=-1)
    gathered_keys, gathered_values, gathered_seg = (
        lax.all_gather(keys_low, "seq", axis=0, tiled=True),
        lax.all_gather(values_low, "seq", axis=0, tiled=True),
        lax.all_gather(seg_local, "seq", axis=0, tiled=True),
    )
    total_rows = gathered_keys.shape[0]
    size = block_rows()

    def key_step(query_sum, index):
        first = index * size
        keys = lax.dynamic_slice_in_dim(gathered_keys, first, size, 0).reshape(size, HEADS, HEAD)
        values = lax.dynamic_slice_in_dim(gathered_values, first, size, 0).reshape(
            size, HEADS, HEAD
        )
        key_seg = lax.dynamic_slice_in_dim(gathered_seg, first, size, 0)
        key_pos = first + jnp.arange(size, dtype=jnp.int32)
        query_part, key_block, value_block = key_block_grads(
            queries,
            grad_out,
            log_total,
            delta,
            positions,
            seg_local,
            keys,
            values,
            key_pos,
            key_seg,
            scale,
        )
        pair = jnp.concatenate([key_block.reshape(size, D), value_block.reshape(size, D)], axis=1)
        return (query_sum + query_part, pair)

    query_grad, pairs = lax.scan(
        key_step,
        jnp.zeros((rows, HEADS, HEAD), jnp.float32),
        jnp.arange(total_rows // size, dtype=jnp.int32),
    )
    pair_grad = lax.psum_scatter(
        pairs.reshape(total_rows, 2 * D).astype(jnp.bfloat16),
        "seq",
        scatter_dimension=0,
        tiled=True,
    ).astype(jnp.float32)
    projected_grad = jnp.concatenate([query_grad.reshape(rows, D), pair_grad], axis=1).astype(
        jnp.bfloat16
    )
    self_weight_grad = outer_sum(normed_one_low, projected_grad)
    stream_part, first_gain_grad, first_shift_grad = first_back(
        back_product(projected_grad, self_weight)
    )
    input_grad = stream_one_grad + stream_part
    shares = (
        lax.psum_scatter(
            first_gain_grad.astype(jnp.bfloat16), "batch", scatter_dimension=0, tiled=True
        ).astype(jnp.float32),
        lax.psum_scatter(
            first_shift_grad.astype(jnp.bfloat16), "batch", scatter_dimension=0, tiled=True
        ).astype(jnp.float32),
        lax.psum_scatter(
            self_weight_grad.astype(jnp.bfloat16), "batch", scatter_dimension=0, tiled=True
        ).astype(jnp.float32),
        lax.psum_scatter(
            self_output_grad.astype(jnp.bfloat16), "batch", scatter_dimension=0, tiled=True
        ).astype(jnp.float32),
        lax.psum_scatter(
            second_gain_grad.astype(jnp.bfloat16), "batch", scatter_dimension=0, tiled=True
        ).astype(jnp.float32),
        lax.psum_scatter(
            second_shift_grad.astype(jnp.bfloat16), "batch", scatter_dimension=0, tiled=True
        ).astype(jnp.float32),
        lax.psum_scatter(
            query_weight_grad.astype(jnp.bfloat16), "batch", scatter_dimension=0, tiled=True
        ).astype(jnp.float32),
        lax.psum_scatter(
            memory_weight_grad.astype(jnp.bfloat16), "batch", scatter_dimension=0, tiled=True
        ).astype(jnp.float32),
        lax.psum_scatter(
            cross_output_grad.astype(jnp.bfloat16), "batch", scatter_dimension=0, tiled=True
        ).astype(jnp.float32),
        lax.psum_scatter(
            third_gain_grad.astype(jnp.bfloat16), "batch", scatter_dimension=0, tiled=True
        ).astype(jnp.float32),
        lax.psum_scatter(
            third_shift_grad.astype(jnp.bfloat16), "batch", scatter_dimension=0, tiled=True
        ).astype(jnp.float32),
        lax.psum_scatter(
            up_grad.astype(jnp.bfloat16), "batch", scatter_dimension=0, tiled=True
        ).astype(jnp.float32),
        lax.psum_scatter(
            down_grad.astype(jnp.bfloat16), "batch", scatter_dimension=0, tiled=True
        ).astype(jnp.float32),
    )
    sums = (
        lax.psum(shares[0].astype(jnp.bfloat16), "seq").astype(jnp.float32),
        lax.psum(shares[1].astype(jnp.bfloat16), "seq").astype(jnp.float32),
        lax.psum(shares[2].astype(jnp.bfloat16), "seq").astype(jnp.float32),
        lax.psum(shares[3].astype(jnp.bfloat16), "seq").astype(jnp.float32),
        lax.psum(shares[4].astype(jnp.bfloat16), "seq").astype(jnp.float32),
        lax.psum(shares[5].astype(jnp.bfloat16), "seq").astype(jnp.float32),
        lax.psum(shares[6].astype(jnp.bfloat16), "seq").astype(jnp.float32),
        lax.psum(shares[7].astype(jnp.bfloat16), "seq").astype(jnp.float32),
        lax.psum(shares[8].astype(jnp.bfloat16), "seq").astype(jnp.float32),
        lax.psum(shares[9].astype(jnp.bfloat16), "seq").astype(jnp.float32),
        lax.psum(shares[10].astype(jnp.bfloat16), "seq").astype(jnp.float32),
        lax.psum(shares[11].astype(jnp.bfloat16), "seq").astype(jnp.float32),
        lax.psum(shares[12].astype(jnp.bfloat16), "seq").astype(jnp.float32),
    )
    return (
        result[None],
        input_grad[None],
        neighbour_grad,
        sums[0],
        sums[1],
        sums[2],
        sums[3],
        sums[4],
        sums[5],
        sums[6],
        sums[7],
        sums[8],
        sums[9],
        sums[10],
        sums[11],
        sums[12],
    )


def solution(mesh):
    placed = (
        P("batch", "seq", None),
        P("batch", "seq"),
        P("batch", "seq", None, None, None),
        P(),
        P(),
        P(),
        P(),
        P(),
        P(),
        P(),
        P(),
        P(),
        P(),
        P(),
        P(),
        P(),
        P("batch", "seq", None),
    )
    sizes = mesh.shape
    if sizes["seq"] == 8 and sizes["batch"] == 4:
        body = partial(on_device, sizes["seq"], sizes["batch"])
    else:
        body = plain_on_device
    return jax.shard_map(
        body,
        mesh=mesh,
        in_specs=placed,
        out_specs=(
            P("batch", "seq", None),
            P("batch", "seq", None),
            P("batch", "seq", None, None, None),
            P("batch"),
            P("batch"),
            P("batch", None),
            P("batch", None),
            P("batch"),
            P("batch"),
            P("batch", None),
            P("batch", None),
            P("batch", None),
            P("batch"),
            P("batch"),
            P("batch", None),
            P("batch", None),
        ),
        check_vma=False,
    )
```

```python
import functools
from functools import partial

import jax
import jax.numpy as jnp
from jax import lax
from jax.experimental import pallas as pl
from jax.experimental.pallas import tpu as pltpu
from jax.sharding import PartitionSpec as P
import math
from types import SimpleNamespace

D = 768
HEADS = 12
HEAD = 64
STRETCH = 64
NEIGHBOURS = 2
NEIGHBOUR_LEN = 128
SPAN = NEIGHBOURS * NEIGHBOUR_LEN
EPSILON = 1e-05
NEGATIVE = -1e30
MESH = pl.DeviceIdType.MESH
VM = pltpu.VMEM
F32 = jnp.float32
BF16 = jnp.bfloat16


def matmul(left, right):
    return jnp.dot(left, right, preferred_element_type=F32)


def outer_sum(left, right):
    return lax.dot_general(left, right, (((0,), (0,)), ((), ())), preferred_element_type=F32)


def back_product(left, right):
    return lax.dot_general(left, right, (((1,), (1,)), ((), ())), preferred_element_type=F32)


def low_lanes(shape):
    return lax.broadcasted_iota(jnp.int32, shape, len(shape) - 1) < HEAD


def swap_lanes(values):
    return pltpu.roll(values, HEAD, 1)


def as_row(vector):
    return vector[...].reshape(1, D)


def full_norm(values, gain, shift):
    mean = jnp.mean(values, axis=-1, keepdims=True)
    centred = values - mean
    spread = jnp.mean(centred * centred, axis=-1, keepdims=True)
    return centred * lax.rsqrt(spread + EPSILON) * gain + shift


class Plan:
    def __init__(self, devices, rows):
        self.devices = devices
        self.rows = rows
        self.groups = math.gcd(devices, HEADS)
        self.members = devices // self.groups
        self.slots = HEADS // self.groups

    def place(self):
        me = lax.axis_index("seq")
        return me, lax.div(me, self.members), lax.rem(me, self.members)


def seq_device(index):
    return (index, lax.axis_index("batch"))


def greet(devices):
    barrier = pltpu.get_barrier_semaphore()
    for device in devices:
        pl.semaphore_signal(barrier, inc=1, device_id=device, device_id_type=MESH)
    pl.semaphore_wait(barrier, len(devices))


def send(source, target, send_sem, recv_sem, device):
    return pltpu.make_async_remote_copy(
        src_ref=source,
        dst_ref=target,
        send_sem=send_sem,
        recv_sem=recv_sem,
        device_id=device,
        device_id_type=MESH,
    )


def pack_rows(values, head):
    half = values.shape[0] // 2
    top, bottom = values[:half], values[half:]
    low = low_lanes((half, 2 * HEAD))
    if head % 2 == 0:
        return jnp.where(low, top, swap_lanes(bottom))
    return jnp.where(low, swap_lanes(top), bottom)


def hide(plan, scores, k, g, member, start):
    causal = k == g
    if not (causal or k == 0 or g == plan.groups - 1):
        return scores
    at = lax.broadcasted_iota(jnp.int32, scores.shape, 0)
    allowed = at >= start - k * plan.members * plan.rows
    if causal:
        allowed = allowed & (at <= member * plan.rows + lax.broadcasted_iota(jnp.int32, scores.shape, 1))
    return jnp.where(allowed, scores, NEGATIVE)


def attend_kernel(plan, *refs):
    (
        tokens, gain, shift, segments, far_weight, far_neighbours, far_memory_weight,
        normed, logs, starts, context, edge, far_queries, far_pairs, far_outs, far_memory, far_packed,
        queries, pairs, outs, memory, packed, weight, neighbours, memory_weight,
        segs, projected, pack_pairs, pack_queries, got_queries, sent_context, got_context,
        pair_send, pair_recv, query_send, query_recv, pass_send, pass_recv,
        back_send, back_recv, seg_send, seg_recv, edge_send, edge_recv, load_sems, memory_sems, store_sems,
    ) = refs
    me, group, member = plan.place()
    devices, groups, members, slots, rows = plan.devices, plan.groups, plan.members, plan.slots, plan.rows
    others = [lax.rem(me + i, devices) for i in range(1, devices)]
    loads = [
        pltpu.make_async_copy(far_weight, weight, load_sems.at[0]),
        pltpu.make_async_copy(far_neighbours, neighbours, load_sems.at[1]),
        pltpu.make_async_copy(far_memory_weight, memory_weight, load_sems.at[2]),
    ]
    for copy in loads:
        copy.start()
    greet([seq_device(o) for o in others])
    half = rows // 2
    stretches = neighbours.shape[0] // SPAN
    low = low_lanes((rows, 2 * HEAD))

    seg_copies = []
    segs[me] = jnp.broadcast_to(segments[...].astype(F32), (8, rows))
    for i, o in enumerate(others):
        copy = send(segs.at[me], segs.at[me], seg_send.at[i], seg_recv.at[me], seq_device(o))
        copy.start()
        seg_copies.append(copy)
    last_rows = pl.ds((stretches - 1) * SPAN, SPAN)
    edge_copy = send(far_neighbours.at[last_rows], edge, edge_send, edge_recv, seq_device(jnp.minimum(me + 1, devices - 1)))

    @pl.when(me < devices - 1)
    def _():
        edge_copy.start()

    normed[...] = full_norm(tokens[...].astype(F32), as_row(gain), as_row(shift)).astype(BF16)

    loads[0].wait()

    @pl.loop(0, 3)
    def _(j):
        columns = pl.ds(pl.multiple_of(j * D, D), D)
        projected[:, columns] = matmul(normed[...], weight[:, columns])

    def pair_copy(slot, away):
        to = lax.rem(group + away, groups)
        return send(
            pack_pairs.at[to * slots + slot], pairs.at[slot, me],
            pair_send.at[slot, away - 1], pair_recv.at[slot, group], seq_device(to * members + member),
        )

    def query_copy(slot, away):
        to = lax.rem(group + away, groups)
        return send(
            pack_queries.at[to * slots + slot], got_queries.at[slot, group],
            query_send.at[slot, away - 1], query_recv.at[slot, group], seq_device(to * members + member),
        )

    def arrived_pair(slot, origin):
        return send(
            pack_pairs.at[0], pairs.at[slot, origin * members + member],
            pair_send.at[slot, 0], pair_recv.at[slot, origin], seq_device(me),
        )

    def arrived_query(slot, origin):
        return send(
            pack_queries.at[0], got_queries.at[slot, origin],
            query_send.at[slot, 0], query_recv.at[slot, origin], seq_device(me),
        )

    def pass_copy(slot, origin, away):
        to = lax.rem(member + away, members)
        place = origin * members + member
        return send(
            pairs.at[slot, place], pairs.at[slot, place],
            pass_send.at[slot, origin, away - 1], pass_recv.at[slot, place], seq_device(group * members + to),
        )

    def passed(slot, origin, away):
        source = lax.rem(member + away, members)
        place = origin * members + source
        return send(
            pairs.at[slot, place], pairs.at[slot, place],
            pass_send.at[slot, origin, 0], pass_recv.at[slot, place], seq_device(me),
        )

    for slot in range(slots):
        for head in range(slot, HEADS, slots):
            block = (head // 2) * 128
            key = projected[:, D + block : D + block + 128]
            value = projected[:, 2 * D + block : 2 * D + block + 128]
            if head % 2 == 0:
                pair = jnp.where(low, key, swap_lanes(value))
            else:
                pair = jnp.where(low, swap_lanes(key), value)
            pack_pairs[head] = pair.astype(BF16)
            query = projected[:, block : block + 128].astype(BF16).astype(F32) * (HEAD ** -0.5)
            pack_queries[head] = pack_rows(query, head).astype(BF16)
        for away in range(1, groups):
            pair_copy(slot, away).start()
            query_copy(slot, away).start()
    for slot in range(slots):
        pairs[slot, me] = pack_pairs[group * slots + slot]
        got_queries[slot, group] = pack_queries[group * slots + slot]
        for away in range(1, members):
            pass_copy(slot, group, away).start()

    for copy in loads[1:]:
        copy.wait()

    def memory_copy(s):
        return pltpu.make_async_copy(memory.at[s], far_memory.at[s], memory_sems.at[s])

    @pl.loop(0, stretches)
    def _(s):
        some = pl.ds(pl.multiple_of(s * SPAN, SPAN), SPAN)
        memory[s + 1] = matmul(neighbours[some], memory_weight[...]).astype(BF16)
        memory_copy(s + 1).start()

    @pl.when(me > 0)
    def _():
        edge_copy.wait_recv()
        memory[0] = matmul(edge[...], memory_weight[...]).astype(BF16)

    @pl.when(me == 0)
    def _():
        memory[0] = jnp.zeros_like(memory[0])
        edge[...] = jnp.zeros_like(edge)

    memory_copy(0).start()

    per = groups // members
    wide_low = low_lanes((D, 2 * HEAD))

    def columns_of(part, head):
        first = part * D + head // 2 * 128
        return weight[:, first : first + 128].astype(F32), head % 2

    for slot in range(slots):
        for owner in range(members):
            heads = [(owner * per + i) * slots + slot for i in range(per)]
            first = (slot * members + owner) * per * 3 * HEAD
            for i, head in enumerate(heads):
                (key, odd), (value, _) = columns_of(1, head), columns_of(2, head)
                pair = jnp.where(wide_low, swap_lanes(key), value) if odd else jnp.where(wide_low, key, swap_lanes(value))
                packed[:, first + i * 128 : first + i * 128 + 128] = pair.astype(BF16)
            (one, odd), (two, other) = columns_of(0, heads[0]), columns_of(0, heads[1])
            pair = jnp.where(wide_low, swap_lanes(one) if odd else one, two if other else swap_lanes(two))
            packed[:, first + per * 128 : first + per * 128 + 128] = pair.astype(BF16)
    packed_copy = pltpu.make_async_copy(packed, far_packed, memory_sems.at[stretches + 1])
    packed_copy.start()

    for copy in seg_copies:
        copy.wait_send()
    for i in range(1, devices):
        source = lax.rem(me + i, devices)
        send(segs.at[source], segs.at[source], seg_send.at[0], seg_recv.at[source], seq_device(me)).wait_recv()

    counts = [
        jnp.sum(jnp.sum((segs[:, 0, :] == value).astype(F32), axis=1, keepdims=True), axis=0, keepdims=True)
        for value in (0.0, 1.0)
    ]
    for g in range(groups):
        mine = segs[g * members + member]
        starts[g] = jnp.where(mine == 0.0, 0.0, counts[0] + jnp.where(mine == 1.0, 0.0, counts[1])).astype(jnp.int32)

    def back_copy(slot, to):
        return send(
            sent_context.at[slot, to], got_context.at[group * slots + slot],
            back_send.at[slot, to], back_recv.at[group * slots + slot], seq_device(to * members + member),
        )

    def stores(slot):
        return [
            pltpu.make_async_copy(queries.at[slot], far_queries.at[slot], store_sems.at[slot, 0]),
            pltpu.make_async_copy(pairs.at[slot], far_pairs.at[slot], store_sems.at[slot, 1]),
            pltpu.make_async_copy(outs.at[slot], far_outs.at[slot], store_sems.at[slot, 2]),
        ]

    def one_slot(slot, carry):
        for away in range(1, groups):
            origin = lax.rem(group + away, groups)
            arrived_pair(slot, origin).wait_recv()
            for beyond in range(1, members):
                pass_copy(slot, origin, beyond).start()
        for away in range(1, groups):
            origin = lax.rem(group + away, groups)
            arrived_query(slot, origin).wait_recv()
        for origin in range(groups):
            for beyond in range(1, members):
                passed(slot, origin, beyond).wait_recv()
        half_low = low_lanes((half, 2 * HEAD))
        for g in range(groups):
            packed = got_queries[slot, g].astype(F32)
            queries[slot, g, :half] = jnp.where(half_low, packed, 0.0).astype(BF16)
            queries[slot, g, half:] = jnp.where(half_low, swap_lanes(packed), 0.0).astype(BF16)
            query = queries[slot, g]
            scores = []
            for k in range(g + 1):
                tile = pairs[slot, k * members : (k + 1) * members].reshape(members * rows, 128)
                scores.append(hide(plan, back_product(tile, query), k, g, member, starts[g][:1]))
            top = functools.reduce(jnp.maximum, [jnp.max(s, axis=0, keepdims=True) for s in scores])
            total, out = 0.0, 0.0
            for k in range(g + 1):
                tile = pairs[slot, k * members : (k + 1) * members].reshape(members * rows, 128)
                chance = jnp.exp(scores[k] - top)
                total = total + jnp.sum(chance, axis=0, keepdims=True)
                out = out + outer_sum(tile, chance.astype(BF16))
            logs[slot, g] = jnp.broadcast_to(top + jnp.log(total), (8, rows))
            done = jnp.transpose(out / total)
            outs[slot, g] = done
            out_low = done.astype(BF16).astype(F32)
            packed_out = jnp.where(half_low, swap_lanes(out_low[:half]), out_low[half:]).astype(BF16)

            @pl.when(group != g)
            def _():
                sent_context[slot, g] = packed_out
                back_copy(slot, g).start()

            @pl.when(group == g)
            def _():
                got_context[group * slots + slot] = packed_out

        for copy in stores(slot):
            copy.start()
        return carry

    lax.fori_loop(0, slots, one_slot, 0)

    @pl.when(me < devices - 1)
    def _():
        edge_copy.wait_send()

    for slot in range(slots):
        for copy in stores(slot):
            copy.wait()
        for away in range(1, groups):
            origin = lax.rem(group + away, groups)
            pair_copy(slot, away).wait_send()
            query_copy(slot, away).wait_send()
            send(
                sent_context.at[slot, 0], got_context.at[origin * slots + slot],
                back_send.at[slot, 0], back_recv.at[origin * slots + slot], seq_device(me),
            ).wait_recv()
            back_copy(slot, origin).wait_send()
        for origin in range(groups):
            for beyond in range(1, members):
                pass_copy(slot, origin, beyond).wait_send()

    packed_copy.wait()

    @pl.loop(0, stretches + 1)
    def _(s):
        memory_copy(s).wait()

    for two in range(HEADS // 2):
        first = got_context[2 * two].astype(F32)
        second = got_context[2 * two + 1].astype(F32)
        half_low = low_lanes((half, 2 * HEAD))
        columns = slice(two * 128, two * 128 + 128)
        context[:half, columns] = jnp.where(half_low, first, swap_lanes(second)).astype(BF16)
        context[half:, columns] = jnp.where(half_low, swap_lanes(first), second).astype(BF16)


def attend(plan, tokens, gain, shift, segments, weight, neighbours, memory_weight):
    devices, groups, members, slots, rows = plan.devices, plan.groups, plan.members, plan.slots, plan.rows
    half = rows // 2
    stretches = neighbours.shape[0] // SPAN
    dma = pltpu.SemaphoreType.DMA
    near = [
        ((rows, D), BF16),
        ((slots, groups, 8, rows), F32),
        ((groups, 8, rows), jnp.int32),
        ((rows, D), BF16),
        ((SPAN, D), BF16),
    ]
    far = [
        ((slots, groups, rows, 128), BF16),
        ((slots, devices, rows, 128), BF16),
        ((slots, groups, rows, 128), F32),
        ((stretches + 1, SPAN, 2 * D), BF16),
        ((D, 3 * D), BF16),
    ]
    vmem, hbm = pl.BlockSpec(memory_space=VM), pl.BlockSpec(memory_space=pl.ANY)
    return pl.pallas_call(
        partial(attend_kernel, plan),
        out_shape=[jax.ShapeDtypeStruct(*s) for s in near + far],
        in_specs=[vmem] * 4 + [hbm] * 3,
        out_specs=[vmem] * len(near) + [hbm] * len(far),
        scratch_shapes=[VM(*s) for s in far]
        + [
            VM(weight.shape, BF16),
            VM(neighbours.shape, BF16),
            VM(memory_weight.shape, BF16),
            VM((devices, 8, rows), F32),
            VM((rows, 3 * D), F32),
            VM((HEADS, rows, 128), BF16),
            VM((HEADS, half, 128), BF16),
            VM((slots, groups, half, 128), BF16),
            VM((slots, groups, half, 128), BF16),
            VM((HEADS, half, 128), BF16),
            dma((slots, groups)),
            dma((slots, groups)),
            dma((slots, groups)),
            dma((slots, groups)),
            dma((slots, groups, members)),
            dma((slots, devices)),
            dma((slots, groups)),
            dma((HEADS,)),
            dma((devices,)),
            dma((devices,)),
            dma,
            dma,
            dma((3,)),
            dma((stretches + 2,)),
            dma((slots, 3)),
        ],
        compiler_params=pltpu.CompilerParams(
            collective_id=0, has_side_effects=True, vmem_limit_bytes=60 << 20
        ),
        name="attend",
    )(tokens, gain, shift, segments, weight, neighbours, memory_weight)


class Product:
    def __init__(self, matrix, first, count, at=0):
        self.matrix, self.first, self.count, self.at = matrix, first, count, at


class Share:
    def __init__(self, rows, columns, order, pieces, vectors=None):
        self.rows, self.columns, self.order, self.pieces, self.vectors = rows, columns, order, pieces, vectors


def shares_of(batch, groups, ff):
    short, tall = D // (batch * groups), ff // (batch * groups * 2)
    half = D // 2
    return [
        Share(tall, half, "xyz", []),
        Share(tall, half, "yxz", []),
        Share(short, ff // 4, "xyz", [Product(0, 0, ff // 4)]),
        Share(short, ff // 4, "zyx", [Product(0, ff // 4, ff // 4)]),
        Share(short, 512, "zyx", []),
        Share(short, 256 + half, "xzy", [Product(0, 0, half, 256)]),
        Share(short, half, "yxz", [Product(1, 0, half)]),
        Share(short, half, "xzy", [Product(2, 0, half)]),
        Share(short, half, "yzx", [Product(3, 0, half)]),
        Share(short, half, "xzy", [Product(4, 0, half)]),
        Share(short, 256, "yxz", [Product(5, 0, 256)]),
        Share(short, 256, "yzx", [Product(5, 256, 128)], vectors=128),
    ]


EARLY_STEPS = (2, 2, 1, 1)
EARLY = len(EARLY_STEPS)


def axes_after(share, steps):
    return "".join(axis for axis in "zyx" if axis not in share.order[:steps])

SCHEDULE = (
    (), (), (), (), (0,), (6, 1), (), (7,), (1, 2), (4,), (7, 5), (-1, 2, -2, 6, 8), (9, 3), (),
    (8, 0, 5, 10), (4, 11, 9), (4,), (2, 3), (), (1,), (), (7, 6), (5, 10, 11, 3, 8), (4, 7), (0, 6, 8), (),
    (), (9, 10), (5,), (2, 11, 9, 11), (6,), (10, 8), (4, 9, 11), (2, 3, 5, 4, 10), (6, 8, 7), (11,),
    (5, 9, 1, 10), (7,), (8, 11, 3, 9, 0, 10),
)


def part_shape(share, batch, axes):
    sizes = {"z": batch, "y": 2, "x": 2}
    return tuple(sizes[a] for a in axes) + (share.rows, share.columns)


def step_shapes(share, batch, axes, order):
    shapes = []
    for axis in order:
        axes = axes.replace(axis, "")
        lead = (batch - 1,) if axis == "z" else ()
        shapes.append(lead + part_shape(share, batch, axes))
    return shapes


def add(a, b):
    return (a.astype(F32) + b.astype(F32)).astype(BF16)


class Engine:
    def __init__(self, plan, batch, shares, sums, arrivals, gathered, send_sems, recv_sems, keep_sems):
        self.plan, self.batch, self.shares = plan, batch, shares
        self.sums, self.arrivals, self.gathered = sums, arrivals, gathered
        self.send_sems, self.recv_sems, self.keep_sems = send_sems, recv_sems, keep_sems
        me, group, member = plan.place()
        self.me, self.group, self.member = me, group, member
        self.z = lax.axis_index("batch")
        self.x, self.y = lax.rem(group, 2), lax.div(group, 2)
        self.partner = seq_device(group * plan.members + 1 - member)
        chip = lambda g: seq_device(g * plan.members + member)
        self.across = {"x": chip(self.y * 2 + 1 - self.x), "y": chip((1 - self.y) * 2 + self.x)}
        self.diagonal = chip((1 - self.y) * 2 + 1 - self.x)
        self.layers = [lax.rem(self.z + i, batch) for i in range(1, batch)]

    def peers(self):
        return [self.partner, self.across["x"], self.across["y"], self.diagonal] + [
            (self.me, layer) for layer in self.layers
        ]

    def steps(self, s, fill, axes, order, stop=None):
        total, share = self.sums[s], self.shares[s]
        own = {"x": self.x, "y": self.y, "z": self.z}
        count = 0

        def sems():
            nonlocal count
            count += 1
            return self.send_sems.at[s, count - 1], self.recv_sems.at[s, count - 1]

        fill()
        done = {}
        for number, axis in enumerate(order):
            where = lambda spots: tuple(spots.get(a, slice(None)) for a in axes)
            arrived = self.arrivals[s][number]
            copies = []
            if axis == "z":
                for i, layer in enumerate(self.layers):
                    copies.append(
                        send(total.at[where({**done, "z": layer})], arrived.at[i], *sems(), (self.me, layer))
                    )
            else:
                copies.append(
                    send(total.at[where({**done, axis: 1 - own[axis]})], arrived, *sems(), self.across[axis])
                )
            for copy in copies:
                copy.start()
            yield
            for copy in copies:
                copy.wait()
            done[axis] = own[axis]
            spot = where(done)
            value = total[spot].astype(F32)
            if axis == "z":
                for i in range(self.batch - 1):
                    value = value + arrived[i].astype(F32)
            else:
                value = value + arrived[...].astype(F32)
            if stop is None or number < len(order) - 1:
                total[spot] = value.astype(BF16)
            else:
                stop[...] = value.astype(BF16)
        if stop is not None:
            return
        out = self.gathered[s]
        block = total.at[where(done)]
        first, second = share.order.replace("z", "")[::-1]
        home = out.at[self.member, self.y, self.x]
        keep = pltpu.make_async_copy(block, home, self.keep_sems.at[s])
        keep.start()
        copy = send(block, home, *sems(), self.across[first])
        copy.start()
        yield
        copy.wait()
        came = (self.member, 1 - self.y, self.x) if first == "y" else (self.member, self.y, 1 - self.x)
        copies = [send(block, home, *sems(), self.across[second])]
        copies.append(send(out.at[came], out.at[came], *sems(), self.across[second]))
        for copy in copies:
            copy.start()
        keep.wait()
        yield
        for copy in copies:
            copy.wait()
        copy = send(out.at[self.member], out.at[self.member], *sems(), self.partner)
        copy.start()
        yield
        copy.wait()


def spread_to(target, rows, values, at):
    layers, groups = target.shape[0], target.shape[1] * target.shape[2]
    for layer in range(layers):
        for g in range(groups):
            start = (layer * groups + g) * rows
            target[layer, g // 2, g % 2, :, pl.ds(at, values.shape[1])] = values[start : start + rows].astype(BF16)


def tail_kernel(plan, batch, shares, arrival_counts, names, *refs):
    r = SimpleNamespace(**dict(zip(names, refs)))
    refs = refs[len(names) :]
    takes = iter(refs)
    neighbour_grad = next(takes)
    gathered = [next(takes) for _ in shares]
    two_left = [next(takes) for _ in range(4)]
    two_right = [next(takes) for _ in range(3 + plan.slots)]
    give_right = [next(takes) for _ in range(plan.slots)]
    sums = [next(takes) for _ in shares]
    arrivals = [[next(takes) for _ in range(n)] for n in arrival_counts]
    (
        queries, pairs, outs, got_grads, grads, deltas, pair_sum, query_sum,
        give, took, sent_pair, got_pair, sent_query, got_query, vector_rows, other_rows,
        turned_weight, slopes, memory_weight, stage, edge_sent, edge_got,
        load_sems, out_send, out_recv, give_send, give_recv, pair_send, pair_recv, query_send, query_recv,
        own_sems, swap_send, swap_recv, state_sems, near_sems, stage_sems, edge_send, edge_recv, send_sems, recv_sems, keep_sems,
    ) = takes
    me, group, member = plan.place()
    devices, groups, members, slots, rows = plan.devices, plan.groups, plan.members, plan.slots, plan.rows
    half = rows // 2
    half_low = low_lanes((half, 2 * HEAD))
    low = low_lanes((rows, 2 * HEAD))
    engine = Engine(plan, batch, shares, sums, arrivals, gathered, send_sems, recv_sems, keep_sems)
    partner = engine.partner
    before = jnp.maximum(me - 1, 0)
    greet(
        [seq_device(lax.rem(me + i, devices)) for i in range(1, devices)]
        + [(me, layer) for layer in engine.layers]
    )

    def load(slot):
        spot = slot % 2
        return [
            pltpu.make_async_copy(r.queries.at[slot], queries.at[spot], load_sems.at[spot, 0]),
            pltpu.make_async_copy(r.pairs.at[slot], pairs.at[spot], load_sems.at[spot, 1]),
            pltpu.make_async_copy(r.outs.at[slot], outs.at[spot], load_sems.at[spot, 2]),
        ]

    for copy in load(0):
        copy.start()

    def out_copy(slot, away):
        to = lax.rem(group + away, groups)
        return send(
            r.packed_grads.at[to * slots + slot], got_grads.at[slot, group],
            out_send.at[slot, away - 1], out_recv.at[slot, group], seq_device(to * members + member),
        )

    for slot in range(slots):
        for away in range(1, groups):
            out_copy(slot, away).start()
        got_grads[slot, group] = r.packed_grads[group * slots + slot]

    state_loads = [
        pltpu.make_async_copy(getattr(r, "state%d" % s), sums[s], state_sems.at[s]) for s in range(EARLY)
    ]
    stretches = slopes.shape[0] // SPAN - 1
    near_loads = [
        pltpu.make_async_copy(r.memory_grad, slopes, near_sems.at[0]),
        pltpu.make_async_copy(r.memory_weight, memory_weight, near_sems.at[1]),
    ]
    first = sums[EARLY].shape[-1]
    rest = r.memory_part.shape[-1] - first
    memory_loads = [
        pltpu.make_async_copy(r.memory_part.at[:, :, :, :, pl.ds(0, first)], sums[EARLY], near_sems.at[2]),
        pltpu.make_async_copy(
            r.memory_part.at[:, :, :, :, pl.ds(first, rest)],
            sums[EARLY + 1].at[:, :, :, :, pl.ds(0, rest)],
            near_sems.at[3],
        ),
    ]
    packed_load = pltpu.make_async_copy(r.weight, turned_weight, near_sems.at[4])
    for copy in state_loads + memory_loads + near_loads + [packed_load]:
        copy.start()

    lefts = [getattr(r, "left%d" % m) for m in range(4)]
    rights = [getattr(r, "right%d" % m) for m in range(3)]
    here, there = pl.ds(0, rows), pl.ds(rows, rows)

    def left_swaps(m):
        return [
            pltpu.make_async_copy(lefts[m], two_left[m].at[here], own_sems.at[m, 0]),
            send(lefts[m], two_left[m].at[there], swap_send.at[m, 0], swap_recv.at[m, 0], partner),
        ]

    def right_swaps(m):
        width = rights[m].shape[1] // 2
        mine = pl.ds(pl.multiple_of(member * width, 128), width)
        theirs = pl.ds(pl.multiple_of((1 - member) * width, 128), width)
        return [
            pltpu.make_async_copy(rights[m].at[:, mine], two_right[m].at[here], own_sems.at[m, 1]),
            send(rights[m].at[:, theirs], two_right[m].at[there], swap_send.at[m, 1], swap_recv.at[m, 1], partner),
        ]

    swaps = {}
    for m in range(3):
        swaps[m] = left_swaps(m) + right_swaps(m)
        for copy in swaps[m]:
            copy.start()
    last_left = left_swaps(3)
    for copy in last_left:
        copy.start()

    def edge_copy():
        return send(edge_sent, edge_got, edge_send, edge_recv, seq_device(before))

    def stage_copy(s):
        return pltpu.make_async_copy(
            stage.at[s % 2], neighbour_grad.at[pl.ds(s * SPAN, SPAN)], stage_sems.at[s % 2]
        )

    def neighbour_grads(numbers):
        for s in numbers:
            if s >= 2:
                stage_copy(s - 2).wait()
            part = back_product(slopes[(s + 1) * SPAN : (s + 2) * SPAN, :], memory_weight[...])
            stage[s % 2] = part.astype(BF16)
            if s == stretches - 1:

                @pl.when(me < devices - 1)
                def _():
                    edge_copy().wait_recv()
                    stage[s % 2] = (part + edge_got[...].astype(F32)).astype(BF16)

            stage_copy(s).start()

    def slot_swap(slot):
        return send(
            give_right[slot], two_right[3 + slot].at[there], swap_send.at[4 + slot, 1], swap_recv.at[4 + slot, 1], partner
        )

    def arrive(slot):
        for away in range(1, groups):
            origin = lax.rem(group + away, groups)
            head = origin * slots + slot
            send(
                sent_query.at[slot, 0], got_query.at[head],
                query_send.at[slot, 0], query_recv.at[head], partner,
            ).wait_recv()
            send(
                sent_pair.at[0], got_pair.at[head], pair_send.at[slot, 0], pair_recv.at[head], partner,
            ).wait_recv()
        for owner, target in ((1 - member, give_right[slot]), (member, two_right[3 + slot].at[here])):
            heads = [(owner * 2 + i) * slots + slot for i in range(2)]
            for i in range(2):
                target[:, i * 128 : (i + 1) * 128] = got_pair[heads[i]]
            first, second = [got_query[head].astype(F32) for head in heads]
            target[:half, 256:384] = jnp.where(half_low, first, swap_lanes(second)).astype(BF16)
            target[half:, 256:384] = jnp.where(half_low, swap_lanes(first), second).astype(BF16)
            if target is give_right[slot]:
                slot_swap(slot).start()

    waited = set()
    last_left_done = []

    def spread(s, values, at):
        spread_to(sums[s], shares[s].rows, values, at)

    def fill(s):
        if EARLY <= s < EARLY + 2:
            memory_loads[s - EARLY].wait()
        for piece in shares[s].pieces:
            m = piece.matrix
            if m not in waited:
                waited.add(m)
                if m < 3:
                    for copy in swaps[m]:
                        copy.wait()
                else:
                    slot_swap(m - 3).wait()
            if m >= 3 and not last_left_done:
                last_left_done.append(m)
                for copy in last_left:
                    copy.wait()
            tile = piece.count if piece.count <= 512 else 384
            for t in range(piece.count // tile):
                first = piece.first + t * tile
                spread(s, outer_sum(two_left[min(m, 3)][...], two_right[m][:, first : first + tile]), piece.at + t * tile)
        if shares[s].vectors is not None:
            vector_copy.wait()
            mine = vector_rows[member] + other_rows[...]
            wide = jnp.concatenate([mine, jnp.zeros((120, D), F32)], axis=0)
            spread(s, jnp.transpose(wide), shares[s].vectors)

    def ready(s):
        state_loads[s].wait()

    running = []
    for s, share in enumerate(shares):
        if s < EARLY:
            axes = axes_after(share, EARLY_STEPS[s])
            running.append(engine.steps(s, partial(ready, s), axes, share.order[EARLY_STEPS[s] :]))
        else:
            running.append(engine.steps(s, partial(fill, s), "zyx", share.order))

    def advance(*numbers):
        for n in numbers:
            next(running[n], None)

    advance(0, 1, 2, 3, 4, 5)
    advance(6, 7)

    def give_copy(slot, away):
        to = lax.rem(member + away, members)
        return send(
            give.at[away - 1], took.at[slot, away - 1],
            give_send.at[slot, away - 1], give_recv.at[slot, away - 1], seq_device(group * members + to),
        )

    def pair_copy(slot, to):
        return send(
            sent_pair.at[to], got_pair.at[group * slots + slot],
            pair_send.at[slot, to], pair_recv.at[group * slots + slot], seq_device(to * members + member),
        )

    def query_copy(slot, to):
        return send(
            sent_query.at[slot, to], got_query.at[group * slots + slot],
            query_send.at[slot, to], query_recv.at[group * slots + slot], seq_device(to * members + member),
        )

    def tick():
        for action in next(schedule, ()):
            if action < 0:
                arrive(-1 - action)
            else:
                advance(action)

    schedule = iter(SCHEDULE)
    for slot in range(slots):
        spot = slot % 2
        for copy in load(slot):
            copy.wait()
        if slot + 1 < slots:
            for copy in load(slot + 1):
                copy.start()
        for away in range(1, groups):
            origin = lax.rem(group + away, groups)
            out_copy(slot, away).wait_send()
            send(
                r.packed_grads.at[0], got_grads.at[slot, origin],
                out_send.at[slot, 0], out_recv.at[slot, origin], partner,
            ).wait_recv()
        for g in range(groups):
            part = got_grads[slot, g].astype(F32)
            top = jnp.where(half_low, 0.0, swap_lanes(part))
            bottom = jnp.where(half_low, 0.0, part)
            grads[g, :half] = top.astype(BF16)
            grads[g, half:] = bottom.astype(BF16)
            product = jnp.concatenate([top, bottom], axis=0) * outs[spot, g]
            deltas[g] = jnp.broadcast_to(jnp.sum(jnp.transpose(product), axis=0, keepdims=True), (8, rows))
        for k in range(groups):
            total = 0.0
            tile = pairs[spot, k * members : (k + 1) * members].reshape(members * rows, 128)
            for g in range(k, groups):
                query, grad = queries[spot, g], grads[g]
                scores = hide(plan, back_product(tile, query), k, g, member, r.starts[g][:1])
                chance = jnp.exp(scores - r.logs[slot, g][:1])
                chance_grad = back_product(tile, grad)
                score_grad = (chance * (chance_grad - deltas[g][:1])).astype(BF16)
                total = total + matmul(score_grad, query) + matmul(chance.astype(BF16), grad)
                part = outer_sum(tile, score_grad)
                query_sum[g] = part if k == 0 else query_sum[g] + part
            pair_sum[k * members : (k + 1) * members] = total.reshape(members, rows, 128)
            if k < groups - 1:
                tick()
        for away in range(1, members):
            to = lax.rem(member + away, members)
            if slot > 0:
                give_copy(slot - 1, away).wait_send()
            for g in range(groups):
                give[away - 1, g] = pair_sum[g * members + to].astype(BF16)
            give_copy(slot, away).start()
        for g in range(groups):
            total = jnp.transpose(query_sum[g]) * (HEAD ** -0.5)
            packed = jnp.where(half_low, total[:half], swap_lanes(total[half:])).astype(BF16)

            @pl.when(group != g)
            def _():
                sent_query[slot, g] = packed
                query_copy(slot, g).start()

            @pl.when(group == g)
            def _():
                got_query[group * slots + slot] = packed

        for away in range(1, members):
            give_copy(slot, away).wait_recv()
        for g in range(groups):
            total = pair_sum[g * members + member]
            for away in range(1, members):
                total = total + took[slot, away - 1, g].astype(F32)
            total = total.astype(BF16)

            @pl.when(group != g)
            def _():
                if slot > 0:
                    pair_copy(slot - 1, g).wait_send()
                sent_pair[g] = total
                pair_copy(slot, g).start()

            @pl.when(group == g)
            def _():
                got_pair[group * slots + slot] = total

        if slot == 0:
            for copy in near_loads:
                copy.wait()
            edge_sent[...] = back_product(slopes[0:SPAN, :], memory_weight[...]).astype(BF16)

            @pl.when(me > 0)
            def _():
                edge_copy().start()

        tick()

    tick()
    arrive(slots - 1)
    tick()
    packed_load.wait()
    normed_grad = 0.0
    for slot in range(slots):
        for owner, part in ((member, two_right[3 + slot][here]), (1 - member, give_right[slot][...])):
            columns = pl.ds(pl.multiple_of(slot * D + owner * (D // 2), 128), D // 2)
            normed_grad = normed_grad + back_product(part, turned_weight[:, columns])
    values = r.tokens[...].astype(F32)
    centred = values - jnp.mean(values, axis=1, keepdims=True)
    inverse = lax.rsqrt(jnp.mean(centred * centred, axis=1, keepdims=True) + EPSILON)
    unit = centred * inverse
    vector_rows[0] = jnp.concatenate(
        [jnp.sum(normed_grad * unit, axis=0, keepdims=True), r.vectors[0:2], jnp.zeros((5, D), F32)], axis=0
    )
    vector_rows[1] = jnp.concatenate(
        [jnp.sum(normed_grad, axis=0, keepdims=True), r.vectors[2:4], jnp.zeros((5, D), F32)], axis=0
    )
    vector_copy = send(
        vector_rows.at[1 - member], other_rows, swap_send.at[3, 1], swap_recv.at[3, 1], partner
    )
    vector_copy.start()
    tick()
    scaled = normed_grad * as_row(r.gain)
    input_grad = r.stream_grad[...] + inverse * (
        scaled
        - jnp.mean(scaled, axis=1, keepdims=True)
        - unit * jnp.mean(scaled * unit, axis=1, keepdims=True)
    )
    r.input_grad[...] = input_grad.astype(BF16)
    tick()
    for s in range(stretches):
        neighbour_grads([s])
        tick()
    for _ in range(40):
        tick()
    for _ in range(8):
        advance(*range(len(shares)))

    for s in range(max(stretches - 2, 0), stretches):
        stage_copy(s).wait()

    @pl.when(me > 0)
    def _():
        edge_copy().wait_send()

    for slot in range(slots):
        for away in range(1, members):
            if slot == slots - 1:
                give_copy(slot, away).wait_send()
        for away in range(1, groups):
            origin = lax.rem(group + away, groups)
            if slot == slots - 1:
                pair_copy(slot, origin).wait_send()
            query_copy(slot, origin).wait_send()


def tail(plan, batch, packed_grads, queries, pairs, outs, logs, starts, lefts, rights, states,
    memory_part, memory_grad, memory_weight, weight, tokens, gain, stream_grad, vectors, ff,
):
    devices, groups, members, slots, rows = plan.devices, plan.groups, plan.members, plan.slots, plan.rows
    half = rows // 2
    shares = shares_of(batch, groups, ff)
    dma = pltpu.SemaphoreType.DMA
    inputs = dict(packed_grads=packed_grads, logs=logs, starts=starts, tokens=tokens, gain=gain)
    inputs.update(stream_grad=stream_grad, vectors=vectors)
    small = len(inputs)
    inputs.update(queries=queries, pairs=pairs, outs=outs, weight=weight)
    inputs.update({"left%d" % m: left for m, left in enumerate(lefts)})
    inputs.update({"right%d" % m: right for m, right in enumerate(rights)})
    inputs.update({"state%d" % m: state for m, state in enumerate(states)})
    inputs.update(memory_part=memory_part, memory_grad=memory_grad, memory_weight=memory_weight)
    widths = [right.shape[1] // 2 for right in rights] + [D // 2] * slots
    early = EARLY_STEPS + (0,) * (len(shares) - EARLY)
    axes = [axes_after(share, count) for share, count in zip(shares, early)]
    orders = [share.order[count:] for share, count in zip(shares, early)]
    steps = [step_shapes(share, batch, axes[n], orders[n]) for n, share in enumerate(shares)]
    scratch = [VM((2 * rows, left.shape[1]), BF16) for left in lefts]
    scratch += [VM((2 * rows, width), BF16) for width in widths]
    scratch += [VM((rows, D // 2), BF16)] * slots
    scratch += [VM(part_shape(share, batch, axes[n]), BF16) for n, share in enumerate(shares)]
    scratch += [VM(shape, BF16) for shapes in steps for shape in shapes]
    span_rows = memory_grad.shape[0]
    scratch += [
        VM((2, groups, rows, 128), BF16),
        VM((2, devices, rows, 128), BF16),
        VM((2, groups, rows, 128), F32),
        VM((slots, groups, half, 128), BF16),
        VM((groups, rows, 128), BF16),
        VM((groups, 8, rows), F32),
        VM((devices, rows, 128), F32),
        VM((groups, 128, rows), F32),
        VM((members - 1, groups, rows, 128), BF16),
        VM((slots, members - 1, groups, rows, 128), BF16),
        VM((groups, rows, 128), BF16),
        VM((HEADS, rows, 128), BF16),
        VM((slots, groups, half, 128), BF16),
        VM((HEADS, half, 128), BF16),
        VM((2, 8, D), F32),
        VM((8, D), F32),
        VM((D, 3 * D), BF16),
        VM((span_rows, 2 * D), BF16),
        VM((D, 2 * D), BF16),
        VM((2, SPAN, D), BF16),
        VM((SPAN, D), BF16),
        VM((SPAN, D), BF16),
        dma((2, 3)),
        dma((slots, groups)),
        dma((slots, groups)),
        dma((slots, members - 1)),
        dma((slots, members - 1)),
        dma((slots, groups)),
        dma((HEADS,)),
        dma((slots, groups)),
        dma((HEADS,)),
        dma((4, 2)),
        dma((4 + slots, 2)),
        dma((4 + slots, 2)),
        dma((EARLY,)),
        dma((5,)),
        dma((2,)),
        dma,
        dma,
        dma((len(shares), 6 + batch)),
        dma((len(shares), 6 + batch)),
        dma((len(shares),)),
    ]
    names = list(inputs) + ["input_grad"]
    out = pl.pallas_call(
        partial(tail_kernel, plan, batch, shares, [len(s) for s in steps], names),
        out_shape=[jax.ShapeDtypeStruct((rows, D), BF16), jax.ShapeDtypeStruct((span_rows - SPAN, D), BF16)]
        + [jax.ShapeDtypeStruct((2, 2, 2, s.rows, s.columns), BF16) for s in shares],
        in_specs=[pl.BlockSpec(memory_space=VM)] * small + [pl.BlockSpec(memory_space=pl.ANY)] * (len(inputs) - small),
        out_specs=[pl.BlockSpec(memory_space=VM)] + [pl.BlockSpec(memory_space=pl.ANY)] * (1 + len(shares)),
        scratch_shapes=scratch,
        compiler_params=pltpu.CompilerParams(
            collective_id=1, has_side_effects=True, vmem_limit_bytes=62 << 20
        ),
        name="tail",
    )(*inputs.values())
    return out[0], out[1], out[2:]


def widen_kernel(plan, *refs):
    shares, (low_result, low_input, low_neighbour) = refs[:12], refs[12:15]
    down, up, cross_out, memory, query, self_out, self_weight, result, input_grad, neighbour_grad = refs[15:25]
    vectors, kept = refs[25:31], refs[31]
    step = pl.program_id(0)

    def put(out, s, at, first, count):
        for core in range(2):
            width = out.shape[1] // 2
            block = shares[s][core, 0, 0, :, first : first + count]
            out[:, core * width + at : core * width + at + count] = block.astype(F32)

    for part in range(2):
        for core in range(2):
            tall = shares[part].shape[3]
            out_rows = slice(part * tall, part * tall + tall)
            down[out_rows, core * (D // 2) : (core + 1) * (D // 2)] = shares[part][core, 0, 0].astype(F32)
    quarter = up.shape[1] // 4
    put(up, 2, 0, 0, quarter)
    put(up, 3, quarter, 0, quarter)
    put(memory, 4, 0, 0, 512)
    put(memory, 5, 512, 0, 256)
    put(cross_out, 5, 0, 256, D // 2)
    put(query, 6, 0, 0, D // 2)
    put(self_out, 7, 0, 0, D // 2)
    rows = shares[8].shape[3]
    low = low_lanes((rows, 2 * HEAD))

    def block(head, spot):
        g, slot = head // plan.slots, head % plan.slots
        core, i = g // 2, g % 2
        spot = i if spot is None else spot
        s, first = (8 + slot, spot * 128) if slot < 2 else (10, spot * 128) if spot < 2 else (11, 0)
        return shares[s][core, 0, 0, :, first : first + 128].astype(F32), i

    for two in range(HEADS // 2):
        heads = (2 * two, 2 * two + 1)
        columns = slice(two * 128, two * 128 + 128)
        (one, i), (other, j) = [block(head, 2) for head in heads]
        self_weight[:, columns] = jnp.where(low, swap_lanes(one) if i else one, other if j else swap_lanes(other))
        one, other = [block(head, None)[0] for head in heads]
        self_weight[:, slice(D + two * 128, D + two * 128 + 128)] = jnp.where(low, one, swap_lanes(other))
        self_weight[:, slice(2 * D + two * 128, 2 * D + two * 128 + 128)] = jnp.where(low, swap_lanes(one), other)
    result[...] = low_result[...]
    input_grad[...] = low_input[...].astype(F32)
    neighbour_grad[...] = low_neighbour[...].astype(F32)
    for core in range(2):
        kept[core, pl.ds(pl.multiple_of(step * rows, 16), rows)] = shares[11][core, 0, 0, :, 128:].astype(F32)

    @pl.when(step == 3)
    def _():
        for core in range(2):
            turned = jnp.transpose(kept[core])
            for n in range(3):
                vectors[core * 3 + n][...] = turned[n]


def widen(plan, batch, ff, shares, result, input_grad, neighbour_grad):
    rows = plan.rows
    ins = [pl.BlockSpec((2, 1, 1) + s.shape[3:], lambda i: (0, i // 2, i % 2, 0, 0)) for s in shares]
    passed = [result, input_grad, neighbour_grad]
    ins += [pl.BlockSpec((a.shape[0] // 4, D), lambda i: (i, 0)) for a in passed]
    layout = [(ff, D), (D, ff), (D, D), (D, 2 * D), (D, D), (D, D), (D, 3 * D)]
    layout = [(r // batch, c) for r, c in layout] + [a.shape for a in passed]
    kinds = [F32] * 7 + [BF16, F32, F32]
    outs = [pl.BlockSpec((r // 4, c), lambda i: (i, 0)) for r, c in layout]
    outs += [pl.BlockSpec((D // batch,), lambda i: (0,))] * 6
    return pl.pallas_call(
        partial(widen_kernel, plan),
        grid=(4,),
        in_specs=ins,
        out_specs=outs,
        out_shape=[jax.ShapeDtypeStruct(shape, kind) for shape, kind in zip(layout, kinds)]
        + [jax.ShapeDtypeStruct((D // batch,), F32)] * 6,
        scratch_shapes=[VM((2, D // batch, 128), F32)],
        compiler_params=pltpu.CompilerParams(vmem_limit_bytes=60 << 20),
        name="widen",
    )(*shares, *passed)


FOLD = 256 // HEAD


def stack_heads(values):
    lane = lax.broadcasted_iota(jnp.int32, values.shape, 1) // HEAD
    return jnp.concatenate([jnp.where(lane == h, values, jnp.zeros_like(values)) for h in range(FOLD)], axis=0)


def unstack_heads(stacked):
    count = stacked.shape[0] // FOLD
    lane = lax.broadcasted_iota(jnp.int32, (count, stacked.shape[1]), 1) // HEAD
    total = jnp.where(lane == 0, stacked[:count], 0.0)
    for h in range(1, FOLD):
        total = total + jnp.where(lane == h, stacked[h * count : (h + 1) * count], 0.0)
    return total


def cross_chances(queries, keys):
    scores = back_product(queries, keys)
    chance = jnp.exp(scores - jnp.max(scores, axis=1, keepdims=True))
    return chance / jnp.sum(chance, axis=1, keepdims=True)


def norm_parts(values):
    centred = values - jnp.mean(values, axis=1, keepdims=True)
    inverse = lax.rsqrt(jnp.mean(centred * centred, axis=1, keepdims=True) + EPSILON)
    return centred * inverse, inverse


def norm_back(values, gain, grad):
    unit, inverse = norm_parts(values)
    scaled = grad * gain
    inner = inverse * (
        scaled - jnp.mean(scaled, axis=1, keepdims=True) - unit * jnp.mean(scaled * unit, axis=1, keepdims=True)
    )
    return jnp.sum(grad * unit, axis=0, keepdims=True), jnp.sum(grad, axis=0, keepdims=True), inner


def middle_kernel(plan, batch, shares, arrival_counts, names, *refs):
    r = SimpleNamespace(**dict(zip(names, refs)))
    takes = iter(refs[len(names) :])
    sums = [next(takes) for _ in range(EARLY)]
    arrivals = [[next(takes) for _ in range(n)] for n in arrival_counts]
    (
        up, down, active, two_normed, give_upper, two_upper, two_grad, slopes,
        stream_one, stream_two, normed_grad, summed, moved_queries, moved_grads, moved,
        load_sems, own_sems, tile_send, tile_recv, swap_send, swap_recv, group_sems, near_sems, send_sems, recv_sems,
    ) = takes
    me, group, member = plan.place()
    rows, groups = plan.rows, plan.groups
    states = [getattr(r, "state%d" % s) for s in range(EARLY)]
    engine = Engine(plan, batch, shares, sums, arrivals, None, send_sems, recv_sems, None)
    partner = engine.partner
    greet(engine.peers())
    here, there = pl.ds(0, rows), pl.ds(rows, rows)
    ff = up.shape[1]
    loads = [
        pltpu.make_async_copy(r.memory, slopes, load_sems.at[2]),
        pltpu.make_async_copy(r.up_weight, up, load_sems.at[0]),
        pltpu.make_async_copy(r.down_weight, down, load_sems.at[1]),
    ]
    for copy in loads:
        copy.start()
    half = D // 2
    mine = pl.ds(pl.multiple_of(member * half, 128), half)
    theirs = pl.ds(pl.multiple_of((1 - member) * half, 128), half)
    grad_swap = [
        pltpu.make_async_copy(r.cotangent.at[:, mine], two_grad.at[here], own_sems.at[0]),
        send(r.cotangent.at[:, theirs], two_grad.at[there], swap_send.at[0], swap_recv.at[0], partner),
    ]
    for copy in grad_swap:
        copy.start()
    at = lax.broadcasted_iota(jnp.int32, (rows, 1), 0)
    keep = ((me > 0) | (at >= STRETCH - 1)).astype(F32)
    stretches = slopes.shape[0]

    def move(values):
        wide = jnp.concatenate([values, jnp.zeros((STRETCH, D), F32)], axis=0)
        return pltpu.roll(wide, 1, 0).astype(BF16).reshape(stretches, STRETCH, D)

    def move_back():
        whole = moved[...].reshape(stretches * STRETCH, D)
        return pltpu.roll(whole, stretches * STRETCH - 1, 0)[:rows]

    stream_one[...] = r.tokens[...].astype(F32) + matmul(r.context[...], r.self_output[...])
    normed_two = (norm_parts(stream_one[...])[0] * as_row(r.second_gain) + as_row(r.second_shift)).astype(BF16)
    r.normed_two[...] = normed_two
    cross_queries = matmul(normed_two, r.query_weight[...]).astype(BF16).astype(F32) * (HEAD ** -0.5)
    moved_queries[...] = move(cross_queries)
    loads[0].wait()

    @pl.loop(0, stretches)
    def _(i):
        for c in range(D // 256):
            columns = slice(c * 256, c * 256 + 256)
            values = slice(D + c * 256, D + c * 256 + 256)
            chances = cross_chances(stack_heads(moved_queries[i, :, columns]), slopes[i, :, columns])
            moved[i, :, columns] = unstack_heads(matmul(chances.astype(BF16), slopes[i, :, values]))

    cross_low = (move_back() * keep).astype(BF16)
    r.cross_low[...] = cross_low
    stream_two[...] = stream_one[...] + matmul(cross_low, r.cross_output[...])
    two_normed[here] = (norm_parts(stream_two[...])[0] * as_row(r.third_gain) + as_row(r.third_shift)).astype(BF16)
    normed_swap = send(two_normed.at[here], two_normed.at[there], swap_send.at[1], swap_recv.at[1], partner)
    normed_swap.start()
    normed_grad[...] = jnp.zeros_like(normed_grad)
    summed[...] = jnp.zeros_like(summed)
    for copy in loads[1:]:
        copy.wait()
    tile = 512
    tiles = ff // tile

    def tile_copy(t):
        columns = pl.ds(pl.multiple_of(t * tile, tile), tile)
        return send(
            active.at[here, columns], active.at[there, columns], tile_send.at[t], tile_recv.at[t], partner
        )

    @pl.loop(0, tiles)
    def _(t):
        columns = pl.ds(pl.multiple_of(t * tile, tile), tile)
        upper = matmul(two_normed[here], up[:, columns])
        density = jnp.exp(upper * upper * -0.5) * (2.0 * math.pi) ** -0.5
        below = 0.5 + 0.5 * lax.erf(upper * 0.5 ** 0.5)
        active_low = (upper * below).astype(BF16)
        active[here, columns] = active_low
        tile_copy(t).start()
        grad = back_product(r.cotangent[...], down[columns])
        upper_low = (grad * (below + upper * density)).astype(BF16)
        spot = pl.ds(pl.multiple_of(lax.rem(t, tiles // 2) * tile, tile), tile)

        @pl.when(lax.div(t, tiles // 2) == member)
        def _():
            two_upper[here, spot] = upper_low

        @pl.when(lax.div(t, tiles // 2) != member)
        def _():
            give_upper[:, spot] = upper_low

        summed[...] += matmul(active_low, down[columns])
        normed_grad[...] += back_product(upper_low, up[:, columns])

    near = down.at[pl.ds(0, stretches * SPAN)]
    near_loads = [
        pltpu.make_async_copy(r.edge, down.at[pl.ds(0, SPAN)], near_sems.at[0]),
        pltpu.make_async_copy(r.neighbours, down.at[pl.ds(SPAN, (stretches - 1) * SPAN)], near_sems.at[1]),
    ]
    for copy in near_loads:
        copy.start()
    upper_swap = send(give_upper, two_upper.at[there], swap_send.at[2], swap_recv.at[2], partner)
    upper_swap.start()
    r.result[...] = (stream_two[...] + summed[...]).astype(BF16)

    def fill_down(s):
        if s > 0:
            return
        for copy in grad_swap:
            copy.wait()

        @pl.loop(0, tiles)
        def _(t):
            tile_copy(t).wait()

        deep = ff // batch
        tall = shares[0].rows
        for layer in range(batch):
            values = outer_sum(active[:, layer * deep : (layer + 1) * deep], two_grad[...]).astype(BF16)
            for g in range(groups):
                for part in range(2):
                    start = (g * 2 + part) * tall
                    sums[part][layer, g // 2, g % 2] = values[start : start + tall]

    def fill_up(s):
        if s == 2:
            normed_swap.wait()
            upper_swap.wait()
        piece = shares[s].pieces[0]
        for first in range(0, piece.count, 384):
            tile_values = outer_sum(two_normed[...], two_upper[:, piece.first + first : piece.first + first + 384])
            spread_to(sums[s], shares[s].rows, tile_values, first)

    fills = [fill_down, fill_down, fill_up, fill_up]
    running = [
        engine.steps(s, partial(fills[s], s), "zyx", shares[s].order[: EARLY_STEPS[s]], states[s])
        for s in range(EARLY)
    ]
    for run in running:
        next(run, None)

    gain_grad, shift_grad, inner = norm_back(stream_two[...], as_row(r.third_gain), normed_grad[...])
    r.vectors[1:2] = gain_grad
    r.vectors[3:4] = shift_grad
    stream_two_grad = r.cotangent[...].astype(F32) + inner
    normed_grad[...] = stream_two_grad
    branch_low = stream_two_grad.astype(BF16)
    r.branch[...] = branch_low
    moved_grads[...] = move(back_product(branch_low, r.cross_output[...]) * keep)

    def group_copy(i):
        return pltpu.make_async_copy(slopes.at[i], r.memory_grad.at[i], group_sems.at[i])

    @pl.loop(0, stretches)
    def _(i):
        for c in range(D // 256):
            columns = slice(c * 256, c * 256 + 256)
            values = slice(D + c * 256, D + c * 256 + 256)
            stacked = stack_heads(moved_queries[i, :, columns])
            stacked_grad = stack_heads(moved_grads[i, :, columns])
            keys = slopes[i, :, columns]
            chances = cross_chances(stacked, keys)
            chance_grad = back_product(stacked_grad, slopes[i, :, values])
            total = jnp.sum(chances * chance_grad, axis=1, keepdims=True)
            score_grad = (chances * (chance_grad - total)).astype(BF16)
            moved[i, :, columns] = unstack_heads(matmul(score_grad, keys)) * (HEAD ** -0.5)
            slopes[i, :, columns] = outer_sum(score_grad, stacked).astype(BF16)
            slopes[i, :, values] = outer_sum(chances.astype(BF16), stacked_grad).astype(BF16)
        group_copy(i).start()

    for run in running[:2]:
        next(run, None)
    query_grad = move_back().astype(BF16)
    r.query_grad[...] = query_grad
    gain_grad, shift_grad, inner = norm_back(
        stream_one[...], as_row(r.second_gain), back_product(query_grad, r.query_weight[...])
    )
    r.vectors[0:1] = gain_grad
    r.vectors[2:3] = shift_grad
    r.vectors[4:8] = jnp.zeros((4, D), F32)
    stream_one_grad = normed_grad[...] + inner
    r.stream_grad[...] = stream_one_grad
    self_low = stream_one_grad.astype(BF16)
    r.self_low[...] = self_low
    grad_out = back_product(self_low, r.self_output[...]).astype(BF16).astype(F32)

    for head in range(HEADS):
        block = (head // 2) * 128
        r.packed_grads[head] = pack_rows(grad_out[:, block : block + 128], head).astype(BF16)

    for copy in near_loads:
        copy.wait()
    span_rows = stretches * SPAN

    def memory_tile(owner, t):
        columns = pl.ds(pl.multiple_of(owner * D + t * 256, 256), 256)
        return outer_sum(near[...], slopes[:, :, columns].reshape(span_rows, 256)).astype(BF16)

    for t in range(D // 256):
        up[:, t * 256 : t * 256 + 256] = memory_tile(1 - member, t)
    memory_swap = send(
        up.at[:, pl.ds(0, D)], up.at[:, pl.ds(D, D)], swap_send.at[3], swap_recv.at[3], partner
    )
    memory_swap.start()
    for t in range(D // 256):
        up[:, 2 * D + t * 256 : 2 * D + t * 256 + 256] = memory_tile(member, t)
    for run in running:
        next(run, None)
    memory_swap.wait()
    r.memory_part[...] = add(up[:, 2 * D : 3 * D], up[:, D : 2 * D])

    @pl.loop(0, stretches)
    def _(i):
        group_copy(i).wait()


def middle(plan, batch, tokens, context, self_output, second_gain, second_shift, third_gain, third_shift, query_weight, memory, neighbours, edge, cross_output, up_weight, down_weight, cotangent):
    rows = plan.rows
    ff = up_weight.shape[1]
    stretches = memory.shape[0]
    shares = shares_of(batch, plan.groups, ff)
    dma = pltpu.SemaphoreType.DMA
    inputs = dict(
        tokens=tokens, context=context, self_output=self_output, second_gain=second_gain, second_shift=second_shift,
        third_gain=third_gain, third_shift=third_shift, query_weight=query_weight,
        cross_output=cross_output, cotangent=cotangent,
    )
    near = len(inputs)
    inputs.update(memory=memory, up_weight=up_weight, down_weight=down_weight, neighbours=neighbours, edge=edge)
    low = ((rows, D), BF16)
    outputs = dict(
        result=low, normed_two=low, cross_low=low, branch=low, query_grad=low, self_low=low,
        packed_grads=((HEADS, rows // 2, 128), BF16), memory_part=((D, D), BF16),
        stream_grad=((rows, D), F32), vectors=((8, D), F32),
    )
    steps = [step_shapes(shares[s], batch, "zyx", shares[s].order[: EARLY_STEPS[s]]) for s in range(EARLY)]
    for s in range(EARLY):
        outputs["state%d" % s] = (part_shape(shares[s], batch, axes_after(shares[s], EARLY_STEPS[s])), BF16)
    far = len(outputs)
    outputs.update(memory_grad=(memory.shape, BF16))
    scratch = [VM(part_shape(shares[s], batch, "zyx"), BF16) for s in range(EARLY)]
    scratch += [VM(shape, BF16) for shapes in steps for shape in shapes]
    scratch += [
        VM((D, ff), BF16),
        VM((ff, D), BF16),
        VM((2 * rows, ff), BF16),
        VM((2 * rows, D), BF16),
        VM((rows, ff // 2), BF16),
        VM((2 * rows, ff // 2), BF16),
        VM((2 * rows, D // 2), BF16),
        VM(memory.shape, BF16),
        VM((rows, D), F32),
        VM((rows, D), F32),
        VM((rows, D), F32),
        VM((rows, D), F32),
        VM((stretches, STRETCH, D), BF16),
        VM((stretches, STRETCH, D), BF16),
        VM((stretches, STRETCH, D), F32),
        dma((3,)),
        dma((1,)),
        dma((ff // 512,)),
        dma((ff // 512,)),
        dma((4,)),
        dma((4,)),
        dma((stretches,)),
        dma((2,)),
        dma((EARLY, batch - 1)),
        dma((EARLY, batch - 1)),
    ]
    names = list(inputs) + list(outputs)
    out = pl.pallas_call(
        partial(middle_kernel, plan, batch, shares, [len(s) for s in steps], names),
        out_shape=[jax.ShapeDtypeStruct(*shape) for shape in outputs.values()],
        in_specs=[pl.BlockSpec(memory_space=VM)] * near + [pl.BlockSpec(memory_space=pl.ANY)] * (len(inputs) - near),
        out_specs=[pl.BlockSpec(memory_space=VM)] * far + [pl.BlockSpec(memory_space=pl.ANY)],
        scratch_shapes=scratch,
        compiler_params=pltpu.CompilerParams(
            collective_id=2, has_side_effects=True, vmem_limit_bytes=62 << 20
        ),
        name="middle",
    )(*inputs.values())
    return SimpleNamespace(**dict(zip(outputs, out)))


def on_device(devices, batch, tokens, segment_ids, neighbours, first_gain, first_shift, self_weight, self_output, second_gain,
    second_shift, query_weight, memory_weight, cross_output, third_gain, third_shift, up_weight, down_weight, cotangent,
):
    rows = tokens.shape[1]
    plan = Plan(devices, rows)
    stretch_count = neighbours.shape[1]
    ff = up_weight.shape[1]
    neighbour_rows = neighbours[0].reshape(stretch_count * SPAN, D)
    normed_one, logs, starts, context, edge, queries, pairs, outs, memory, packed = attend(
        plan, tokens[0], first_gain, first_shift, segment_ids, self_weight, neighbour_rows, memory_weight
    )
    mid = middle(
        plan, batch, tokens[0], context, self_output, second_gain, second_shift, third_gain, third_shift, query_weight,
        memory, neighbour_rows, edge, cross_output, up_weight, down_weight, cotangent[0],
    )
    input_grad, neighbour_grad, shares = tail(
        plan,
        batch,
        mid.packed_grads,
        queries,
        pairs,
        outs,
        logs,
        starts,
        [mid.cross_low, mid.normed_two, context, normed_one],
        [mid.branch, mid.query_grad, mid.self_low],
        [getattr(mid, "state%d" % s) for s in range(EARLY)],
        mid.memory_part.reshape(batch, 2, 2, D // (batch * 4), D),
        mid.memory_grad.reshape((stretch_count + 1) * SPAN, 2 * D),
        memory_weight,
        packed,
        tokens[0],
        first_gain,
        mid.stream_grad,
        mid.vectors,
        ff,
    )
    wide = widen(plan, batch, ff, shares, mid.result, input_grad, neighbour_grad)
    down, up, cross_out, memory_w, query, self_out, self_w, result, input_grad, neighbour_grad = wide[:10]
    vector = wide[10:]
    return (
        result[None],
        input_grad[None],
        neighbour_grad.reshape(neighbours.shape),
        vector[0],
        vector[3],
        self_w,
        self_out,
        vector[1],
        vector[4],
        query,
        memory_w,
        cross_out,
        vector[2],
        vector[5],
        up,
        down,
    )


def from_behind(array, axis, by):
    devices = lax.axis_size(axis)
    pairs = [(i, i + by) for i in range(devices) if 0 <= i + by < devices]
    return lax.ppermute(array, axis, pairs)


def layer_norm(values, gain, shift):
    mean = jnp.mean(values, axis=-1, keepdims=True)
    centred = values - mean
    spread = jnp.mean(centred * centred, axis=-1, keepdims=True)
    return centred * lax.rsqrt(spread + EPSILON) * gain + shift


def block_rows():
    return 512


def causal_allowed(query_pos, query_seg, key_pos, key_seg):
    return (query_pos[:, None] >= key_pos[None, :]) & (query_seg[:, None] == key_seg[None, :])


def key_block_grads(
    queries, grad_out, log_total, delta, query_pos, query_seg, keys, values, key_pos, key_seg, scale
):
    allowed = causal_allowed(query_pos, query_seg, key_pos, key_seg)[None]
    scores = jnp.einsum("qhd,khd->hqk", queries, keys, preferred_element_type=jnp.float32) * scale
    chances = jnp.where(
        allowed, jnp.exp(jnp.where(allowed, scores, NEGATIVE) - log_total[..., None]), 0.0
    )
    prob_grad = jnp.einsum("qhd,khd->hqk", grad_out, values, preferred_element_type=jnp.float32)
    score_low = (chances * (prob_grad - delta[..., None])).astype(jnp.bfloat16)
    query_part = (
        jnp.einsum("hqk,khd->qhd", score_low, keys, preferred_element_type=jnp.float32) * scale
    )
    key_part = (
        jnp.einsum("hqk,qhd->khd", score_low, queries, preferred_element_type=jnp.float32) * scale
    )
    value_part = jnp.einsum(
        "hqk,qhd->khd", chances.astype(jnp.bfloat16), grad_out, preferred_element_type=jnp.float32
    )
    return (query_part, key_part, value_part)


def plain_on_device(
    tokens,
    segment_ids,
    neighbours,
    first_gain,
    first_shift,
    self_weight,
    self_output,
    second_gain,
    second_shift,
    query_weight,
    memory_weight,
    cross_output,
    third_gain,
    third_shift,
    up_weight,
    down_weight,
    cotangent,
):
    rows = tokens.shape[1]
    seq_index = lax.axis_index("seq")
    scale = HEAD ** (-0.5)
    stream = tokens[0].astype(jnp.float32)
    seg_local = segment_ids[0]
    positions = seq_index * rows + jnp.arange(rows, dtype=jnp.int32)
    normed_one, first_back = jax.vjp(layer_norm, stream, first_gain, first_shift)
    normed_one_low = normed_one.astype(jnp.bfloat16)
    projected = matmul(normed_one_low, self_weight).astype(jnp.bfloat16)
    queries = projected[:, :D].reshape(rows, HEADS, HEAD)
    keys_low = projected[:, D : 2 * D]
    values_low = projected[:, 2 * D :]
    start_state = (
        jnp.full((HEADS, rows), NEGATIVE, jnp.float32),
        jnp.zeros((HEADS, rows), jnp.float32),
        jnp.zeros((HEADS, rows, HEAD), jnp.float32),
    )
    carry = start_state
    piece_keys = lax.all_gather(keys_low, "seq", axis=0, tiled=True)
    piece_values = lax.all_gather(values_low, "seq", axis=0, tiled=True)
    piece_seg = lax.all_gather(seg_local, "seq", axis=0, tiled=True)
    count = piece_keys.shape[0]
    fold_size = block_rows()

    def step(state, index):
        maxes, totals, running = state
        first = index * fold_size
        keys = lax.dynamic_slice_in_dim(piece_keys, first, fold_size, 0).reshape(
            fold_size, HEADS, HEAD
        )
        values = lax.dynamic_slice_in_dim(piece_values, first, fold_size, 0).reshape(
            fold_size, HEADS, HEAD
        )
        key_seg = lax.dynamic_slice_in_dim(piece_seg, first, fold_size, 0)
        key_pos = first + jnp.arange(fold_size, dtype=jnp.int32)
        allowed = causal_allowed(positions, seg_local, key_pos, key_seg)[None]
        scores = (
            jnp.einsum("qhd,khd->hqk", queries, keys, preferred_element_type=jnp.float32) * scale
        )
        scores = jnp.where(allowed, scores, NEGATIVE)
        new_max = jnp.maximum(maxes, jnp.max(scores, axis=-1))
        factor = jnp.exp(maxes - new_max)
        weights = jnp.where(allowed, jnp.exp(scores - new_max[..., None]), 0.0)
        totals = totals * factor + jnp.sum(weights, axis=-1)
        running = running * factor[..., None] + jnp.einsum(
            "hqk,khd->hqd", weights.astype(jnp.bfloat16), values, preferred_element_type=jnp.float32
        )
        return ((new_max, totals, running), None)

    carry, unused = lax.scan(step, carry, jnp.arange(count // fold_size, dtype=jnp.int32))
    maxes, totals, running = carry
    log_total = maxes + jnp.log(totals)
    context = running / totals[..., None]
    context_low = jnp.transpose(context, (1, 0, 2)).reshape(rows, D).astype(jnp.bfloat16)
    stream_one = stream + matmul(context_low, self_output)
    normed_two, second_back = jax.vjp(layer_norm, stream_one, second_gain, second_shift)
    normed_two_low = normed_two.astype(jnp.bfloat16)
    cross_queries = matmul(normed_two_low, query_weight).astype(jnp.bfloat16)
    stretch_count = neighbours.shape[1]
    span = NEIGHBOURS * NEIGHBOUR_LEN
    groups = stretch_count + 1
    neighbour_rows = neighbours[0].reshape(stretch_count * span, D)
    memory = (
        matmul(neighbour_rows, memory_weight)
        .astype(jnp.bfloat16)
        .reshape(stretch_count, span, 2 * D)
    )
    previous = from_behind(memory[stretch_count - 1], "seq", 1)
    extended = jnp.concatenate([previous[None], memory], axis=0)
    memory_keys = extended[:, :, :D].reshape(groups, span, HEADS, HEAD)
    memory_values = extended[:, :, D:].reshape(groups, span, HEADS, HEAD)
    pad_top = jnp.zeros((1, D), jnp.bfloat16)
    pad_end = jnp.zeros((STRETCH - 1, D), jnp.bfloat16)
    padded_queries = jnp.concatenate([pad_top, cross_queries, pad_end], axis=0).reshape(
        groups, STRETCH, HEADS, HEAD
    )
    cross_probs = jax.nn.softmax(
        jnp.einsum(
            "gqhd,gkhd->ghqk", padded_queries, memory_keys, preferred_element_type=jnp.float32
        )
        * scale,
        axis=-1,
    )
    cross_probs_low = cross_probs.astype(jnp.bfloat16)
    keep = ((seq_index > 0) | (jnp.arange(rows, dtype=jnp.int32) >= STRETCH - 1)).astype(
        jnp.float32
    )[:, None]
    cross_context = jnp.einsum(
        "ghqk,gkhd->gqhd", cross_probs_low, memory_values, preferred_element_type=jnp.float32
    ).reshape(groups * STRETCH, D)[1 : rows + 1]
    cross_low = (cross_context * keep).astype(jnp.bfloat16)
    stream_two = stream_one + matmul(cross_low, cross_output)
    normed_three, third_back = jax.vjp(layer_norm, stream_two, third_gain, third_shift)
    normed_three_low = normed_three.astype(jnp.bfloat16)
    upper = matmul(normed_three_low, up_weight)
    active, gelu_back = jax.vjp(partial(jax.nn.gelu, approximate=False), upper)
    active_low = active.astype(jnp.bfloat16)
    result = (stream_two + matmul(active_low, down_weight)).astype(jnp.bfloat16)
    grad_low = cotangent[0]
    down_grad = outer_sum(active_low, grad_low)
    active_grad = back_product(grad_low, down_weight)
    upper_low = gelu_back(active_grad)[0].astype(jnp.bfloat16)
    up_grad = outer_sum(normed_three_low, upper_low)
    stream_part, third_gain_grad, third_shift_grad = third_back(back_product(upper_low, up_weight))
    stream_two_grad = grad_low.astype(jnp.float32) + stream_part
    branch_low = stream_two_grad.astype(jnp.bfloat16)
    cross_output_grad = outer_sum(cross_low, branch_low)
    context_grad = (back_product(branch_low, cross_output) * keep).astype(jnp.bfloat16)
    padded_grad = jnp.concatenate([pad_top, context_grad, pad_end], axis=0).reshape(
        groups, STRETCH, HEADS, HEAD
    )
    prob_grad = jnp.einsum(
        "gqhd,gkhd->ghqk", padded_grad, memory_values, preferred_element_type=jnp.float32
    )
    score_low = (
        cross_probs * (prob_grad - jnp.sum(cross_probs * prob_grad, axis=-1, keepdims=True))
    ).astype(jnp.bfloat16)
    cross_query_low = (
        (
            jnp.einsum(
                "ghqk,gkhd->gqhd", score_low, memory_keys, preferred_element_type=jnp.float32
            )
            * scale
        )
        .reshape(groups * STRETCH, D)[1 : rows + 1]
        .astype(jnp.bfloat16)
    )
    key_part = (
        jnp.einsum("ghqk,gqhd->gkhd", score_low, padded_queries, preferred_element_type=jnp.float32)
        * scale
    )
    value_part = jnp.einsum(
        "ghqk,gqhd->gkhd", cross_probs_low, padded_grad, preferred_element_type=jnp.float32
    )
    extended_grad = jnp.concatenate(
        [key_part.reshape(groups, span, D), value_part.reshape(groups, span, D)], axis=-1
    )
    returned = from_behind(extended_grad[0].astype(jnp.bfloat16), "seq", -1).astype(jnp.float32)
    memory_grad = jnp.concatenate(
        [extended_grad[1:stretch_count], (extended_grad[stretch_count] + returned)[None]], axis=0
    )
    memory_grad = memory_grad.astype(jnp.bfloat16).reshape(stretch_count * span, 2 * D)
    memory_weight_grad = outer_sum(neighbour_rows, memory_grad)
    neighbour_grad = back_product(memory_grad, memory_weight).reshape(neighbours.shape)
    query_weight_grad = outer_sum(normed_two_low, cross_query_low)
    stream_part, second_gain_grad, second_shift_grad = second_back(
        back_product(cross_query_low, query_weight)
    )
    stream_one_grad = stream_two_grad + stream_part
    self_low = stream_one_grad.astype(jnp.bfloat16)
    self_output_grad = outer_sum(context_low, self_low)
    grad_out = back_product(self_low, self_output).astype(jnp.bfloat16).reshape(rows, HEADS, HEAD)
    delta = jnp.sum(jnp.transpose(grad_out.astype(jnp.float32), (1, 0, 2)) * context, axis=-1)
    gathered_keys, gathered_values, gathered_seg = (
        lax.all_gather(keys_low, "seq", axis=0, tiled=True),
        lax.all_gather(values_low, "seq", axis=0, tiled=True),
        lax.all_gather(seg_local, "seq", axis=0, tiled=True),
    )
    total_rows = gathered_keys.shape[0]
    size = block_rows()

    def key_step(query_sum, index):
        first = index * size
        keys = lax.dynamic_slice_in_dim(gathered_keys, first, size, 0).reshape(size, HEADS, HEAD)
        values = lax.dynamic_slice_in_dim(gathered_values, first, size, 0).reshape(
            size, HEADS, HEAD
        )
        key_seg = lax.dynamic_slice_in_dim(gathered_seg, first, size, 0)
        key_pos = first + jnp.arange(size, dtype=jnp.int32)
        query_part, key_block, value_block = key_block_grads(
            queries,
            grad_out,
            log_total,
            delta,
            positions,
            seg_local,
            keys,
            values,
            key_pos,
            key_seg,
            scale,
        )
        pair = jnp.concatenate([key_block.reshape(size, D), value_block.reshape(size, D)], axis=1)
        return (query_sum + query_part, pair)

    query_grad, pairs = lax.scan(
        key_step,
        jnp.zeros((rows, HEADS, HEAD), jnp.float32),
        jnp.arange(total_rows // size, dtype=jnp.int32),
    )
    pair_grad = lax.psum_scatter(
        pairs.reshape(total_rows, 2 * D).astype(jnp.bfloat16),
        "seq",
        scatter_dimension=0,
        tiled=True,
    ).astype(jnp.float32)
    projected_grad = jnp.concatenate([query_grad.reshape(rows, D), pair_grad], axis=1).astype(
        jnp.bfloat16
    )
    self_weight_grad = outer_sum(normed_one_low, projected_grad)
    stream_part, first_gain_grad, first_shift_grad = first_back(
        back_product(projected_grad, self_weight)
    )
    input_grad = stream_one_grad + stream_part
    shares = (
        lax.psum_scatter(
            first_gain_grad.astype(jnp.bfloat16), "batch", scatter_dimension=0, tiled=True
        ).astype(jnp.float32),
        lax.psum_scatter(
            first_shift_grad.astype(jnp.bfloat16), "batch", scatter_dimension=0, tiled=True
        ).astype(jnp.float32),
        lax.psum_scatter(
            self_weight_grad.astype(jnp.bfloat16), "batch", scatter_dimension=0, tiled=True
        ).astype(jnp.float32),
        lax.psum_scatter(
            self_output_grad.astype(jnp.bfloat16), "batch", scatter_dimension=0, tiled=True
        ).astype(jnp.float32),
        lax.psum_scatter(
            second_gain_grad.astype(jnp.bfloat16), "batch", scatter_dimension=0, tiled=True
        ).astype(jnp.float32),
        lax.psum_scatter(
            second_shift_grad.astype(jnp.bfloat16), "batch", scatter_dimension=0, tiled=True
        ).astype(jnp.float32),
        lax.psum_scatter(
            query_weight_grad.astype(jnp.bfloat16), "batch", scatter_dimension=0, tiled=True
        ).astype(jnp.float32),
        lax.psum_scatter(
            memory_weight_grad.astype(jnp.bfloat16), "batch", scatter_dimension=0, tiled=True
        ).astype(jnp.float32),
        lax.psum_scatter(
            cross_output_grad.astype(jnp.bfloat16), "batch", scatter_dimension=0, tiled=True
        ).astype(jnp.float32),
        lax.psum_scatter(
            third_gain_grad.astype(jnp.bfloat16), "batch", scatter_dimension=0, tiled=True
        ).astype(jnp.float32),
        lax.psum_scatter(
            third_shift_grad.astype(jnp.bfloat16), "batch", scatter_dimension=0, tiled=True
        ).astype(jnp.float32),
        lax.psum_scatter(
            up_grad.astype(jnp.bfloat16), "batch", scatter_dimension=0, tiled=True
        ).astype(jnp.float32),
        lax.psum_scatter(
            down_grad.astype(jnp.bfloat16), "batch", scatter_dimension=0, tiled=True
        ).astype(jnp.float32),
    )
    sums = (
        lax.psum(shares[0].astype(jnp.bfloat16), "seq").astype(jnp.float32),
        lax.psum(shares[1].astype(jnp.bfloat16), "seq").astype(jnp.float32),
        lax.psum(shares[2].astype(jnp.bfloat16), "seq").astype(jnp.float32),
        lax.psum(shares[3].astype(jnp.bfloat16), "seq").astype(jnp.float32),
        lax.psum(shares[4].astype(jnp.bfloat16), "seq").astype(jnp.float32),
        lax.psum(shares[5].astype(jnp.bfloat16), "seq").astype(jnp.float32),
        lax.psum(shares[6].astype(jnp.bfloat16), "seq").astype(jnp.float32),
        lax.psum(shares[7].astype(jnp.bfloat16), "seq").astype(jnp.float32),
        lax.psum(shares[8].astype(jnp.bfloat16), "seq").astype(jnp.float32),
        lax.psum(shares[9].astype(jnp.bfloat16), "seq").astype(jnp.float32),
        lax.psum(shares[10].astype(jnp.bfloat16), "seq").astype(jnp.float32),
        lax.psum(shares[11].astype(jnp.bfloat16), "seq").astype(jnp.float32),
        lax.psum(shares[12].astype(jnp.bfloat16), "seq").astype(jnp.float32),
    )
    return (
        result[None],
        input_grad[None],
        neighbour_grad,
        sums[0],
        sums[1],
        sums[2],
        sums[3],
        sums[4],
        sums[5],
        sums[6],
        sums[7],
        sums[8],
        sums[9],
        sums[10],
        sums[11],
        sums[12],
    )


def solution(mesh):
    placed = (
        P("batch", "seq", None),
        P("batch", "seq"),
        P("batch", "seq", None, None, None),
        P(),
        P(),
        P(),
        P(),
        P(),
        P(),
        P(),
        P(),
        P(),
        P(),
        P(),
        P(),
        P(),
        P("batch", "seq", None),
    )
    sizes = mesh.shape
    if sizes["seq"] == 8 and sizes["batch"] == 4:
        body = partial(on_device, sizes["seq"], sizes["batch"])
    else:
        body = plain_on_device
    return jax.shard_map(
        body,
        mesh=mesh,
        in_specs=placed,
        out_specs=(
            P("batch", "seq", None),
            P("batch", "seq", None),
            P("batch", "seq", None, None, None),
            P("batch"),
            P("batch"),
            P("batch", None),
            P("batch", None),
            P("batch"),
            P("batch"),
            P("batch", None),
            P("batch", None),
            P("batch", None),
            P("batch"),
            P("batch"),
            P("batch", None),
            P("batch", None),
        ),
        check_vma=False,
    )
```
